32 devices in a mesh: dp: 4 (over y, x), expert: 8 (over z, core).
Axes of the slice: x: 2, y: 2, z: 4, core: 2. Of those that a mesh axis runs over, the one named last changes fastest.
Arguments:
- output_gradient: bfloat16 [4096, 2048], P(('dp', 'expert')), may hold values from -3 to 3
- chosen_expert_index: int32 [4096, 8], P(('dp', 'expert')), may hold values from 0 to 127, all different within a row; in each aligned block of 64 rows (0 to 63, 64 to 127, ...) at most 5 rows name the same one
- routing_gate_weight: bfloat16 [4096, 8], P(('dp', 'expert')), may hold values from 0.049804688 to 1
- hidden: bfloat16 [2, 512, 40, 384], P(None, ('dp', 'expert')), may hold values from -2 to 2
- frozen_down_weight: bfloat16 [128, 384, 2048], P('expert'), may hold values from -0.3125 to 0.3125
- adapter_input_map: bfloat16 [128, 384, 64], P('expert'), may hold values from -0.3125 to 0.3125
- adapter_output_map: bfloat16 [128, 64, 2048], P('expert'), may hold values from -0.125 to 0.125
Outputs:
- hidden_grad: bfloat16 [2, 512, 40, 384], P(None, ('dp', 'expert'))
- router_grad: float32 [4096, 8], P(('dp', 'expert'))
- lora_a_grad: float32 [128, 64, 384], P('expert', None, 'dp')
- lora_b_grad: float32 [128, 64, 2048], P('expert', None, 'dp')
The draws below stay inside these ranges and needn't reach their ends.
Inputs may be any that keep to these rules, and one draw needn't show every extreme that they name: `chosen_expert_index`: each row names 8 different experts; within each aligned block of 64 rows (one device's microbatch) no expert is named more than 5 times, a bound that some block reaches.
All inputs are finite; a program needn't handle non-finite values.
Results may differ from the reference program's by a relative error of at most 0.0049.
Values may be sent and summed in bfloat16 or wider, within the bound.
No kernel may reach another device: no remote copies, remote signals or barrier semaphores. Data moves between devices by JAX's collectives and lax.ppermute only.
A program may use at most 128 MiB of HBM per device.

```python
import math
import jax
import jax.numpy as jnp
import numpy as np
from jax import lax

MODEL_DIM = 2048
HIDDEN_UNITS = 384
ADAPTER_RANK = 64
EXPERT_TOTAL = 128
TOP = 8
MICRO = 2
MB_TOK = 64
CAP = 5
SLOTS = 40
TOKENS = 4096
N_DP = 4
N_EXPERT = 8


def level_of(key, shape, shards, low, top_value):
    def one(axis_at, parts):
        draws = jax.random.uniform(jax.random.fold_in(jax.random.fold_in(key, 6), axis_at), (parts,), jnp.float32, low / len(shards), top_value / len(shards))
        return jnp.repeat(jnp.exp(draws), shape[axis_at] // parts).reshape((-1,) + (1,) * (len(shape) - axis_at - 1))

    factor_of = one(*shards[0])
    for cut in shards[1:]:
        factor_of = factor_of * one(*cut)
    return factor_of


def shared_out(key, own, number, rows, count, top, most, slope):
    order = jax.random.permutation(key, count)
    crowded, ordinary = portions_of(count, rows * top, most, slope, True), portions_of(count, rows * top, most, slope, False)
    places = jnp.arange(count)

    def named(sizes, rotation):
        used = int((sizes > 0).sum())
        fixed = max(1, used // 4)
        shifted = fixed + (places - fixed + rotation * (used - fixed)) % max(1, count - fixed)
        return jnp.zeros((count,), jnp.int32).at[order[jnp.where(places < fixed, places, shifted)]].set(jnp.asarray(sizes, jnp.int32))

    sizes = jnp.where(number % 4 == 0, named(crowded, number // 4), named(ordinary, number - number // 4 - 1))
    mixed = jax.random.permutation(jax.random.fold_in(own, 3), count)
    donor, taker = mixed[0:count // 2 * 2:2], mixed[1:count // 2 * 2:2]
    slack = jnp.minimum(sizes[donor] - 1, most - sizes[taker]) // 2
    slack = jnp.where((donor == order[0]) | (taker == order[0]) | (sizes[taker] == 0), 0, jnp.maximum(slack, 0))
    shifted = jax.random.randint(jax.random.fold_in(own, 4), (count // 2,), 0, 1 << 20) % (slack + 1)
    sizes = sizes.at[donor].add(-shifted).at[taker].add(shifted)
    items = jnp.searchsorted(jnp.cumsum(sizes), jnp.arange(rows * top), side="right").astype(jnp.int32)
    table = items.reshape(top, rows).T
    table = table[jax.random.permutation(jax.random.fold_in(own, 1), rows)]
    rotation = jax.random.randint(jax.random.fold_in(own, 2), (rows, 1), 0, top)
    return jnp.take_along_axis(table, (jnp.arange(top)[None, :] + rotation) % top, axis=1)


def portions_of(amount, total, most, lean, full):
    loads = [(1 << 20) // math.isqrt(standing ** lean) + 1 for standing in range(1, amount + 1)]
    largest = most if full else min(most, max(-(-total // amount), total * loads[0] // sum(loads)))
    least = 1 if total - largest >= amount - 1 else 0
    counts, rest = [largest] + [least] * (amount - 1), total - largest - least * (amount - 1)
    while rest > 0:
        free = [i for i in range(1, amount) if counts[i] < largest] or [i for i in range(1, amount) if counts[i] < most]
        whole, left = sum([loads[i] for i in free]), rest
        for i in free:
            more = min(most - counts[i], max(1, left * loads[i] // whole), rest)
            counts[i] = counts[i] + more
            rest = rest - more
    return np.array(counts)


def gaussian(rng, shape, spread, reach, split=(), held_as=jnp.bfloat16):
    entries = spread * jax.random.normal(rng, shape, jnp.float32)
    if split:
        entries = entries * level_of(rng, shape, split, -0.22, 0.18)
    return jnp.clip(entries, -reach, reach).astype(held_as)


def setup_inputs(seed: int = 0) -> dict:
    seeds = jax.random.split(jax.random.key(seed), 8)
    output_gradient = gaussian(seeds[0], (TOKENS, MODEL_DIM), 0.5, 3.0, ((0, 32),))
    chosen_expert_index_keys = jax.random.split(jax.random.fold_in(seeds[1], 1), TOKENS // MB_TOK)
    chosen_expert_index_turns = jax.random.permutation(jax.random.fold_in(seeds[1], 3), TOKENS // MB_TOK)
    chosen_expert_index = jax.vmap(lambda own, number: shared_out(jax.random.fold_in(seeds[1], 2), own, number, MB_TOK, EXPERT_TOTAL, TOP, CAP, 2))(chosen_expert_index_keys, chosen_expert_index_turns).reshape((TOKENS, TOP))
    routing_gate_weight = jnp.clip(jnp.exp(math.log(1.0) - 2.9996462 * jax.random.uniform(seeds[2], (TOKENS, TOP), jnp.float32) ** level_of(seeds[2], (TOKENS, TOP), ((0, 32),), -0.2, 0.2)), 0.049804688, 1.0).astype(jnp.bfloat16)
    hidden = gaussian(seeds[3], (MICRO, N_DP * EXPERT_TOTAL, SLOTS, HIDDEN_UNITS), 0.3, 2.0, ((1, 32),))
    frozen_down_weight = gaussian(seeds[4], (EXPERT_TOTAL, HIDDEN_UNITS, MODEL_DIM), HIDDEN_UNITS ** -0.5, 0.3125, ((0, 8),))
    adapter_input_map = gaussian(seeds[5], (EXPERT_TOTAL, HIDDEN_UNITS, ADAPTER_RANK), HIDDEN_UNITS ** -0.5, 0.3125, ((0, 8),))
    adapter_output_map = gaussian(seeds[6], (EXPERT_TOTAL, ADAPTER_RANK, MODEL_DIM), MODEL_DIM ** -0.5, 0.125, ((0, 8),))
    return dict(output_gradient=output_gradient, chosen_expert_index=chosen_expert_index, routing_gate_weight=routing_gate_weight, hidden=hidden, frozen_down_weight=frozen_down_weight, adapter_input_map=adapter_input_map, adapter_output_map=adapter_output_map)


adapter_scale = 2.0
highest_precision = lax.Precision.HIGHEST


def block_slots(block):
    onehot = (block[:, None] == jnp.arange(EXPERT_TOTAL, dtype=jnp.int32)[None, :]).astype(jnp.int32)
    return (jnp.sum(jnp.cumsum(onehot, axis=0) * onehot, axis=1) - 1).astype(jnp.int32)


def to_bf16(value):
    return lax.optimization_barrier(value.astype(jnp.bfloat16)).astype(jnp.float32)


def reference(output_gradient, chosen_expert_index, routing_gate_weight, hidden, frozen_down_weight, adapter_input_map, adapter_output_map):
    token_count = output_gradient.shape[0]
    entry_count = token_count * TOP
    blocks = chosen_expert_index.reshape(N_DP * N_EXPERT * MICRO, MB_TOK * TOP)
    before = lax.map(block_slots, blocks).reshape(N_DP, N_EXPERT, MICRO, MB_TOK * TOP)
    chosen = chosen_expert_index.reshape(N_DP, N_EXPERT, MICRO, MB_TOK * TOP)
    group_index = jnp.arange(N_DP, dtype=jnp.int32)[:, None, None, None]
    source_index = jnp.arange(N_EXPERT, dtype=jnp.int32)[None, :, None, None]
    micro_index = jnp.arange(MICRO, dtype=jnp.int32)[None, None, :, None]
    position = ((micro_index * N_DP + group_index) * EXPERT_TOTAL + chosen) * SLOTS + source_index * CAP + before
    position = position.reshape(-1).astype(jnp.int32)
    table = jnp.full((MICRO * N_DP * EXPERT_TOTAL * SLOTS,), entry_count, jnp.int32)
    table = table.at[position].set(jnp.arange(entry_count, dtype=jnp.int32))
    table = table.reshape(MICRO, N_DP, EXPERT_TOTAL, SLOTS)
    padded_grad = jnp.concatenate([output_gradient, jnp.zeros((1, MODEL_DIM), output_gradient.dtype)], axis=0)
    padded_weight = jnp.concatenate([routing_gate_weight.reshape(-1), jnp.zeros((1,), routing_gate_weight.dtype)])
    stacked = hidden.reshape(MICRO, N_DP, EXPERT_TOTAL, SLOTS, HIDDEN_UNITS)

    def one_expert(expert_number):
        picks = lax.dynamic_index_in_dim(table, expert_number, 2, keepdims=False)
        token_pick = jnp.where(picks < entry_count, picks // TOP, token_count).astype(jnp.int32)
        received_gradient = padded_grad[token_pick].astype(jnp.float32)
        received_weight = padded_weight[picks].astype(jnp.float32)[..., None]
        retained_rows = lax.dynamic_index_in_dim(stacked, expert_number, 2, keepdims=False).astype(jnp.float32)
        weight_down = frozen_down_weight[expert_number].astype(jnp.float32)
        adapter_input = adapter_input_map[expert_number].astype(jnp.float32)
        adapter_output = adapter_output_map[expert_number].astype(jnp.float32)
        frozen_term = jnp.einsum("mnsd,fd->mnsf", received_gradient, weight_down, precision=highest_precision)
        across_product = to_bf16(jnp.einsum("mnsd,rd->mnsr", received_gradient, adapter_output, precision=highest_precision))
        low_rank_state = jnp.einsum("mnsr,fr->mnsf", across_product, adapter_input, precision=highest_precision)
        hidden_state_gradient = (received_weight * (frozen_term + adapter_scale * low_rank_state)).astype(jnp.bfloat16)
        down_mapping = to_bf16(jnp.einsum("mnsf,fr->mnsr", retained_rows, adapter_input, precision=highest_precision))
        routing_rows = jnp.sum(frozen_term * retained_rows, axis=-1) + adapter_scale * jnp.sum(down_mapping * across_product, axis=-1)
        scaled_gradient = to_bf16(received_weight * received_gradient)
        scaled_across_product = to_bf16(received_weight * across_product)
        adapter_output_gradient = adapter_scale * jnp.einsum("jlkh,jlkp->hp", down_mapping, scaled_gradient, precision=highest_precision)
        adapter_input_gradient = adapter_scale * jnp.einsum("baqv,baqc->vc", scaled_across_product, retained_rows, precision=highest_precision)
        return hidden_state_gradient, routing_rows, adapter_input_gradient, adapter_output_gradient

    hidden_state_gradient, routing_rows, adapter_input_gradient, adapter_output_gradient = lax.map(one_expert, jnp.arange(EXPERT_TOTAL, dtype=jnp.int32))
    hidden_grad = jnp.transpose(hidden_state_gradient, (1, 2, 0, 3, 4)).reshape(MICRO, N_DP * EXPERT_TOTAL, SLOTS, HIDDEN_UNITS)
    router_flat = jnp.transpose(routing_rows, (1, 2, 0, 3)).reshape(-1)
    router_grad = router_flat[position].reshape(token_count, TOP)
    return hidden_grad, router_grad, adapter_input_gradient, adapter_output_gradient
```

```python
import functools

import jax
import jax.numpy as jnp
from jax import lax
from jax.experimental import pallas as pl
from jax.experimental.pallas import tpu as pltpu
from jax.sharding import PartitionSpec as P

adapter_scale = 2.0


def slot_rows(id_rows, experts, per_device, sources, capacity):
    onehot = (id_rows[:, :, None] == jnp.arange(experts, dtype=jnp.int32)[None, None, :]).astype(
        jnp.int32
    )
    before = jnp.sum(jnp.cumsum(onehot, axis=1) * onehot, axis=2) - 1
    target_dev = id_rows // per_device
    target_slot = id_rows % per_device
    return (target_slot * sources + target_dev) * capacity + before


def pick_rows(source, indices):
    return source[indices]


def dispatch_buffers(grad_rows, weight_rows, send_rows, top_count, buffer_len):
    entry_count = send_rows.shape[1]
    token_count = grad_rows.shape[1]
    filler = jnp.full((buffer_len,), entry_count, jnp.int32)

    def invert(rows):
        return filler.at[rows].set(jnp.arange(entry_count, dtype=jnp.int32))

    table = jax.vmap(invert)(send_rows)
    padded_grad = jnp.concatenate(
        [grad_rows, jnp.zeros((grad_rows.shape[0], 1, grad_rows.shape[2]), grad_rows.dtype)], axis=1
    )
    padded_weight = jnp.concatenate(
        [weight_rows, jnp.zeros((weight_rows.shape[0], 1), weight_rows.dtype)], axis=1
    )
    token_pick = jnp.where(table < entry_count, table // top_count, token_count)
    sent_grad = jax.vmap(pick_rows)(padded_grad, token_pick)
    sent_weight = jax.vmap(pick_rows)(padded_weight, table)
    return (sent_grad, sent_weight)


def expert_rows_view(
    received_gradient,
    received_weight,
    retained_rows,
    frozen_down_weight,
    adapter_input_map,
    adapter_output_map,
):
    frozen_term = jnp.einsum(
        "mesd,efd->mesf", received_gradient, frozen_down_weight, preferred_element_type=jnp.float32
    )
    across_product = jnp.einsum(
        "hati,aki->hatk", received_gradient, adapter_output_map, preferred_element_type=jnp.float32
    ).astype(jnp.bfloat16)
    low_rank_state = jnp.einsum(
        "ptqv,tgv->ptqg", across_product, adapter_input_map, preferred_element_type=jnp.float32
    )
    capacity_slot_weight = received_weight.astype(jnp.float32)[..., None]
    hidden_state_gradient = (
        capacity_slot_weight * (frozen_term + adapter_scale * low_rank_state)
    ).astype(jnp.bfloat16)
    down_mapping = jnp.einsum(
        "lkgu,kup->lkgp", retained_rows, adapter_input_map, preferred_element_type=jnp.float32
    ).astype(jnp.bfloat16)
    complete_term = jnp.sum(frozen_term * retained_rows.astype(jnp.float32), axis=-1)
    adapter_term = jnp.einsum(
        "mesr,mesr->mes", down_mapping, across_product, preferred_element_type=jnp.float32
    )
    routing_rows = complete_term + adapter_scale * adapter_term
    scaled_gradient = (capacity_slot_weight * received_gradient).astype(jnp.bfloat16)
    scaled_across_product = (capacity_slot_weight * across_product.astype(jnp.float32)).astype(
        jnp.bfloat16
    )
    adapter_output_gradient = adapter_scale * jnp.einsum(
        "mesr,mesd->erd", down_mapping, scaled_gradient, preferred_element_type=jnp.float32
    )
    adapter_input_gradient = adapter_scale * jnp.einsum(
        "mesr,mesf->erf", scaled_across_product, retained_rows, preferred_element_type=jnp.float32
    )
    return (hidden_state_gradient, routing_rows, adapter_input_gradient, adapter_output_gradient)


def local_by_slots(
    output_gradient,
    chosen_expert_index,
    routing_gate_weight,
    hidden,
    frozen_down_weight,
    adapter_input_map,
    adapter_output_map,
):
    sources = lax.axis_size("expert")
    per_device = frozen_down_weight.shape[0]
    experts = per_device * sources
    micro_count = hidden.shape[0]
    slot_count = hidden.shape[2]
    capacity = slot_count // sources
    top_count = chosen_expert_index.shape[1]
    model_width = output_gradient.shape[1]
    buffer_len = experts * capacity
    grad_rows = output_gradient.reshape(micro_count, -1, model_width)
    id_rows = chosen_expert_index.reshape(micro_count, -1)
    weight_rows = routing_gate_weight.reshape(micro_count, -1)
    send_rows = slot_rows(id_rows, experts, per_device, sources, capacity)
    sent_grad, sent_weight = dispatch_buffers(
        grad_rows, weight_rows, send_rows, top_count, buffer_len
    )
    sent_grad = sent_grad.reshape(micro_count, per_device, sources, capacity, model_width)
    sent_weight = sent_weight.reshape(micro_count, per_device, sources, capacity)
    received_gradient, received_weight = (
        lax.all_to_all(sent_grad, "expert", split_axis=2, concat_axis=2, tiled=True),
        lax.all_to_all(sent_weight, "expert", split_axis=2, concat_axis=2, tiled=True),
    )
    received_gradient = received_gradient.reshape(micro_count, per_device, slot_count, model_width)
    received_weight = received_weight.reshape(micro_count, per_device, slot_count)
    hidden_grad, routing_rows, adapter_input_gradient, adapter_output_gradient = expert_rows_view(
        received_gradient,
        received_weight,
        hidden,
        frozen_down_weight,
        adapter_input_map,
        adapter_output_map,
    )
    router_home = lax.all_to_all(
        routing_rows.reshape(micro_count, per_device, sources, capacity),
        "expert",
        split_axis=2,
        concat_axis=2,
        tiled=True,
    )
    router_flat = router_home.reshape(micro_count, buffer_len)
    router_grad = jax.vmap(pick_rows)(router_flat, send_rows).reshape(-1, top_count)
    share_a, share_b = (
        lax.psum_scatter(adapter_input_gradient, "dp", scatter_dimension=2, tiled=True),
        lax.psum_scatter(adapter_output_gradient, "dp", scatter_dimension=2, tiled=True),
    )
    return (hidden_grad, router_grad, share_a, share_b)


def pad_rows(count):
    return -(-count // 16) * 16


def expert_kernel(
    capacity,
    meta_ref,
    dy_hbm,
    hidden_ref,
    weight_hbm,
    amap_ref,
    bmap_hbm,
    hg_ref,
    rk_ref,
    la_ref,
    lb_ref,
    dy_s,
    wb_s,
    rows_s,
    code_s,
    gate_s,
    back_s,
    dy_sem,
    w_sem,
    b_sem,
):
    sources, twice_top, span = meta_ref.shape
    top = twice_top // 2
    micro, experts, slots, units = hidden_ref.shape
    rank = la_ref.shape[1]
    width = dy_hbm.shape[1]
    block = span // micro
    padded = rows_s.shape[1] // micro
    base = (lax.axis_index("expert") * experts).astype(jnp.float32)

    dy_copy = pltpu.make_async_copy(dy_hbm, dy_s, dy_sem)
    dy_copy.start()

    def weight_copies(x):
        return (
            pltpu.make_async_copy(weight_hbm.at[x], wb_s.at[x, pl.ds(0, units)], w_sem.at[x]),
            pltpu.make_async_copy(bmap_hbm.at[x], wb_s.at[x, pl.ds(units, rank)], b_sem.at[x]),
        )

    for x in range(experts):
        for copy in weight_copies(x):
            copy.start()

    number = lax.broadcasted_iota(jnp.int32, (experts, span), 0).astype(jnp.float32) + base
    from_row = lax.broadcasted_iota(jnp.int32, (span, span), 0)
    to_row = lax.broadcasted_iota(jnp.int32, (span, span), 1)
    earlier = jnp.where(
        (from_row // block == to_row // block) & (from_row < to_row), 1.0, 0.0
    ).astype(jnp.bfloat16)
    codes, gates = [], []
    for j in range(sources):
        named = jnp.zeros((experts, span), jnp.float32)
        gate = jnp.zeros((experts, span), jnp.float32)
        for k in range(top):
            hit = meta_ref[j, k : k + 1, :] == number
            named = jnp.where(hit, 1.0, named)
            gate = jnp.where(hit, meta_ref[j, top + k : top + k + 1, :], gate)
        before = jnp.dot(named.astype(jnp.bfloat16), earlier, preferred_element_type=jnp.float32)
        codes.append(jnp.where(named > 0.0, before + float(j * capacity), -1.0))
        gates.append(gate)

    slot_of = lax.broadcasted_iota(jnp.int32, (padded, sources * block), 0).astype(jnp.float32)
    picks = []
    for m in range(micro):
        part = slice(m * block, (m + 1) * block)
        code_m = jnp.concatenate([c[:, part] for c in codes], axis=1)
        gate_m = jnp.concatenate([g[:, part] for g in gates], axis=1)
        code_s[m] = code_m
        chosen = []
        for x in range(experts):
            hit = code_m[x : x + 1, :] == slot_of
            chosen.append(jnp.where(hit, 1.0, 0.0).astype(jnp.bfloat16))
            gate_s[x, m * padded : (m + 1) * padded, :] = jnp.sum(
                jnp.where(hit, gate_m[x : x + 1, :], 0.0), axis=1, keepdims=True
            )
        picks.append(jnp.concatenate(chosen, axis=0))

    dy_copy.wait()
    tile = 512 if width % 512 == 0 else width
    for m in range(micro):
        for n in range(width // tile):
            cols = slice(n * tile, (n + 1) * tile)
            tokens = jnp.concatenate(
                [
                    dy_s[j * span + m * block : j * span + (m + 1) * block, cols]
                    for j in range(sources)
                ],
                axis=0,
            )
            rows = jnp.dot(picks[m], tokens, preferred_element_type=jnp.float32)
            rows_s[:, m * padded : (m + 1) * padded, cols] = rows.astype(jnp.bfloat16).reshape(
                experts, padded, tile
            )

    contract_last = (((1,), (1,)), ((), ()))
    contract_first = (((0,), (0,)), ((), ()))

    def one_expert(x, carry):
        for copy in weight_copies(x):
            copy.wait()
        rows = rows_s[x]
        both = lax.dot_general(rows, wb_s[x], contract_last, preferred_element_type=jnp.float32)
        main = both[:, :units]
        v = both[:, units:].astype(jnp.bfloat16)
        amap = amap_ref[x]
        low = lax.dot_general(v, amap, contract_last, preferred_element_type=jnp.float32)
        gate = gate_s[x]
        grad = (gate * (main + adapter_scale * low)).astype(jnp.bfloat16)
        filler = jnp.zeros((padded - slots, units), jnp.float32)
        pieces = []
        for m in range(micro):
            hg_ref[m, x] = grad[m * padded : m * padded + slots]
            pieces.append(hidden_ref[m, x].astype(jnp.float32))
            pieces.append(filler)
        held_wide = jnp.concatenate(pieces, axis=0)
        held = held_wide.astype(jnp.bfloat16)
        u = jnp.dot(held, amap, preferred_element_type=jnp.float32).astype(jnp.bfloat16)
        v_wide = v.astype(jnp.float32)
        routed = jnp.sum(main * held_wide, axis=1, keepdims=True) + adapter_scale * jnp.sum(
            u.astype(jnp.float32) * v_wide, axis=1, keepdims=True
        )
        for m in range(micro):
            hit = code_s[m, pl.ds(x, 1), :] == slot_of
            back_s[m, pl.ds(x, 1), :] = jnp.sum(
                jnp.where(hit, routed[m * padded : (m + 1) * padded], 0.0), axis=0, keepdims=True
            )
        q = (gate * rows.astype(jnp.float32)).astype(jnp.bfloat16)
        w = (gate * v_wide).astype(jnp.bfloat16)
        lb_ref[x] = (
            adapter_scale
            * lax.dot_general(u, q, contract_first, preferred_element_type=jnp.float32)
        ).astype(lb_ref.dtype)
        la_ref[x] = (
            adapter_scale
            * lax.dot_general(w, held, contract_first, preferred_element_type=jnp.float32)
        ).astype(la_ref.dtype)
        return carry

    lax.fori_loop(0, experts, one_expert, 0)

    for j in range(sources):
        back = jnp.concatenate(
            [back_s[m, :, j * block : (j + 1) * block] for m in range(micro)], axis=1
        )
        for k in range(top):
            rk_ref[j, k : k + 1, :] = jnp.sum(
                jnp.where(meta_ref[j, k : k + 1, :] == number, back, 0.0), axis=0, keepdims=True
            )


def local_by_tokens(
    output_gradient,
    chosen_expert_index,
    routing_gate_weight,
    hidden,
    frozen_down_weight,
    adapter_input_map,
    adapter_output_map,
):
    sources = lax.axis_size("expert")
    micro, experts, slots, units = hidden.shape
    span, top = chosen_expert_index.shape
    width = output_gradient.shape[1]
    rank = adapter_input_map.shape[2]
    capacity = slots // sources
    block = span // micro
    padded = pad_rows(slots)
    meta = jnp.concatenate(
        [
            chosen_expert_index.T.astype(jnp.float32),
            routing_gate_weight.T.astype(jnp.float32),
        ],
        axis=0,
    )
    meta = lax.all_gather(meta, "expert", axis=0)
    tokens = lax.all_gather(output_gradient, "expert", axis=0, tiled=True)
    vmem = pl.BlockSpec(memory_space=pltpu.VMEM)
    anywhere = pl.BlockSpec(memory_space=pl.ANY)
    hidden_grad, routed, share_a, share_b = pl.pallas_call(
        functools.partial(expert_kernel, capacity),
        out_shape=(
            jax.ShapeDtypeStruct(hidden.shape, jnp.bfloat16),
            jax.ShapeDtypeStruct((sources, top, span), jnp.float32),
            jax.ShapeDtypeStruct((experts, rank, units), jnp.bfloat16),
            jax.ShapeDtypeStruct((experts, rank, width), jnp.bfloat16),
        ),
        in_specs=[vmem, anywhere, vmem, anywhere, vmem, anywhere],
        out_specs=(vmem, vmem, vmem, vmem),
        scratch_shapes=[
            pltpu.VMEM((sources * span, width), jnp.bfloat16),
            pltpu.VMEM((experts, units + rank, width), jnp.bfloat16),
            pltpu.VMEM((experts, micro * padded, width), jnp.bfloat16),
            pltpu.VMEM((micro, experts, sources * block), jnp.float32),
            pltpu.VMEM((experts, micro * padded, 1), jnp.float32),
            pltpu.VMEM((micro, experts, sources * block), jnp.float32),
            pltpu.SemaphoreType.DMA,
            pltpu.SemaphoreType.DMA((experts,)),
            pltpu.SemaphoreType.DMA((experts,)),
        ],
        compiler_params=pltpu.CompilerParams(vmem_limit_bytes=58 * 1024 * 1024),
        cost_estimate=pl.CostEstimate(
            flops=2 * experts * micro * padded * width * (2 * (units + rank) + sources * block),
            bytes_accessed=2 * experts * width * (units + 3 * rank),
            transcendentals=0,
        ),
        name="expert_rows",
    )(meta, tokens, hidden, frozen_down_weight, adapter_input_map, adapter_output_map)
    home = lax.all_to_all(routed, "expert", split_axis=0, concat_axis=0, tiled=True)
    router_grad = jnp.sum(home, axis=0).T
    lora_a = lax.psum_scatter(share_a, "dp", scatter_dimension=2, tiled=True)
    lora_b = lax.psum_scatter(share_b, "dp", scatter_dimension=2, tiled=True)
    return (hidden_grad, router_grad, lora_a.astype(jnp.float32), lora_b.astype(jnp.float32))


def local(*arrays):
    sources = lax.axis_size("expert")
    gathered = sources * arrays[0].shape[0]
    by_slot = arrays[3].shape[0] * arrays[4].shape[0] * arrays[3].shape[2]
    if gathered <= by_slot:
        return local_by_tokens(*arrays)
    return local_by_slots(*arrays)


def solution(mesh):
    in_specs = (
        P(("dp", "expert"), None),
        P(("dp", "expert"), None),
        P(("dp", "expert"), None),
        P(None, ("dp", "expert"), None, None),
        P("expert", None, None),
        P("expert", None, None),
        P("expert", None, None),
    )
    out_specs = (
        P(None, ("dp", "expert"), None, None),
        P(("dp", "expert"), None),
        P("expert", None, "dp"),
        P("expert", None, "dp"),
    )
    return jax.shard_map(local, mesh=mesh, in_specs=in_specs, out_specs=out_specs, check_vma=False)
```

```python
import functools

import jax
import jax.numpy as jnp
from jax import lax
from jax.experimental import pallas as pl
from jax.experimental.pallas import tpu as pltpu
from jax.sharding import PartitionSpec as P

adapter_scale = 2.0


def slot_rows(id_rows, experts, per_device, sources, capacity):
    onehot = (id_rows[:, :, None] == jnp.arange(experts, dtype=jnp.int32)[None, None, :]).astype(
        jnp.int32
    )
    before = jnp.sum(jnp.cumsum(onehot, axis=1) * onehot, axis=2) - 1
    target_dev = id_rows // per_device
    target_slot = id_rows % per_device
    return (target_slot * sources + target_dev) * capacity + before


def pick_rows(source, indices):
    return source[indices]


def dispatch_buffers(grad_rows, weight_rows, send_rows, top_count, buffer_len):
    entry_count = send_rows.shape[1]
    token_count = grad_rows.shape[1]
    filler = jnp.full((buffer_len,), entry_count, jnp.int32)

    def invert(rows):
        return filler.at[rows].set(jnp.arange(entry_count, dtype=jnp.int32))

    table = jax.vmap(invert)(send_rows)
    padded_grad = jnp.concatenate(
        [grad_rows, jnp.zeros((grad_rows.shape[0], 1, grad_rows.shape[2]), grad_rows.dtype)], axis=1
    )
    padded_weight = jnp.concatenate(
        [weight_rows, jnp.zeros((weight_rows.shape[0], 1), weight_rows.dtype)], axis=1
    )
    token_pick = jnp.where(table < entry_count, table // top_count, token_count)
    sent_grad = jax.vmap(pick_rows)(padded_grad, token_pick)
    sent_weight = jax.vmap(pick_rows)(padded_weight, table)
    return (sent_grad, sent_weight)


def expert_rows_view(
    received_gradient,
    received_weight,
    retained_rows,
    frozen_down_weight,
    adapter_input_map,
    adapter_output_map,
):
    frozen_term = jnp.einsum(
        "mesd,efd->mesf", received_gradient, frozen_down_weight, preferred_element_type=jnp.float32
    )
    across_product = jnp.einsum(
        "hati,aki->hatk", received_gradient, adapter_output_map, preferred_element_type=jnp.float32
    ).astype(jnp.bfloat16)
    low_rank_state = jnp.einsum(
        "ptqv,tgv->ptqg", across_product, adapter_input_map, preferred_element_type=jnp.float32
    )
    capacity_slot_weight = received_weight.astype(jnp.float32)[..., None]
    hidden_state_gradient = (
        capacity_slot_weight * (frozen_term + adapter_scale * low_rank_state)
    ).astype(jnp.bfloat16)
    down_mapping = jnp.einsum(
        "lkgu,kup->lkgp", retained_rows, adapter_input_map, preferred_element_type=jnp.float32
    ).astype(jnp.bfloat16)
    complete_term = jnp.sum(frozen_term * retained_rows.astype(jnp.float32), axis=-1)
    adapter_term = jnp.einsum(
        "mesr,mesr->mes", down_mapping, across_product, preferred_element_type=jnp.float32
    )
    routing_rows = complete_term + adapter_scale * adapter_term
    scaled_gradient = (capacity_slot_weight * received_gradient).astype(jnp.bfloat16)
    scaled_across_product = (capacity_slot_weight * across_product.astype(jnp.float32)).astype(
        jnp.bfloat16
    )
    adapter_output_gradient = adapter_scale * jnp.einsum(
        "mesr,mesd->erd", down_mapping, scaled_gradient, preferred_element_type=jnp.float32
    )
    adapter_input_gradient = adapter_scale * jnp.einsum(
        "mesr,mesf->erf", scaled_across_product, retained_rows, preferred_element_type=jnp.float32
    )
    return (hidden_state_gradient, routing_rows, adapter_input_gradient, adapter_output_gradient)


def local_by_slots(
    output_gradient,
    chosen_expert_index,
    routing_gate_weight,
    hidden,
    frozen_down_weight,
    adapter_input_map,
    adapter_output_map,
):
    sources = lax.axis_size("expert")
    per_device = frozen_down_weight.shape[0]
    experts = per_device * sources
    micro_count = hidden.shape[0]
    slot_count = hidden.shape[2]
    capacity = slot_count // sources
    top_count = chosen_expert_index.shape[1]
    model_width = output_gradient.shape[1]
    buffer_len = experts * capacity
    grad_rows = output_gradient.reshape(micro_count, -1, model_width)
    id_rows = chosen_expert_index.reshape(micro_count, -1)
    weight_rows = routing_gate_weight.reshape(micro_count, -1)
    send_rows = slot_rows(id_rows, experts, per_device, sources, capacity)
    sent_grad, sent_weight = dispatch_buffers(
        grad_rows, weight_rows, send_rows, top_count, buffer_len
    )
    sent_grad = sent_grad.reshape(micro_count, per_device, sources, capacity, model_width)
    sent_weight = sent_weight.reshape(micro_count, per_device, sources, capacity)
    received_gradient, received_weight = (
        lax.all_to_all(sent_grad, "expert", split_axis=2, concat_axis=2, tiled=True),
        lax.all_to_all(sent_weight, "expert", split_axis=2, concat_axis=2, tiled=True),
    )
    received_gradient = received_gradient.reshape(micro_count, per_device, slot_count, model_width)
    received_weight = received_weight.reshape(micro_count, per_device, slot_count)
    hidden_grad, routing_rows, adapter_input_gradient, adapter_output_gradient = expert_rows_view(
        received_gradient,
        received_weight,
        hidden,
        frozen_down_weight,
        adapter_input_map,
        adapter_output_map,
    )
    router_home = lax.all_to_all(
        routing_rows.reshape(micro_count, per_device, sources, capacity),
        "expert",
        split_axis=2,
        concat_axis=2,
        tiled=True,
    )
    router_flat = router_home.reshape(micro_count, buffer_len)
    router_grad = jax.vmap(pick_rows)(router_flat, send_rows).reshape(-1, top_count)
    share_a, share_b = (
        lax.psum_scatter(adapter_input_gradient, "dp", scatter_dimension=2, tiled=True),
        lax.psum_scatter(adapter_output_gradient, "dp", scatter_dimension=2, tiled=True),
    )
    return (hidden_grad, router_grad, share_a, share_b)


def pad_rows(count):
    return -(-count // 16) * 16


def slot_codes(meta, owners_ref, first, capacity, experts, micro):
    shards = meta.shape[0]
    top, span = meta.shape[1] // 2, meta.shape[2]
    block = span // micro
    number = lax.broadcasted_iota(jnp.int32, (experts, span), 0).astype(jnp.float32) + first
    from_row = lax.broadcasted_iota(jnp.int32, (span, span), 0)
    to_row = lax.broadcasted_iota(jnp.int32, (span, span), 1)
    earlier = jnp.where(
        (from_row // block == to_row // block) & (from_row < to_row), 1.0, 0.0
    ).astype(jnp.bfloat16)
    codes, gates = [], []
    for j in range(shards):
        named = jnp.zeros((experts, span), jnp.float32)
        gate = jnp.zeros((experts, span), jnp.float32)
        for k in range(top):
            hit = meta[j, k : k + 1, :] == number
            named = jnp.where(hit, 1.0, named)
            gate = jnp.where(hit, meta[j, top + k : top + k + 1, :], gate)
        before = jnp.dot(named.astype(jnp.bfloat16), earlier, preferred_element_type=jnp.float32)
        offset = (owners_ref[j] * capacity).astype(jnp.float32)
        codes.append(jnp.where(named > 0.0, before + offset, -1.0))
        gates.append(gate)
    parts = [slice(m * block, (m + 1) * block) for m in range(micro)]
    return (
        [jnp.concatenate([c[:, part] for c in codes], axis=1) for part in parts],
        [jnp.concatenate([g[:, part] for g in gates], axis=1) for part in parts],
    )


contract_last = (((1,), (1,)), ((), ()))
contract_first = (((0,), (0,)), ((), ()))


def expert_kernel(capacity, group_count, shards, *refs):
    owners_ref, meta_ref = refs[:2]
    token_refs = refs[2 : 2 + shards]
    hidden_ref, u_ref, weight_hbm, amap_ref, bmap_hbm = refs[2 + shards : 7 + shards]
    hg_ref, rk_ref = refs[7 + shards : 9 + shards]
    la_refs = refs[9 + shards : 9 + shards + group_count]
    dy_s, wb_s, rows_s, code_s, gate_s, back_s, dy_sem, w_sem, b_sem = refs[
        9 + shards + group_count :
    ]
    twice_top, span = meta_ref.shape[1:]
    top = twice_top // 2
    micro, experts, slots, units = hidden_ref.shape
    rank = amap_ref.shape[1]
    width = dy_s.shape[2]
    block = span // micro
    padded = rows_s.shape[1] // micro
    first = (lax.axis_index("expert") * experts).astype(jnp.float32)
    group = lax.axis_index("dp")

    token_copies = [
        pltpu.make_async_copy(token_refs[i].at[pl.ds(0, span)], dy_s.at[i], dy_sem.at[i])
        for i in range(shards)
    ]
    for copy in token_copies:
        copy.start()

    def weight_copies(x):
        return (
            pltpu.make_async_copy(weight_hbm.at[x], wb_s.at[x, pl.ds(0, units)], w_sem.at[x]),
            pltpu.make_async_copy(bmap_hbm.at[x], wb_s.at[x, pl.ds(units, rank)], b_sem.at[x]),
        )

    for x in range(experts):
        for copy in weight_copies(x):
            copy.start()

    codes, gates = slot_codes(meta_ref[...], owners_ref, first, capacity, experts, micro)
    slot_of = lax.broadcasted_iota(jnp.int32, (padded, shards * block), 0).astype(jnp.float32)
    picks = []
    for m in range(micro):
        code_s[m] = codes[m]
        chosen = []
        for x in range(experts):
            hit = codes[m][x : x + 1, :] == slot_of
            chosen.append(jnp.where(hit, 1.0, 0.0).astype(jnp.bfloat16))
            gate_s[x, m * padded : (m + 1) * padded, :] = jnp.sum(
                jnp.where(hit, gates[m][x : x + 1, :], 0.0), axis=1, keepdims=True
            )
        picks.append(jnp.concatenate(chosen, axis=0))

    for copy in token_copies:
        copy.wait()
    tile = 512 if width % 512 == 0 else width
    for m in range(micro):
        for n in range(width // tile):
            cols = slice(n * tile, (n + 1) * tile)
            tokens = jnp.concatenate(
                [dy_s[i, m * block : (m + 1) * block, cols] for i in range(shards)], axis=0
            )
            rows = jnp.dot(picks[m], tokens, preferred_element_type=jnp.float32)
            rows_s[:, m * padded : (m + 1) * padded, cols] = rows.astype(jnp.bfloat16).reshape(
                experts, padded, tile
            )

    def one_expert(x):
        rows = rows_s[x]
        both = lax.dot_general(rows, wb_s[x], contract_last, preferred_element_type=jnp.float32)
        main = both[:, :units]
        v = both[:, units:].astype(jnp.bfloat16)
        low = jnp.dot(v, amap_ref[x], preferred_element_type=jnp.float32)
        gate = gate_s[x]
        grad = (gate * (main + adapter_scale * low)).astype(jnp.bfloat16)
        filler = jnp.zeros((padded - slots, units), jnp.float32)
        pieces = []
        for m in range(micro):
            hg_ref[m, x] = grad[m * padded : m * padded + slots]
            pieces.append(hidden_ref[m, x].astype(jnp.float32))
            pieces.append(filler)
        held_wide = jnp.concatenate(pieces, axis=0)
        held = held_wide.astype(jnp.bfloat16)
        v_wide = v.astype(jnp.float32)
        routed = jnp.sum(main * held_wide, axis=1, keepdims=True) + adapter_scale * jnp.sum(
            u_ref[x].astype(jnp.float32) * v_wide, axis=1, keepdims=True
        )
        for m in range(micro):
            hit = code_s[m, pl.ds(x, 1), :] == slot_of
            back_s[m, pl.ds(x, 1), :] = jnp.sum(
                jnp.where(hit, routed[m * padded : (m + 1) * padded], 0.0), axis=0, keepdims=True
            )
        w = (gate * v_wide).astype(jnp.bfloat16)
        la = adapter_scale * lax.dot_general(
            w, held, contract_first, preferred_element_type=jnp.float32
        )
        share = units // group_count
        for s in range(group_count):
            aim = lax.rem(group + s, group_count)
            mine = la[:, :share]
            for k in range(1, group_count):
                mine = jnp.where(aim == k, la[:, k * share : (k + 1) * share], mine)
            la_refs[s][x] = mine.astype(la_refs[s].dtype)

    batch = 2 if experts % 2 == 0 else 1

    def some_experts(step, carry):
        for i in range(batch):
            for copy in weight_copies(step * batch + i):
                copy.wait()
        for i in range(batch):
            one_expert(step * batch + i)
        return carry

    lax.fori_loop(0, experts // batch, some_experts, 0)

    number = lax.broadcasted_iota(jnp.int32, (experts, span), 0).astype(jnp.float32) + first
    for i in range(shards):
        back = jnp.concatenate(
            [back_s[m, :, i * block : (i + 1) * block] for m in range(micro)], axis=1
        )
        found = [
            jnp.sum(
                jnp.where(meta_ref[i, k : k + 1, :] == number, back, 0.0), axis=0, keepdims=True
            )
            for k in range(top)
        ]
        rk_ref[owners_ref[i]] = jnp.concatenate(found, axis=0)


def adapter_kernel(capacity, micro, group_count, shards, *refs):
    owners_ref, meta_ref = refs[:2]
    token_refs = refs[2 : 2 + shards]
    near_refs = refs[2 + shards : 1 + shards + group_count]
    far_refs = refs[1 + shards + group_count : shards + 2 * group_count]
    u_refs = refs[shards + 2 * group_count : shards + 3 * group_count]
    lb_ref, tok_s, q_s, u_s, sem = refs[shards + 3 * group_count :]
    span = meta_ref.shape[3]
    experts, tall, rank = u_refs[0].shape
    share = lb_ref.shape[2]
    half = shards // 2
    padded = tall // micro
    block = span // micro
    first = (lax.axis_index("expert") * experts).astype(jnp.float32)
    group = lax.axis_index("dp")
    cols = pl.ds(pl.multiple_of(group * share, share), share)
    copies = []
    for g in range(group_count):
        for i in range(shards):
            if g == 0:
                source = token_refs[i].at[pl.ds(0, span), cols]
            elif i < half:
                source = near_refs[g - 1].at[i, pl.ds(0, span)]
            else:
                source = far_refs[g - 1].at[i - half, pl.ds(0, span)]
            copies.append(pltpu.make_async_copy(source, tok_s.at[g, i], sem.at[g, i]))
    for copy in copies:
        copy.start()
    slot_of = lax.broadcasted_iota(jnp.int32, (padded, shards * block), 0).astype(jnp.float32)
    for g in range(group_count):
        u_s[:, g * tall : (g + 1) * tall, :] = u_refs[g][...]
        codes, gates = slot_codes(meta_ref[g], owners_ref, first, capacity, experts, micro)
        for i in range(shards):
            copies[g * shards + i].wait()
        for m in range(micro):
            picks = jnp.concatenate(
                [
                    jnp.where(
                        codes[m][x : x + 1, :] == slot_of, gates[m][x : x + 1, :], 0.0
                    ).astype(jnp.bfloat16)
                    for x in range(experts)
                ],
                axis=0,
            )
            tokens = jnp.concatenate(
                [tok_s[g, i, m * block : (m + 1) * block, :] for i in range(shards)], axis=0
            )
            q = jnp.dot(picks, tokens, preferred_element_type=jnp.float32).astype(jnp.bfloat16)
            at = g * tall + m * padded
            q_s[:, at : at + padded, :] = q.reshape(experts, padded, share)
    for x in range(experts):
        lb_ref[x] = adapter_scale * lax.dot_general(
            u_s[x], q_s[x], contract_first, preferred_element_type=jnp.float32
        )


def ring_order(count):
    return list(range(0, count, 2)) + list(range(1, count, 2))[::-1]


def local_by_tokens(
    output_gradient,
    chosen_expert_index,
    routing_gate_weight,
    hidden,
    frozen_down_weight,
    adapter_input_map,
    adapter_output_map,
):
    sources = lax.axis_size("expert")
    group_count = lax.axis_size("dp")
    micro, experts, slots, units = hidden.shape
    span, top = chosen_expert_index.shape
    width = output_gradient.shape[1]
    rank = adapter_input_map.shape[2]
    capacity = slots // sources
    block = span // micro
    padded = pad_rows(slots)
    share = width // group_count
    pairs = sources // 2
    me = lax.axis_index("expert")
    group = lax.axis_index("dp")

    order = ring_order(pairs)
    place = {z: i for i, z in enumerate(order)}
    ring = [
        (2 * z + c, 2 * order[(place[z] + 1) % pairs] + c) for z in range(pairs) for c in range(2)
    ]
    swap = [(e, e ^ 1) for e in range(sources)]
    owner_table = [
        [
            2 * order[(place[e // 2] - i) % pairs] + (e % 2 if near else 1 - e % 2)
            for near in (True, False)
            for i in range(pairs)
        ]
        for e in range(sources)
    ]
    owners = jnp.asarray(owner_table, jnp.int32)[me]

    amap = jnp.swapaxes(adapter_input_map, 1, 2)
    u = jnp.einsum("mesk,exk->emsx", hidden, amap, preferred_element_type=jnp.float32)
    u = u.astype(jnp.bfloat16)
    u = jnp.pad(u, ((0, 0), (0, 0), (0, padded - slots), (0, 0))).reshape(
        experts, micro * padded, rank
    )

    def shift_groups(array, by):
        return lax.ppermute(
            array, "dp", [(d, (d + by) % group_count) for d in range(group_count)]
        )

    u_all = [u] + [shift_groups(u, s) for s in range(1, group_count)]

    names = jnp.concatenate(
        [chosen_expert_index.T.astype(jnp.bfloat16), routing_gate_weight.T], axis=0
    )
    lines = 2 * top * span // share
    names = jnp.tile(names.reshape(lines, share), (1, group_count))
    extra = -(-lines // 8) * 8
    sent = jnp.concatenate(
        [output_gradient, jnp.pad(names, ((0, extra - lines), (0, 0)))], axis=0
    )

    near = [sent]
    for _ in range(pairs - 1):
        near.append(lax.ppermute(near[-1], "expert", ring))
    far = [lax.ppermute(piece, "expert", swap) for piece in near]
    pieces = near + far

    def names_of(piece):
        return piece[..., span : span + lines, :share].reshape(
            piece.shape[:-2] + (2 * top, span)
        )

    own_meta = jnp.stack([names_of(piece) for piece in pieces]).astype(jnp.float32)

    crossing, returned = [], []
    for s in range(1, group_count):
        aim = lax.rem(group + s, group_count) * share
        columns = jnp.stack(
            [lax.dynamic_slice_in_dim(piece, aim, share, axis=1) for piece in near]
        )
        crossing.append(shift_groups(columns, s))
    for columns in crossing:
        returned.append(lax.ppermute(columns, "expert", swap))
    all_meta = jnp.concatenate(
        [own_meta[None]]
        + [
            jnp.concatenate([names_of(a), names_of(b)], axis=0)[None].astype(jnp.float32)
            for a, b in zip(crossing, returned)
        ],
        axis=0,
    )

    vmem = pl.BlockSpec(memory_space=pltpu.VMEM)
    smem = pl.BlockSpec(memory_space=pltpu.SMEM)
    anywhere = pl.BlockSpec(memory_space=pl.ANY)
    part_a = jax.ShapeDtypeStruct((experts, rank, units // group_count), jnp.bfloat16)
    hidden_grad, routed, *parts = pl.pallas_call(
        functools.partial(expert_kernel, capacity, group_count, sources),
        out_shape=(
            jax.ShapeDtypeStruct(hidden.shape, jnp.bfloat16),
            jax.ShapeDtypeStruct((sources, top, span), jnp.float32),
        )
        + (part_a,) * group_count,
        in_specs=[smem, vmem] + [anywhere] * sources + [vmem, vmem, anywhere, vmem, anywhere],
        out_specs=(vmem,) * (2 + group_count),
        scratch_shapes=[
            pltpu.VMEM((sources, span, width), jnp.bfloat16),
            pltpu.VMEM((experts, units + rank, width), jnp.bfloat16),
            pltpu.VMEM((experts, micro * padded, width), jnp.bfloat16),
            pltpu.VMEM((micro, experts, sources * block), jnp.float32),
            pltpu.VMEM((experts, micro * padded, 1), jnp.float32),
            pltpu.VMEM((micro, experts, sources * block), jnp.float32),
            pltpu.SemaphoreType.DMA((sources,)),
            pltpu.SemaphoreType.DMA((experts,)),
            pltpu.SemaphoreType.DMA((experts,)),
        ],
        compiler_params=pltpu.CompilerParams(vmem_limit_bytes=58 * 1024 * 1024),
        cost_estimate=pl.CostEstimate(
            flops=2 * experts * micro * padded * width * (units + rank + sources * block),
            bytes_accessed=2 * experts * width * (units + rank) + 2 * sources * span * width,
            transcendentals=0,
        ),
        name="expert_rows",
    )(owners, own_meta, *pieces, hidden, u, frozen_down_weight, amap, adapter_output_map)

    home = lax.all_to_all(routed, "expert", split_axis=0, concat_axis=0, tiled=True)
    router_grad = jnp.sum(home, axis=0).T
    lora_a = parts[0].astype(jnp.float32)
    for s in range(1, group_count):
        lora_a = lora_a + shift_groups(parts[s], s).astype(jnp.float32)

    lora_b = pl.pallas_call(
        functools.partial(adapter_kernel, capacity, micro, group_count, sources),
        out_shape=jax.ShapeDtypeStruct((experts, rank, share), jnp.float32),
        in_specs=[smem, vmem]
        + [anywhere] * (sources + 2 * (group_count - 1))
        + [vmem] * group_count,
        out_specs=vmem,
        scratch_shapes=[
            pltpu.VMEM((group_count, sources, span, share), jnp.bfloat16),
            pltpu.VMEM((experts, group_count * micro * padded, share), jnp.bfloat16),
            pltpu.VMEM((experts, group_count * micro * padded, rank), jnp.bfloat16),
            pltpu.SemaphoreType.DMA((group_count, sources)),
        ],
        compiler_params=pltpu.CompilerParams(vmem_limit_bytes=40 * 1024 * 1024),
        cost_estimate=pl.CostEstimate(
            flops=2 * experts * micro * padded * share * group_count * (rank + sources * block),
            bytes_accessed=2 * group_count * sources * span * share + 4 * experts * rank * share,
            transcendentals=0,
        ),
        name="adapter_columns",
    )(owners, all_meta, *pieces, *crossing, *returned, *u_all)
    return (hidden_grad, router_grad, lora_a, lora_b)


def local(*arrays):
    sources, groups = lax.axis_size("expert"), lax.axis_size("dp")
    span, width = arrays[0].shape
    top, (micro, experts, slots, units) = arrays[1].shape[1], arrays[3].shape
    even = sources % 2 == 0 and width % (128 * groups) == 0 and units % groups == 0
    packs = 2 * top * span % (width // groups) == 0 and (width // groups) % span == 0
    exact = experts * sources <= 256
    if even and packs and exact and sources * span <= micro * experts * slots:
        return local_by_tokens(*arrays)
    return local_by_slots(*arrays)


def solution(mesh):
    in_specs = (
        P(("dp", "expert"), None),
        P(("dp", "expert"), None),
        P(("dp", "expert"), None),
        P(None, ("dp", "expert"), None, None),
        P("expert", None, None),
        P("expert", None, None),
        P("expert", None, None),
    )
    out_specs = (
        P(None, ("dp", "expert"), None, None),
        P(("dp", "expert"), None),
        P("expert", None, "dp"),
        P("expert", None, "dp"),
    )
    return jax.shard_map(local, mesh=mesh, in_specs=in_specs, out_specs=out_specs, check_vma=False)
```

```python
import functools

import jax
import jax.numpy as jnp
from jax import lax
from jax.experimental import pallas as pl
from jax.experimental.pallas import tpu as pltpu
from jax.sharding import PartitionSpec as P

adapter_scale = 2.0


def slot_rows(id_rows, experts, per_device, sources, capacity):
    onehot = (id_rows[:, :, None] == jnp.arange(experts, dtype=jnp.int32)[None, None, :]).astype(
        jnp.int32
    )
    before = jnp.sum(jnp.cumsum(onehot, axis=1) * onehot, axis=2) - 1
    target_dev = id_rows // per_device
    target_slot = id_rows % per_device
    return (target_slot * sources + target_dev) * capacity + before


def pick_rows(source, indices):
    return source[indices]


def dispatch_buffers(grad_rows, weight_rows, send_rows, top_count, buffer_len):
    entry_count = send_rows.shape[1]
    token_count = grad_rows.shape[1]
    filler = jnp.full((buffer_len,), entry_count, jnp.int32)

    def invert(rows):
        return filler.at[rows].set(jnp.arange(entry_count, dtype=jnp.int32))

    table = jax.vmap(invert)(send_rows)
    padded_grad = jnp.concatenate(
        [grad_rows, jnp.zeros((grad_rows.shape[0], 1, grad_rows.shape[2]), grad_rows.dtype)], axis=1
    )
    padded_weight = jnp.concatenate(
        [weight_rows, jnp.zeros((weight_rows.shape[0], 1), weight_rows.dtype)], axis=1
    )
    token_pick = jnp.where(table < entry_count, table // top_count, token_count)
    sent_grad = jax.vmap(pick_rows)(padded_grad, token_pick)
    sent_weight = jax.vmap(pick_rows)(padded_weight, table)
    return (sent_grad, sent_weight)


def expert_rows_view(
    received_gradient,
    received_weight,
    retained_rows,
    frozen_down_weight,
    adapter_input_map,
    adapter_output_map,
):
    frozen_term = jnp.einsum(
        "mesd,efd->mesf", received_gradient, frozen_down_weight, preferred_element_type=jnp.float32
    )
    across_product = jnp.einsum(
        "hati,aki->hatk", received_gradient, adapter_output_map, preferred_element_type=jnp.float32
    ).astype(jnp.bfloat16)
    low_rank_state = jnp.einsum(
        "ptqv,tgv->ptqg", across_product, adapter_input_map, preferred_element_type=jnp.float32
    )
    capacity_slot_weight = received_weight.astype(jnp.float32)[..., None]
    hidden_state_gradient = (
        capacity_slot_weight * (frozen_term + adapter_scale * low_rank_state)
    ).astype(jnp.bfloat16)
    down_mapping = jnp.einsum(
        "lkgu,kup->lkgp", retained_rows, adapter_input_map, preferred_element_type=jnp.float32
    ).astype(jnp.bfloat16)
    complete_term = jnp.sum(frozen_term * retained_rows.astype(jnp.float32), axis=-1)
    adapter_term = jnp.einsum(
        "mesr,mesr->mes", down_mapping, across_product, preferred_element_type=jnp.float32
    )
    routing_rows = complete_term + adapter_scale * adapter_term
    scaled_gradient = (capacity_slot_weight * received_gradient).astype(jnp.bfloat16)
    scaled_across_product = (capacity_slot_weight * across_product.astype(jnp.float32)).astype(
        jnp.bfloat16
    )
    adapter_output_gradient = adapter_scale * jnp.einsum(
        "mesr,mesd->erd", down_mapping, scaled_gradient, preferred_element_type=jnp.float32
    )
    adapter_input_gradient = adapter_scale * jnp.einsum(
        "mesr,mesf->erf", scaled_across_product, retained_rows, preferred_element_type=jnp.float32
    )
    return (hidden_state_gradient, routing_rows, adapter_input_gradient, adapter_output_gradient)


def local_by_slots(
    output_gradient,
    chosen_expert_index,
    routing_gate_weight,
    hidden,
    frozen_down_weight,
    adapter_input_map,
    adapter_output_map,
):
    sources = lax.axis_size("expert")
    per_device = frozen_down_weight.shape[0]
    experts = per_device * sources
    micro_count = hidden.shape[0]
    slot_count = hidden.shape[2]
    capacity = slot_count // sources
    top_count = chosen_expert_index.shape[1]
    model_width = output_gradient.shape[1]
    buffer_len = experts * capacity
    grad_rows = output_gradient.reshape(micro_count, -1, model_width)
    id_rows = chosen_expert_index.reshape(micro_count, -1)
    weight_rows = routing_gate_weight.reshape(micro_count, -1)
    send_rows = slot_rows(id_rows, experts, per_device, sources, capacity)
    sent_grad, sent_weight = dispatch_buffers(
        grad_rows, weight_rows, send_rows, top_count, buffer_len
    )
    sent_grad = sent_grad.reshape(micro_count, per_device, sources, capacity, model_width)
    sent_weight = sent_weight.reshape(micro_count, per_device, sources, capacity)
    received_gradient, received_weight = (
        lax.all_to_all(sent_grad, "expert", split_axis=2, concat_axis=2, tiled=True),
        lax.all_to_all(sent_weight, "expert", split_axis=2, concat_axis=2, tiled=True),
    )
    received_gradient = received_gradient.reshape(micro_count, per_device, slot_count, model_width)
    received_weight = received_weight.reshape(micro_count, per_device, slot_count)
    hidden_grad, routing_rows, adapter_input_gradient, adapter_output_gradient = expert_rows_view(
        received_gradient,
        received_weight,
        hidden,
        frozen_down_weight,
        adapter_input_map,
        adapter_output_map,
    )
    router_home = lax.all_to_all(
        routing_rows.reshape(micro_count, per_device, sources, capacity),
        "expert",
        split_axis=2,
        concat_axis=2,
        tiled=True,
    )
    router_flat = router_home.reshape(micro_count, buffer_len)
    router_grad = jax.vmap(pick_rows)(router_flat, send_rows).reshape(-1, top_count)
    share_a, share_b = (
        lax.psum_scatter(adapter_input_gradient, "dp", scatter_dimension=2, tiled=True),
        lax.psum_scatter(adapter_output_gradient, "dp", scatter_dimension=2, tiled=True),
    )
    return (hidden_grad, router_grad, share_a, share_b)


def pad_rows(count):
    return -(-count // 16) * 16


def read_names(rows, span, top):
    wide = rows.astype(jnp.float32)
    per = wide.shape[1] // span
    lines = [
        wide[k // per : k // per + 1, (k % per) * span : (k % per + 1) * span]
        for k in range(2 * top)
    ]
    return lines[:top], lines[top:]


def slot_codes(names, owners_ref, first, capacity, experts, micro):
    shards = len(names)
    span = names[0][0][0].shape[1]
    block = span // micro
    number = lax.broadcasted_iota(jnp.int32, (experts, span), 0).astype(jnp.float32) + first
    from_row = lax.broadcasted_iota(jnp.int32, (span, span), 0)
    to_row = lax.broadcasted_iota(jnp.int32, (span, span), 1)
    earlier = jnp.where(
        (from_row // block == to_row // block) & (from_row < to_row), 1.0, 0.0
    ).astype(jnp.bfloat16)
    codes, gates = [], []
    for j in range(shards):
        named = jnp.zeros((experts, span), jnp.float32)
        gate = jnp.zeros((experts, span), jnp.float32)
        for name, weight in zip(*names[j]):
            hit = name == number
            named = jnp.where(hit, 1.0, named)
            gate = jnp.where(hit, weight, gate)
        before = jnp.dot(named.astype(jnp.bfloat16), earlier, preferred_element_type=jnp.float32)
        offset = (owners_ref[j] * capacity).astype(jnp.float32)
        codes.append(jnp.where(named > 0.0, before + offset, -1.0))
        gates.append(gate)
    parts = [slice(m * block, (m + 1) * block) for m in range(micro)]
    return (
        [jnp.concatenate([c[:, part] for c in codes], axis=1) for part in parts],
        [jnp.concatenate([g[:, part] for g in gates], axis=1) for part in parts],
    )


contract_last = (((1,), (1,)), ((), ()))
contract_first = (((0,), (0,)), ((), ()))


def expert_kernel(capacity, group_count, shards, *refs):
    owners_ref = refs[0]
    token_refs = refs[1 : 1 + shards]
    hidden_ref, u_ref, weight_hbm, amap_ref, bmap_hbm = refs[1 + shards : 6 + shards]
    hg_ref, rk_ref = refs[6 + shards : 8 + shards]
    la_refs = refs[8 + shards : 8 + shards + group_count]
    dy_s, wb_s, rows_s, code_s, gate_s, back_s, dy_sem, w_sem, b_sem = refs[
        8 + shards + group_count :
    ]
    top, span = rk_ref.shape[1:]
    micro, experts, slots, units = hidden_ref.shape
    rank = amap_ref.shape[1]
    width = dy_s.shape[2]
    block = span // micro
    padded = rows_s.shape[1] // micro
    first = (lax.axis_index("expert") * experts).astype(jnp.float32)
    group = lax.axis_index("dp")

    token_copies = [
        pltpu.make_async_copy(token_refs[i], dy_s.at[i], dy_sem.at[i])
        for i in range(shards)
    ]
    for copy in token_copies:
        copy.start()

    def weight_copies(x):
        return (
            pltpu.make_async_copy(weight_hbm.at[x], wb_s.at[x, pl.ds(0, units)], w_sem.at[x]),
            pltpu.make_async_copy(bmap_hbm.at[x], wb_s.at[x, pl.ds(units, rank)], b_sem.at[x]),
        )

    for x in range(experts):
        for copy in weight_copies(x):
            copy.start()

    for copy in token_copies:
        copy.wait()
    names = [
        read_names(dy_s[i, span:, : width // group_count], span, top) for i in range(shards)
    ]
    codes, gates = slot_codes(names, owners_ref, first, capacity, experts, micro)
    slot_of = lax.broadcasted_iota(jnp.int32, (padded, shards * block), 0).astype(jnp.float32)
    picks = []
    for m in range(micro):
        code_s[m] = codes[m]
        chosen = []
        for x in range(experts):
            hit = codes[m][x : x + 1, :] == slot_of
            chosen.append(jnp.where(hit, 1.0, 0.0).astype(jnp.bfloat16))
            gate_s[x, m * padded : (m + 1) * padded, :] = jnp.sum(
                jnp.where(hit, gates[m][x : x + 1, :], 0.0), axis=1, keepdims=True
            )
        picks.append(jnp.concatenate(chosen, axis=0))

    tile = 512 if width % 512 == 0 else width
    for m in range(micro):
        for n in range(width // tile):
            cols = slice(n * tile, (n + 1) * tile)
            tokens = jnp.concatenate(
                [dy_s[i, m * block : (m + 1) * block, cols] for i in range(shards)], axis=0
            )
            rows = jnp.dot(picks[m], tokens, preferred_element_type=jnp.float32)
            rows_s[:, m * padded : (m + 1) * padded, cols] = rows.astype(jnp.bfloat16).reshape(
                experts, padded, tile
            )

    def one_expert(x, lanes):
        both = lax.dot_general(
            wb_s[x], rows_s[x], contract_last, preferred_element_type=jnp.float32
        ).T
        main = both[:, :units]
        v = both[:, units:].astype(jnp.bfloat16)
        low = jnp.dot(v, amap_ref[x], preferred_element_type=jnp.float32)
        gate = gate_s[x]
        grad = (gate * (main + adapter_scale * low)).astype(jnp.bfloat16)
        filler = jnp.zeros((padded - slots, units), jnp.float32)
        pieces = []
        for m in range(micro):
            hg_ref[m, x] = grad[m * padded : m * padded + slots]
            pieces.append(hidden_ref[m, x].astype(jnp.float32))
            pieces.append(filler)
        held_wide = jnp.concatenate(pieces, axis=0)
        held = held_wide.astype(jnp.bfloat16)
        v_wide = v.astype(jnp.float32)
        routed = jnp.sum(main * held_wide, axis=1, keepdims=True) + adapter_scale * jnp.sum(
            u_ref[lax.rem(x, experts // 2), :, lanes].astype(jnp.float32) * v_wide, axis=1, keepdims=True
        )
        for m in range(micro):
            hit = code_s[m, pl.ds(x, 1), :] == slot_of
            back_s[m, pl.ds(x, 1), :] = jnp.sum(
                jnp.where(hit, routed[m * padded : (m + 1) * padded], 0.0), axis=0, keepdims=True
            )
        w = (gate * v_wide).astype(jnp.bfloat16)
        la = adapter_scale * lax.dot_general(
            w, held, contract_first, preferred_element_type=jnp.float32
        )
        share = units // group_count
        for s in range(group_count):
            aim = lax.rem(group + s, group_count)
            mine = la[:, :share]
            for k in range(1, group_count):
                mine = jnp.where(aim == k, la[:, k * share : (k + 1) * share], mine)
            la_refs[s][x] = mine.astype(la_refs[s].dtype)

    half = experts // 2

    def two_experts(x, carry):
        for copy in weight_copies(x) + weight_copies(x + half):
            copy.wait()
        one_expert(x, slice(0, rank))
        one_expert(x + half, slice(rank, 2 * rank))
        return carry

    lax.fori_loop(0, half, two_experts, 0)

    number = lax.broadcasted_iota(jnp.int32, (experts, span), 0).astype(jnp.float32) + first
    for i in range(shards):
        back = jnp.concatenate(
            [back_s[m, :, i * block : (i + 1) * block] for m in range(micro)], axis=1
        )
        found = [
            jnp.sum(
                jnp.where(name == number, back, 0.0), axis=0, keepdims=True
            )
            for name in names[i][0]
        ]
        rk_ref[owners_ref[i]] = jnp.concatenate(found, axis=0)


def adapter_kernel(capacity, micro, span, top, group_count, shards, *refs):
    others = group_count - 1
    pairs = shards // 2
    early = pairs // 2
    owners_ref = refs[0]
    token_refs = refs[1 : 1 + shards]
    early_refs = refs[1 + shards : 1 + shards + others]
    late_refs = refs[1 + shards + others : 1 + shards + 2 * others]
    swapped_refs = refs[1 + shards + 2 * others : 1 + shards + 3 * others]
    u_refs = refs[1 + shards + 3 * others : 2 + shards + 4 * others]
    lb_ref, tok_s, q_s, sem = refs[2 + shards + 4 * others :]
    experts, rank, share = lb_ref.shape
    tall = u_refs[0].shape[1]
    padded = tall // micro
    block = span // micro
    first = (lax.axis_index("expert") * experts).astype(jnp.float32)
    group = lax.axis_index("dp")
    cols = pl.ds(pl.multiple_of(group * share, share), share)
    copies = []
    for g in range(group_count):
        for i in range(shards):
            far, k = i // pairs, i % pairs
            if g == 0:
                source = token_refs[i].at[:, cols]
            elif k < early:
                source = early_refs[g - 1].at[far * early + k]
            else:
                source = (swapped_refs if far else late_refs)[g - 1].at[k - early]
            copies.append(pltpu.make_async_copy(source, tok_s.at[g, i], sem.at[g, i]))
    for copy in copies:
        copy.start()
    slot_of = lax.broadcasted_iota(jnp.int32, (padded, shards * block), 0).astype(jnp.float32)
    for g in range(group_count):
        for i in range(shards):
            copies[g * shards + i].wait()
        names = [read_names(tok_s[g, i, span:, :], span, top) for i in range(shards)]
        codes, gates = slot_codes(names, owners_ref, first, capacity, experts, micro)
        for m in range(micro):
            picks = jnp.concatenate(
                [
                    jnp.where(
                        codes[m][x : x + 1, :] == slot_of, gates[m][x : x + 1, :], 0.0
                    ).astype(jnp.bfloat16)
                    for x in range(experts)
                ],
                axis=0,
            )
            tokens = jnp.concatenate(
                [tok_s[g, i, m * block : (m + 1) * block, :] for i in range(shards)], axis=0
            )
            q = jnp.dot(picks, tokens, preferred_element_type=jnp.float32).astype(jnp.bfloat16)
            at = g * tall + m * padded
            q_s[:, at : at + padded, :] = q.reshape(experts, padded, share)
    half = experts // 2
    for x in range(half):
        both = jnp.concatenate([u_refs[g][x] for g in range(group_count)], axis=0)
        lb_ref[x] = adapter_scale * lax.dot_general(
            both[:, :rank], q_s[x], contract_first, preferred_element_type=jnp.float32
        )
        lb_ref[x + half] = adapter_scale * lax.dot_general(
            both[:, rank:], q_s[x + half], contract_first, preferred_element_type=jnp.float32
        )


def ring_order(count):
    return list(range(0, count, 2)) + list(range(1, count, 2))[::-1]


def local_by_tokens(
    output_gradient,
    chosen_expert_index,
    routing_gate_weight,
    hidden,
    frozen_down_weight,
    adapter_input_map,
    adapter_output_map,
):
    sources = lax.axis_size("expert")
    group_count = lax.axis_size("dp")
    micro, experts, slots, units = hidden.shape
    span, top = chosen_expert_index.shape
    width = output_gradient.shape[1]
    rank = adapter_input_map.shape[2]
    capacity = slots // sources
    block = span // micro
    padded = pad_rows(slots)
    share = width // group_count
    pairs = sources // 2
    me = lax.axis_index("expert")
    group = lax.axis_index("dp")

    order = ring_order(pairs)
    place = {z: i for i, z in enumerate(order)}
    ring = [
        (2 * z + c, 2 * order[(place[z] + 1) % pairs] + c) for z in range(pairs) for c in range(2)
    ]
    swap = [(e, e ^ 1) for e in range(sources)]
    owner_table = [
        [
            2 * order[(place[e // 2] - i) % pairs] + (e % 2 if near else 1 - e % 2)
            for near in (True, False)
            for i in range(pairs)
        ]
        for e in range(sources)
    ]
    owners = jnp.asarray(owner_table, jnp.int32)[me]

    amap = jnp.swapaxes(adapter_input_map, 1, 2)
    u = jnp.einsum("mesk,exk->emsx", hidden, amap, preferred_element_type=jnp.float32)
    u = u.astype(jnp.bfloat16)
    u = jnp.pad(u, ((0, 0), (0, 0), (0, padded - slots), (0, 0))).reshape(
        2, experts // 2, micro * padded, rank
    )
    u = jnp.concatenate([u[0], u[1]], axis=-1)

    def shift_groups(array, by):
        return lax.ppermute(
            array, "dp", [(d, (d + by) % group_count) for d in range(group_count)]
        )

    def swap_partners(array):
        return lax.ppermute(array, "expert", swap)

    def columns_for(group_shift, chosen):
        aim = lax.rem(group + group_shift, group_count) * share
        return jnp.stack(
            [lax.dynamic_slice_in_dim(piece, aim, share, axis=1) for piece in chosen]
        )

    others = range(1, group_count)
    u_all = [u] + [shift_groups(u, s) for s in others]

    names = jnp.concatenate(
        [chosen_expert_index.T.astype(jnp.bfloat16), routing_gate_weight.T], axis=0
    )
    lines = 2 * top * span // share
    names = jnp.tile(names.reshape(lines, share), (1, group_count))
    extra = -(-lines // 8) * 8
    sent = jnp.concatenate(
        [output_gradient, jnp.pad(names, ((0, extra - lines), (0, 0)))], axis=0
    )

    early = pairs // 2
    near, far = [sent], []
    for step in range(pairs - 1):
        ahead = near[-1]
        if step == pairs - 2:
            ahead, *u_all = lax.optimization_barrier((ahead, *u_all))
        near.append(lax.ppermute(ahead, "expert", ring))
        far.append(swap_partners(near[step]))
    far.append(swap_partners(near[-1]))
    early_columns = [
        shift_groups(columns_for(s, near[:early] + far[:early]), s) for s in others
    ]
    late_columns = [shift_groups(columns_for(s, near[early:]), s) for s in others]
    pieces = near + far

    vmem = pl.BlockSpec(memory_space=pltpu.VMEM)
    smem = pl.BlockSpec(memory_space=pltpu.SMEM)
    anywhere = pl.BlockSpec(memory_space=pl.ANY)
    part_a = jax.ShapeDtypeStruct((experts, rank, units // group_count), jnp.bfloat16)
    hidden_grad, routed, *parts = pl.pallas_call(
        functools.partial(expert_kernel, capacity, group_count, sources),
        out_shape=(
            jax.ShapeDtypeStruct(hidden.shape, jnp.bfloat16),
            jax.ShapeDtypeStruct((sources, top, span), jnp.float32),
        )
        + (part_a,) * group_count,
        in_specs=[smem] + [anywhere] * sources + [vmem, vmem, anywhere, vmem, anywhere],
        out_specs=(vmem,) * (2 + group_count),
        scratch_shapes=[
            pltpu.VMEM((sources, span + extra, width), jnp.bfloat16),
            pltpu.VMEM((experts, units + rank, width), jnp.bfloat16),
            pltpu.VMEM((experts, micro * padded, width), jnp.bfloat16),
            pltpu.VMEM((micro, experts, sources * block), jnp.float32),
            pltpu.VMEM((experts, micro * padded, 1), jnp.float32),
            pltpu.VMEM((micro, experts, sources * block), jnp.float32),
            pltpu.SemaphoreType.DMA((sources,)),
            pltpu.SemaphoreType.DMA((experts,)),
            pltpu.SemaphoreType.DMA((experts,)),
        ],
        compiler_params=pltpu.CompilerParams(vmem_limit_bytes=58 * 1024 * 1024),
        cost_estimate=pl.CostEstimate(
            flops=2 * experts * micro * padded * width * (units + rank + sources * block),
            bytes_accessed=2 * experts * width * (units + rank) + 2 * sources * span * width,
            transcendentals=0,
        ),
        name="expert_rows",
    )(owners, *pieces, hidden, u, frozen_down_weight, amap, adapter_output_map)

    late_columns, parts = lax.optimization_barrier((late_columns, parts))
    swapped = [swap_partners(columns) for columns in late_columns]
    home = lax.all_to_all(routed, "expert", split_axis=0, concat_axis=0, tiled=True)
    arrived = [shift_groups(parts[s], s) for s in others]

    lora_b = pl.pallas_call(
        functools.partial(adapter_kernel, capacity, micro, span, top, group_count, sources),
        out_shape=jax.ShapeDtypeStruct((experts, rank, share), jnp.float32),
        in_specs=[smem]
        + [anywhere] * (sources + 3 * (group_count - 1))
        + [vmem] * group_count,
        out_specs=vmem,
        scratch_shapes=[
            pltpu.VMEM((group_count, sources, span + extra, share), jnp.bfloat16),
            pltpu.VMEM((experts, group_count * micro * padded, share), jnp.bfloat16),
            pltpu.SemaphoreType.DMA((group_count, sources)),
        ],
        compiler_params=pltpu.CompilerParams(vmem_limit_bytes=40 * 1024 * 1024),
        cost_estimate=pl.CostEstimate(
            flops=2 * experts * micro * padded * share * group_count * (rank + sources * block),
            bytes_accessed=2 * group_count * sources * span * share + 4 * experts * rank * share,
            transcendentals=0,
        ),
        name="adapter_columns",
    )(owners, *pieces, *early_columns, *late_columns, *swapped, *u_all)

    home, arrived, lora_b = lax.optimization_barrier((home, arrived, lora_b))
    router_grad = jnp.sum(home, axis=0).T
    lora_a = parts[0].astype(jnp.float32)
    for part in arrived:
        lora_a = lora_a + part.astype(jnp.float32)
    return (hidden_grad, router_grad, lora_a, lora_b)


def local(*arrays):
    sources, groups = lax.axis_size("expert"), lax.axis_size("dp")
    span, width = arrays[0].shape
    top, (micro, experts, slots, units) = arrays[1].shape[1], arrays[3].shape
    even = sources % 4 == 0 and experts % 2 == 0 and width % (128 * groups) == 0 and units % groups == 0
    packs = 2 * top * span % (width // groups) == 0 and (width // groups) % span == 0
    exact = experts * sources <= 256
    if even and packs and exact and sources * span <= micro * experts * slots:
        return local_by_tokens(*arrays)
    return local_by_slots(*arrays)


def solution(mesh):
    in_specs = (
        P(("dp", "expert"), None),
        P(("dp", "expert"), None),
        P(("dp", "expert"), None),
        P(None, ("dp", "expert"), None, None),
        P("expert", None, None),
        P("expert", None, None),
        P("expert", None, None),
    )
    out_specs = (
        P(None, ("dp", "expert"), None, None),
        P(("dp", "expert"), None),
        P("expert", None, "dp"),
        P("expert", None, "dp"),
    )
    return jax.shard_map(local, mesh=mesh, in_specs=in_specs, out_specs=out_specs, check_vma=False)
```

```python
import functools

import jax
import jax.numpy as jnp
from jax import lax
from jax.experimental import pallas as pl
from jax.experimental.pallas import tpu as pltpu
from jax.sharding import PartitionSpec as P

adapter_scale = 2.0


def slot_rows(id_rows, experts, per_device, sources, capacity):
    onehot = (id_rows[:, :, None] == jnp.arange(experts, dtype=jnp.int32)[None, None, :]).astype(
        jnp.int32
    )
    before = jnp.sum(jnp.cumsum(onehot, axis=1) * onehot, axis=2) - 1
    target_dev = id_rows // per_device
    target_slot = id_rows % per_device
    return (target_slot * sources + target_dev) * capacity + before


def pick_rows(source, indices):
    return source[indices]


def dispatch_buffers(grad_rows, weight_rows, send_rows, top_count, buffer_len):
    entry_count = send_rows.shape[1]
    token_count = grad_rows.shape[1]
    filler = jnp.full((buffer_len,), entry_count, jnp.int32)

    def invert(rows):
        return filler.at[rows].set(jnp.arange(entry_count, dtype=jnp.int32))

    table = jax.vmap(invert)(send_rows)
    padded_grad = jnp.concatenate(
        [grad_rows, jnp.zeros((grad_rows.shape[0], 1, grad_rows.shape[2]), grad_rows.dtype)], axis=1
    )
    padded_weight = jnp.concatenate(
        [weight_rows, jnp.zeros((weight_rows.shape[0], 1), weight_rows.dtype)], axis=1
    )
    token_pick = jnp.where(table < entry_count, table // top_count, token_count)
    sent_grad = jax.vmap(pick_rows)(padded_grad, token_pick)
    sent_weight = jax.vmap(pick_rows)(padded_weight, table)
    return (sent_grad, sent_weight)


def expert_rows_view(
    received_gradient,
    received_weight,
    retained_rows,
    frozen_down_weight,
    adapter_input_map,
    adapter_output_map,
):
    frozen_term = jnp.einsum(
        "mesd,efd->mesf", received_gradient, frozen_down_weight, preferred_element_type=jnp.float32
    )
    across_product = jnp.einsum(
        "hati,aki->hatk", received_gradient, adapter_output_map, preferred_element_type=jnp.float32
    ).astype(jnp.bfloat16)
    low_rank_state = jnp.einsum(
        "ptqv,tgv->ptqg", across_product, adapter_input_map, preferred_element_type=jnp.float32
    )
    capacity_slot_weight = received_weight.astype(jnp.float32)[..., None]
    hidden_state_gradient = (
        capacity_slot_weight * (frozen_term + adapter_scale * low_rank_state)
    ).astype(jnp.bfloat16)
    down_mapping = jnp.einsum(
        "lkgu,kup->lkgp", retained_rows, adapter_input_map, preferred_element_type=jnp.float32
    ).astype(jnp.bfloat16)
    complete_term = jnp.sum(frozen_term * retained_rows.astype(jnp.float32), axis=-1)
    adapter_term = jnp.einsum(
        "mesr,mesr->mes", down_mapping, across_product, preferred_element_type=jnp.float32
    )
    routing_rows = complete_term + adapter_scale * adapter_term
    scaled_gradient = (capacity_slot_weight * received_gradient).astype(jnp.bfloat16)
    scaled_across_product = (capacity_slot_weight * across_product.astype(jnp.float32)).astype(
        jnp.bfloat16
    )
    adapter_output_gradient = adapter_scale * jnp.einsum(
        "mesr,mesd->erd", down_mapping, scaled_gradient, preferred_element_type=jnp.float32
    )
    adapter_input_gradient = adapter_scale * jnp.einsum(
        "mesr,mesf->erf", scaled_across_product, retained_rows, preferred_element_type=jnp.float32
    )
    return (hidden_state_gradient, routing_rows, adapter_input_gradient, adapter_output_gradient)


def local_by_slots(
    output_gradient,
    chosen_expert_index,
    routing_gate_weight,
    hidden,
    frozen_down_weight,
    adapter_input_map,
    adapter_output_map,
):
    sources = lax.axis_size("expert")
    per_device = frozen_down_weight.shape[0]
    experts = per_device * sources
    micro_count = hidden.shape[0]
    slot_count = hidden.shape[2]
    capacity = slot_count // sources
    top_count = chosen_expert_index.shape[1]
    model_width = output_gradient.shape[1]
    buffer_len = experts * capacity
    grad_rows = output_gradient.reshape(micro_count, -1, model_width)
    id_rows = chosen_expert_index.reshape(micro_count, -1)
    weight_rows = routing_gate_weight.reshape(micro_count, -1)
    send_rows = slot_rows(id_rows, experts, per_device, sources, capacity)
    sent_grad, sent_weight = dispatch_buffers(
        grad_rows, weight_rows, send_rows, top_count, buffer_len
    )
    sent_grad = sent_grad.reshape(micro_count, per_device, sources, capacity, model_width)
    sent_weight = sent_weight.reshape(micro_count, per_device, sources, capacity)
    received_gradient, received_weight = (
        lax.all_to_all(sent_grad, "expert", split_axis=2, concat_axis=2, tiled=True),
        lax.all_to_all(sent_weight, "expert", split_axis=2, concat_axis=2, tiled=True),
    )
    received_gradient = received_gradient.reshape(micro_count, per_device, slot_count, model_width)
    received_weight = received_weight.reshape(micro_count, per_device, slot_count)
    hidden_grad, routing_rows, adapter_input_gradient, adapter_output_gradient = expert_rows_view(
        received_gradient,
        received_weight,
        hidden,
        frozen_down_weight,
        adapter_input_map,
        adapter_output_map,
    )
    router_home = lax.all_to_all(
        routing_rows.reshape(micro_count, per_device, sources, capacity),
        "expert",
        split_axis=2,
        concat_axis=2,
        tiled=True,
    )
    router_flat = router_home.reshape(micro_count, buffer_len)
    router_grad = jax.vmap(pick_rows)(router_flat, send_rows).reshape(-1, top_count)
    share_a, share_b = (
        lax.psum_scatter(adapter_input_gradient, "dp", scatter_dimension=2, tiled=True),
        lax.psum_scatter(adapter_output_gradient, "dp", scatter_dimension=2, tiled=True),
    )
    return (hidden_grad, router_grad, share_a, share_b)


def pad_rows(count):
    return -(-count // 16) * 16


def read_names(rows, span, top):
    wide = rows.astype(jnp.float32)
    per = wide.shape[1] // span
    lines = [
        wide[k // per : k // per + 1, (k % per) * span : (k % per + 1) * span]
        for k in range(2 * top)
    ]
    return lines[:top], lines[top:]


def slot_codes(names, owners_ref, first, capacity, experts, micro):
    shards = len(names)
    span = names[0][0][0].shape[1]
    block = span // micro
    number = lax.broadcasted_iota(jnp.int32, (experts, span), 0).astype(jnp.float32) + first
    from_row = lax.broadcasted_iota(jnp.int32, (span, span), 0)
    to_row = lax.broadcasted_iota(jnp.int32, (span, span), 1)
    earlier = jnp.where(
        (from_row // block == to_row // block) & (from_row < to_row), 1.0, 0.0
    ).astype(jnp.bfloat16)
    codes, gates = [], []
    for j in range(shards):
        named = jnp.zeros((experts, span), jnp.float32)
        gate = jnp.zeros((experts, span), jnp.float32)
        for name, weight in zip(*names[j]):
            hit = name == number
            named = jnp.where(hit, 1.0, named)
            gate = jnp.where(hit, weight, gate)
        before = jnp.dot(named.astype(jnp.bfloat16), earlier, preferred_element_type=jnp.float32)
        offset = (owners_ref[j] * capacity).astype(jnp.float32)
        codes.append(jnp.where(named > 0.0, before + offset, -1.0))
        gates.append(gate)
    parts = [slice(m * block, (m + 1) * block) for m in range(micro)]
    return (
        [jnp.concatenate([c[:, part] for c in codes], axis=1) for part in parts],
        [jnp.concatenate([g[:, part] for g in gates], axis=1) for part in parts],
    )


contract_last = (((1,), (1,)), ((), ()))
contract_first = (((0,), (0,)), ((), ()))


def expert_kernel(capacity, group_count, shards, *refs):
    owners_ref = refs[0]
    token_refs = refs[1 : 1 + shards]
    hidden_ref, u_ref, weight_hbm, amap_ref, bmap_hbm = refs[1 + shards : 6 + shards]
    hg_ref, rk_ref, la_ref = refs[6 + shards : 9 + shards]
    dy_s, wb_s, rows_s, y_s, code_s, gate_s, back_s, dy_sem, w_sem, b_sem = refs[9 + shards :]
    top, span = rk_ref.shape[1:]
    micro, experts, slots, units = hidden_ref.shape
    rank = amap_ref.shape[1]
    width = dy_s.shape[2]
    block = span // micro
    padded = rows_s.shape[1] // micro
    first = (lax.axis_index("expert") * experts).astype(jnp.float32)

    token_copies = [
        pltpu.make_async_copy(token_refs[i], dy_s.at[i], dy_sem.at[i])
        for i in range(shards)
    ]
    for copy in token_copies:
        copy.start()

    def weight_copies(x):
        return (
            pltpu.make_async_copy(weight_hbm.at[x], wb_s.at[x, pl.ds(0, units)], w_sem.at[x]),
            pltpu.make_async_copy(bmap_hbm.at[x], wb_s.at[x, pl.ds(units, rank)], b_sem.at[x]),
        )

    for x in range(experts):
        for copy in weight_copies(x):
            copy.start()

    for copy in token_copies:
        copy.wait()
    names = [
        read_names(dy_s[i, span:, : width // group_count], span, top) for i in range(shards)
    ]
    codes, gates = slot_codes(names, owners_ref, first, capacity, experts, micro)
    slot_of = lax.broadcasted_iota(jnp.int32, (padded, shards * block), 0).astype(jnp.float32)
    picks = []
    for m in range(micro):
        code_s[m] = codes[m]
        chosen = []
        for x in range(experts):
            hit = codes[m][x : x + 1, :] == slot_of
            chosen.append(jnp.where(hit, 1.0, 0.0).astype(jnp.bfloat16))
            gate_s[x, m * padded : (m + 1) * padded, :] = jnp.sum(
                jnp.where(hit, gates[m][x : x + 1, :], 0.0), axis=1, keepdims=True
            )
        picks.append(jnp.concatenate(chosen, axis=0))

    tile = 512 if width % 512 == 0 else width
    for m in range(micro):
        for n in range(width // tile):
            cols = slice(n * tile, (n + 1) * tile)
            tokens = jnp.concatenate(
                [dy_s[i, m * block : (m + 1) * block, cols] for i in range(shards)], axis=0
            )
            rows = jnp.dot(picks[m], tokens, preferred_element_type=jnp.float32)
            rows_s[:, m * padded : (m + 1) * padded, cols] = rows.astype(jnp.bfloat16).reshape(
                experts, padded, tile
            )

    half = experts // 2

    def main_products(x, carry):
        for copy in weight_copies(2 * x) + weight_copies(2 * x + 1):
            copy.wait()
        for i in range(2):
            y_s[2 * x + i] = lax.dot_general(
                rows_s[2 * x + i],
                wb_s[2 * x + i],
                contract_last,
                preferred_element_type=jnp.float32,
            )
        return carry

    lax.fori_loop(0, half, main_products, 0)

    share = units // group_count
    filler = jnp.zeros((padded - slots, units), jnp.float32)
    batch = 2 if half % 2 == 0 else 1

    def small_steps(step, carry):
        at = [step * batch + i for i in range(batch)]
        picked = [(p, p, slice(0, rank)) for p in at]
        picked += [(p + half, p, slice(rank, 2 * rank)) for p in at]
        xs = [x for x, _, _ in picked]
        mains = [y_s[x, :, :units] for x in xs]
        vs = [y_s[x, :, units:].astype(jnp.bfloat16) for x in xs]
        lows = [
            jnp.dot(v, amap_ref[x], preferred_element_type=jnp.float32) for v, x in zip(vs, xs)
        ]
        gates_x = [gate_s[x] for x in xs]
        wide = [
            jnp.concatenate(
                [
                    part
                    for m in range(micro)
                    for part in (hidden_ref[m, x].astype(jnp.float32), filler)
                ],
                axis=0,
            )
            for x in xs
        ]
        v_wide = [v.astype(jnp.float32) for v in vs]
        ws = [(gate * v).astype(jnp.bfloat16) for gate, v in zip(gates_x, v_wide)]
        las = [
            lax.dot_general(
                w, held.astype(jnp.bfloat16), contract_first, preferred_element_type=jnp.float32
            )
            for w, held in zip(ws, wide)
        ]
        routed = [
            jnp.sum(main * held, axis=1, keepdims=True)
            + adapter_scale
            * jnp.sum(u_ref[p, :, lanes].astype(jnp.float32) * v, axis=1, keepdims=True)
            for main, held, v, (_, p, lanes) in zip(mains, wide, v_wide, picked)
        ]
        grads = [
            (gate * (main + adapter_scale * low)).astype(jnp.bfloat16)
            for gate, main, low in zip(gates_x, mains, lows)
        ]
        for x, grad, la, back in zip(xs, grads, las, routed):
            for m in range(micro):
                hg_ref[m, x] = grad[m * padded : m * padded + slots]
                hit = code_s[m, pl.ds(x, 1), :] == slot_of
                back_s[m, pl.ds(x, 1), :] = jnp.sum(
                    jnp.where(hit, back[m * padded : (m + 1) * padded], 0.0),
                    axis=0,
                    keepdims=True,
                )
            for k in range(group_count):
                la_ref[k, x] = (adapter_scale * la[:, k * share : (k + 1) * share]).astype(
                    la_ref.dtype
                )
        return carry

    lax.fori_loop(0, half // batch, small_steps, 0)

    number = lax.broadcasted_iota(jnp.int32, (experts, span), 0).astype(jnp.float32) + first
    for i in range(shards):
        back = jnp.concatenate(
            [back_s[m, :, i * block : (i + 1) * block] for m in range(micro)], axis=1
        )
        found = [
            jnp.sum(
                jnp.where(name == number, back, 0.0), axis=0, keepdims=True
            )
            for name in names[i][0]
        ]
        rk_ref[owners_ref[i]] = jnp.concatenate(found, axis=0)


def adapter_kernel(capacity, micro, span, top, group_count, shards, *refs):
    pairs = shards // 2
    early = pairs // 2
    owners_ref, early_ref, late_ref, swapped_ref = refs[:4]
    u_refs = refs[4 : 4 + group_count]
    lb_ref, tok_s, q_s, sem = refs[4 + group_count :]
    experts, rank, share = lb_ref.shape
    tall = u_refs[0].shape[1]
    padded = tall // micro
    block = span // micro
    first = (lax.axis_index("expert") * experts).astype(jnp.float32)
    group = lax.axis_index("dp")
    copies = []
    for g in range(group_count):
        home = lax.rem(group - g + group_count, group_count)
        for i in range(shards):
            far, k = i // pairs, i % pairs
            if k < early:
                source = early_ref.at[home, far * early + k]
            else:
                source = (swapped_ref if far else late_ref).at[home, k - early]
            copies.append(pltpu.make_async_copy(source, tok_s.at[g, i], sem.at[g, i]))
    for copy in copies:
        copy.start()
    slot_of = lax.broadcasted_iota(jnp.int32, (padded, shards * block), 0).astype(jnp.float32)
    for g in range(group_count):
        for i in range(shards):
            copies[g * shards + i].wait()
        names = [read_names(tok_s[g, i, span:, :], span, top) for i in range(shards)]
        codes, gates = slot_codes(names, owners_ref, first, capacity, experts, micro)
        for m in range(micro):
            picks = jnp.concatenate(
                [
                    jnp.where(
                        codes[m][x : x + 1, :] == slot_of, gates[m][x : x + 1, :], 0.0
                    ).astype(jnp.bfloat16)
                    for x in range(experts)
                ],
                axis=0,
            )
            tokens = jnp.concatenate(
                [tok_s[g, i, m * block : (m + 1) * block, :] for i in range(shards)], axis=0
            )
            q = jnp.dot(picks, tokens, preferred_element_type=jnp.float32).astype(jnp.bfloat16)
            at = g * tall + m * padded
            q_s[:, at : at + padded, :] = q.reshape(experts, padded, share)
    half = experts // 2
    for x in range(half):
        both = jnp.concatenate([u_refs[g][x] for g in range(group_count)], axis=0)
        lb_ref[x] = adapter_scale * lax.dot_general(
            both[:, :rank], q_s[x], contract_first, preferred_element_type=jnp.float32
        )
        lb_ref[x + half] = adapter_scale * lax.dot_general(
            both[:, rank:], q_s[x + half], contract_first, preferred_element_type=jnp.float32
        )


def ring_order(count):
    return list(range(0, count, 2)) + list(range(1, count, 2))[::-1]


def local_by_tokens(
    output_gradient,
    chosen_expert_index,
    routing_gate_weight,
    hidden,
    frozen_down_weight,
    adapter_input_map,
    adapter_output_map,
):
    sources = lax.axis_size("expert")
    group_count = lax.axis_size("dp")
    micro, experts, slots, units = hidden.shape
    span, top = chosen_expert_index.shape
    width = output_gradient.shape[1]
    rank = adapter_input_map.shape[2]
    capacity = slots // sources
    block = span // micro
    padded = pad_rows(slots)
    share = width // group_count
    pairs = sources // 2
    me = lax.axis_index("expert")
    group = lax.axis_index("dp")

    order = ring_order(pairs)
    place = {z: i for i, z in enumerate(order)}
    ring = [
        (2 * z + c, 2 * order[(place[z] + 1) % pairs] + c) for z in range(pairs) for c in range(2)
    ]
    swap = [(e, e ^ 1) for e in range(sources)]
    owner_table = [
        [
            2 * order[(place[e // 2] - i) % pairs] + (e % 2 if near else 1 - e % 2)
            for near in (True, False)
            for i in range(pairs)
        ]
        for e in range(sources)
    ]
    owners = jnp.asarray(owner_table, jnp.int32)[me]

    amap = jnp.swapaxes(adapter_input_map, 1, 2)
    u = jnp.einsum("mesk,exk->emsx", hidden, amap, preferred_element_type=jnp.float32)
    u = u.astype(jnp.bfloat16)
    u = jnp.pad(u, ((0, 0), (0, 0), (0, padded - slots), (0, 0))).reshape(
        2, experts // 2, micro * padded, rank
    )
    u = jnp.concatenate([u[0], u[1]], axis=-1)

    def shift_groups(array, by):
        return lax.ppermute(
            array, "dp", [(d, (d + by) % group_count) for d in range(group_count)]
        )

    def swap_partners(array):
        return lax.ppermute(array, "expert", swap)

    def exchange_columns(chosen):
        parts = [
            jnp.stack([piece[:, g * share : (g + 1) * share] for piece in chosen])
            for g in range(group_count)
        ]
        return jnp.stack(parts)

    def across_groups(array):
        return lax.all_to_all(array, "dp", split_axis=0, concat_axis=0, tiled=True)

    others = range(1, group_count)
    u_all = [u] + [shift_groups(u, s) for s in others]

    names = jnp.concatenate(
        [chosen_expert_index.T.astype(jnp.bfloat16), routing_gate_weight.T], axis=0
    )
    lines = 2 * top * span // share
    names = jnp.tile(names.reshape(lines, share), (1, group_count))
    extra = -(-lines // 8) * 8
    sent = jnp.concatenate(
        [output_gradient, jnp.pad(names, ((0, extra - lines), (0, 0)))], axis=0
    )

    early = pairs // 2
    near, far = [sent], []
    for step in range(pairs - 1):
        near.append(lax.ppermute(near[-1], "expert", ring))
        far.append(swap_partners(near[step]))
    early_columns = exchange_columns(near[:early] + far[:early])
    early_columns, *u_all = lax.optimization_barrier((early_columns, *u_all))
    early_columns = across_groups(early_columns)
    late_columns = across_groups(exchange_columns(near[early:]))
    far.append(swap_partners(near[-1]))
    pieces = near + far

    vmem = pl.BlockSpec(memory_space=pltpu.VMEM)
    smem = pl.BlockSpec(memory_space=pltpu.SMEM)
    anywhere = pl.BlockSpec(memory_space=pl.ANY)
    hidden_grad, routed, part_a = pl.pallas_call(
        functools.partial(expert_kernel, capacity, group_count, sources),
        out_shape=(
            jax.ShapeDtypeStruct(hidden.shape, jnp.bfloat16),
            jax.ShapeDtypeStruct((sources, top, span), jnp.float32),
            jax.ShapeDtypeStruct(
                (group_count, experts, rank, units // group_count), jnp.bfloat16
            ),
        ),
        in_specs=[smem] + [anywhere] * sources + [vmem, vmem, anywhere, vmem, anywhere],
        out_specs=(vmem,) * 3,
        scratch_shapes=[
            pltpu.VMEM((sources, span + extra, width), jnp.bfloat16),
            pltpu.VMEM((experts, units + rank, width), jnp.bfloat16),
            pltpu.VMEM((experts, micro * padded, width), jnp.bfloat16),
            pltpu.VMEM((experts, micro * padded, units + rank), jnp.float32),
            pltpu.VMEM((micro, experts, sources * block), jnp.float32),
            pltpu.VMEM((experts, micro * padded, 1), jnp.float32),
            pltpu.VMEM((micro, experts, sources * block), jnp.float32),
            pltpu.SemaphoreType.DMA((sources,)),
            pltpu.SemaphoreType.DMA((experts,)),
            pltpu.SemaphoreType.DMA((experts,)),
        ],
        compiler_params=pltpu.CompilerParams(vmem_limit_bytes=58 * 1024 * 1024),
        cost_estimate=pl.CostEstimate(
            flops=2 * experts * micro * padded * width * (units + rank + sources * block),
            bytes_accessed=2 * experts * width * (units + rank) + 2 * sources * span * width,
            transcendentals=0,
        ),
        name="expert_rows",
    )(owners, *pieces, hidden, u, frozen_down_weight, amap, adapter_output_map)

    late_columns, part_a, routed = lax.optimization_barrier((late_columns, part_a, routed))
    swapped = swap_partners(late_columns)
    arrived = across_groups(part_a)
    home = lax.all_to_all(routed, "expert", split_axis=0, concat_axis=0, tiled=True)

    lora_b = pl.pallas_call(
        functools.partial(adapter_kernel, capacity, micro, span, top, group_count, sources),
        out_shape=jax.ShapeDtypeStruct((experts, rank, share), jnp.float32),
        in_specs=[smem] + [anywhere] * 3 + [vmem] * group_count,
        out_specs=vmem,
        scratch_shapes=[
            pltpu.VMEM((group_count, sources, span + extra, share), jnp.bfloat16),
            pltpu.VMEM((experts, group_count * micro * padded, share), jnp.bfloat16),
            pltpu.SemaphoreType.DMA((group_count, sources)),
        ],
        compiler_params=pltpu.CompilerParams(vmem_limit_bytes=58 * 1024 * 1024),
        cost_estimate=pl.CostEstimate(
            flops=2 * experts * micro * padded * share * group_count * (rank + sources * block),
            bytes_accessed=2 * group_count * sources * span * share + 4 * experts * rank * share,
            transcendentals=0,
        ),
        name="adapter_columns",
    )(owners, early_columns, late_columns, swapped, *u_all)

    home, arrived, lora_b = lax.optimization_barrier((home, arrived, lora_b))
    router_grad = jnp.sum(home, axis=0).T
    lora_a = jnp.sum(arrived.astype(jnp.float32), axis=0)
    return (hidden_grad, router_grad, lora_a, lora_b)


def local(*arrays):
    sources, groups = lax.axis_size("expert"), lax.axis_size("dp")
    span, width = arrays[0].shape
    top, (micro, experts, slots, units) = arrays[1].shape[1], arrays[3].shape
    even = sources % 4 == 0 and experts % 2 == 0 and width % (128 * groups) == 0 and units % groups == 0
    packs = 2 * top * span % (width // groups) == 0 and (width // groups) % span == 0
    exact = experts * sources <= 256
    if even and packs and exact and sources * span <= micro * experts * slots:
        return local_by_tokens(*arrays)
    return local_by_slots(*arrays)


def solution(mesh):
    in_specs = (
        P(("dp", "expert"), None),
        P(("dp", "expert"), None),
        P(("dp", "expert"), None),
        P(None, ("dp", "expert"), None, None),
        P("expert", None, None),
        P("expert", None, None),
        P("expert", None, None),
    )
    out_specs = (
        P(None, ("dp", "expert"), None, None),
        P(("dp", "expert"), None),
        P("expert", None, "dp"),
        P("expert", None, "dp"),
    )
    return jax.shard_map(local, mesh=mesh, in_specs=in_specs, out_specs=out_specs, check_vma=False)
```

```python
import functools

import jax
import jax.numpy as jnp
from jax import lax
from jax.experimental import pallas as pl
from jax.experimental.pallas import tpu as pltpu
from jax.sharding import PartitionSpec as P

adapter_scale = 2.0


def slot_rows(id_rows, experts, per_device, sources, capacity):
    onehot = (id_rows[:, :, None] == jnp.arange(experts, dtype=jnp.int32)[None, None, :]).astype(
        jnp.int32
    )
    before = jnp.sum(jnp.cumsum(onehot, axis=1) * onehot, axis=2) - 1
    target_dev = id_rows // per_device
    target_slot = id_rows % per_device
    return (target_slot * sources + target_dev) * capacity + before


def pick_rows(source, indices):
    return source[indices]


def dispatch_buffers(grad_rows, weight_rows, send_rows, top_count, buffer_len):
    entry_count = send_rows.shape[1]
    token_count = grad_rows.shape[1]
    filler = jnp.full((buffer_len,), entry_count, jnp.int32)

    def invert(rows):
        return filler.at[rows].set(jnp.arange(entry_count, dtype=jnp.int32))

    table = jax.vmap(invert)(send_rows)
    padded_grad = jnp.concatenate(
        [grad_rows, jnp.zeros((grad_rows.shape[0], 1, grad_rows.shape[2]), grad_rows.dtype)], axis=1
    )
    padded_weight = jnp.concatenate(
        [weight_rows, jnp.zeros((weight_rows.shape[0], 1), weight_rows.dtype)], axis=1
    )
    token_pick = jnp.where(table < entry_count, table // top_count, token_count)
    sent_grad = jax.vmap(pick_rows)(padded_grad, token_pick)
    sent_weight = jax.vmap(pick_rows)(padded_weight, table)
    return (sent_grad, sent_weight)


def expert_rows_view(
    received_gradient,
    received_weight,
    retained_rows,
    frozen_down_weight,
    adapter_input_map,
    adapter_output_map,
):
    frozen_term = jnp.einsum(
        "mesd,efd->mesf", received_gradient, frozen_down_weight, preferred_element_type=jnp.float32
    )
    across_product = jnp.einsum(
        "hati,aki->hatk", received_gradient, adapter_output_map, preferred_element_type=jnp.float32
    ).astype(jnp.bfloat16)
    low_rank_state = jnp.einsum(
        "ptqv,tgv->ptqg", across_product, adapter_input_map, preferred_element_type=jnp.float32
    )
    capacity_slot_weight = received_weight.astype(jnp.float32)[..., None]
    hidden_state_gradient = (
        capacity_slot_weight * (frozen_term + adapter_scale * low_rank_state)
    ).astype(jnp.bfloat16)
    down_mapping = jnp.einsum(
        "lkgu,kup->lkgp", retained_rows, adapter_input_map, preferred_element_type=jnp.float32
    ).astype(jnp.bfloat16)
    complete_term = jnp.sum(frozen_term * retained_rows.astype(jnp.float32), axis=-1)
    adapter_term = jnp.einsum(
        "mesr,mesr->mes", down_mapping, across_product, preferred_element_type=jnp.float32
    )
    routing_rows = complete_term + adapter_scale * adapter_term
    scaled_gradient = (capacity_slot_weight * received_gradient).astype(jnp.bfloat16)
    scaled_across_product = (capacity_slot_weight * across_product.astype(jnp.float32)).astype(
        jnp.bfloat16
    )
    adapter_output_gradient = adapter_scale * jnp.einsum(
        "mesr,mesd->erd", down_mapping, scaled_gradient, preferred_element_type=jnp.float32
    )
    adapter_input_gradient = adapter_scale * jnp.einsum(
        "mesr,mesf->erf", scaled_across_product, retained_rows, preferred_element_type=jnp.float32
    )
    return (hidden_state_gradient, routing_rows, adapter_input_gradient, adapter_output_gradient)


def local_by_slots(
    output_gradient,
    chosen_expert_index,
    routing_gate_weight,
    hidden,
    frozen_down_weight,
    adapter_input_map,
    adapter_output_map,
):
    sources = lax.axis_size("expert")
    per_device = frozen_down_weight.shape[0]
    experts = per_device * sources
    micro_count = hidden.shape[0]
    slot_count = hidden.shape[2]
    capacity = slot_count // sources
    top_count = chosen_expert_index.shape[1]
    model_width = output_gradient.shape[1]
    buffer_len = experts * capacity
    grad_rows = output_gradient.reshape(micro_count, -1, model_width)
    id_rows = chosen_expert_index.reshape(micro_count, -1)
    weight_rows = routing_gate_weight.reshape(micro_count, -1)
    send_rows = slot_rows(id_rows, experts, per_device, sources, capacity)
    sent_grad, sent_weight = dispatch_buffers(
        grad_rows, weight_rows, send_rows, top_count, buffer_len
    )
    sent_grad = sent_grad.reshape(micro_count, per_device, sources, capacity, model_width)
    sent_weight = sent_weight.reshape(micro_count, per_device, sources, capacity)
    received_gradient, received_weight = (
        lax.all_to_all(sent_grad, "expert", split_axis=2, concat_axis=2, tiled=True),
        lax.all_to_all(sent_weight, "expert", split_axis=2, concat_axis=2, tiled=True),
    )
    received_gradient = received_gradient.reshape(micro_count, per_device, slot_count, model_width)
    received_weight = received_weight.reshape(micro_count, per_device, slot_count)
    hidden_grad, routing_rows, adapter_input_gradient, adapter_output_gradient = expert_rows_view(
        received_gradient,
        received_weight,
        hidden,
        frozen_down_weight,
        adapter_input_map,
        adapter_output_map,
    )
    router_home = lax.all_to_all(
        routing_rows.reshape(micro_count, per_device, sources, capacity),
        "expert",
        split_axis=2,
        concat_axis=2,
        tiled=True,
    )
    router_flat = router_home.reshape(micro_count, buffer_len)
    router_grad = jax.vmap(pick_rows)(router_flat, send_rows).reshape(-1, top_count)
    share_a, share_b = (
        lax.psum_scatter(adapter_input_gradient, "dp", scatter_dimension=2, tiled=True),
        lax.psum_scatter(adapter_output_gradient, "dp", scatter_dimension=2, tiled=True),
    )
    return (hidden_grad, router_grad, share_a, share_b)


def pad_rows(count):
    return -(-count // 16) * 16


def read_names(rows, span, top):
    wide = rows.astype(jnp.float32)
    per = wide.shape[1] // span
    lines = [
        wide[k // per : k // per + 1, (k % per) * span : (k % per + 1) * span]
        for k in range(2 * top)
    ]
    return lines[:top], lines[top:]


def slot_codes(names, first, capacity, experts, micro):
    sources = len(names)
    span = names[0][0][0].shape[1]
    block = span // micro
    number = lax.broadcasted_iota(jnp.int32, (experts, span), 0).astype(jnp.float32) + first
    from_row = lax.broadcasted_iota(jnp.int32, (span, span), 0)
    to_row = lax.broadcasted_iota(jnp.int32, (span, span), 1)
    earlier = jnp.where(
        (from_row // block == to_row // block) & (from_row < to_row), 1.0, 0.0
    ).astype(jnp.bfloat16)
    codes, gates = [], []
    for j in range(sources):
        named = jnp.zeros((experts, span), jnp.float32)
        gate = jnp.zeros((experts, span), jnp.float32)
        for name, weight in zip(*names[j]):
            hit = name == number
            named = jnp.where(hit, 1.0, named)
            gate = jnp.where(hit, weight, gate)
        before = jnp.dot(named.astype(jnp.bfloat16), earlier, preferred_element_type=jnp.float32)
        codes.append(jnp.where(named > 0.0, before + float(j * capacity), -1.0))
        gates.append(gate)

    def arrange(values):
        half = sources // 2
        return [
            [
                jnp.concatenate(
                    [c[:, m * block : (m + 1) * block] for c in values[h * half : (h + 1) * half]],
                    axis=1,
                )
                for h in range(2)
            ]
            for m in range(micro)
        ]

    return arrange(codes), arrange(gates)


def slot_windows(slots):
    half = slots // 2
    return [(h * half // 8 * 8, -(-(h + 1) * half // 8) * 8) for h in range(2)]


def slot_iota(window, lanes):
    shape = (window[1] - window[0], lanes)
    return lax.broadcasted_iota(jnp.int32, shape, 0).astype(jnp.float32) + float(window[0])


def join_windows(first_part, second_part, windows, padded, axis):
    (_, end), (start, last) = windows

    def rows(values, low, high):
        return lax.slice_in_dim(values, low, high, axis=axis)

    parts = [rows(first_part, 0, start)]
    if end > start:
        parts.append(rows(first_part, start, end) + rows(second_part, 0, end - start))
    parts.append(rows(second_part, end - start, last - start))
    if padded > last:
        shape = list(first_part.shape)
        shape[axis] = padded - last
        parts.append(jnp.zeros(shape, first_part.dtype))
    return jnp.concatenate(parts, axis=axis)


contract_last = (((1,), (1,)), ((), ()))
contract_first = (((0,), (0,)), ((), ()))


def expert_kernel(capacity, group_count, shards, *refs):
    owners_ref = refs[0]
    token_refs = refs[1 : 1 + shards]
    hidden_ref, u_ref, weight_hbm, amap_ref, bmap_hbm = refs[1 + shards : 6 + shards]
    hg_ref, rk_ref = refs[6 + shards : 8 + shards]
    la_outs = refs[8 + shards : 8 + shards + group_count]
    scratch = refs[8 + shards + group_count :]
    dy_s, wb_s, rows_s, y_s, code_s, gate_s, back_s, la_s = scratch[:8]
    dy_sem, w_sem, b_sem, la_sem = scratch[8:]
    top, span = rk_ref.shape[1:]
    micro, experts, slots, units = hidden_ref.shape
    rank = amap_ref.shape[1]
    width = dy_s.shape[2]
    block = span // micro
    padded = rows_s.shape[1] // micro
    first = (lax.axis_index("expert") * experts).astype(jnp.float32)

    token_copies = [
        pltpu.make_async_copy(token_refs[i], dy_s.at[owners_ref[i]], dy_sem.at[i])
        for i in range(shards)
    ]
    for copy in token_copies:
        copy.start()

    def weight_copies(x):
        return (
            pltpu.make_async_copy(weight_hbm.at[x], wb_s.at[x, pl.ds(0, units)], w_sem.at[x]),
            pltpu.make_async_copy(bmap_hbm.at[x], wb_s.at[x, pl.ds(units, rank)], b_sem.at[x]),
        )

    for x in range(experts):
        for copy in weight_copies(x):
            copy.start()

    for copy in token_copies:
        copy.wait()
    names = [
        read_names(dy_s[i, span:, : width // group_count], span, top) for i in range(shards)
    ]
    codes, gates = slot_codes(names, first, capacity, experts, micro)
    windows = slot_windows(slots)
    lanes_of = shards // 2 * block
    slot_of = [slot_iota(window, lanes_of) for window in windows]
    picks = []
    for m in range(micro):
        chosen = [[], []]
        for h in range(2):
            code_s[m, h] = codes[m][h]
        for x in range(experts):
            sums = []
            for h in range(2):
                hit = codes[m][h][x : x + 1, :] == slot_of[h]
                chosen[h].append(jnp.where(hit, 1.0, 0.0))
                sums.append(
                    jnp.sum(
                        jnp.where(hit, gates[m][h][x : x + 1, :], 0.0), axis=1, keepdims=True
                    )
                )
            gate_s[x, m * padded : (m + 1) * padded, :] = join_windows(
                sums[0], sums[1], windows, padded, 0
            )
        picks.append([jnp.concatenate(c, axis=0).astype(jnp.bfloat16) for c in chosen])

    tile = 512 if width % 512 == 0 else width
    for m in range(micro):
        for n in range(width // tile):
            cols = slice(n * tile, (n + 1) * tile)
            parts = []
            for h in range(2):
                tokens = jnp.concatenate(
                    [
                        dy_s[j, m * block : (m + 1) * block, cols]
                        for j in range(h * shards // 2, (h + 1) * shards // 2)
                    ],
                    axis=0,
                )
                rows = jnp.dot(picks[m][h], tokens, preferred_element_type=jnp.float32)
                parts.append(rows.reshape(experts, -1, tile))
            rows_s[:, m * padded : (m + 1) * padded, cols] = join_windows(
                parts[0], parts[1], windows, padded, 1
            ).astype(jnp.bfloat16)

    half = experts // 2

    def main_products(x, carry):
        for copy in weight_copies(2 * x) + weight_copies(2 * x + 1):
            copy.wait()
        for i in range(2):
            y_s[2 * x + i] = lax.dot_general(
                rows_s[2 * x + i],
                wb_s[2 * x + i],
                contract_last,
                preferred_element_type=jnp.float32,
            )
        return carry

    lax.fori_loop(0, half, main_products, 0)

    share = units // group_count
    filler = jnp.zeros((padded - slots, units), jnp.float32)
    batch = 2 if half % 2 == 0 else 1

    def small_steps(step, carry):
        at = [step * batch + i for i in range(batch)]
        picked = [(p, p, slice(0, rank)) for p in at]
        picked += [(p + half, p, slice(rank, 2 * rank)) for p in at]
        xs = [x for x, _, _ in picked]
        mains = [y_s[x, :, :units] for x in xs]
        vs = [y_s[x, :, units:].astype(jnp.bfloat16) for x in xs]
        lows = [
            jnp.dot(v, amap_ref[x], preferred_element_type=jnp.float32) for v, x in zip(vs, xs)
        ]
        gates_x = [gate_s[x] for x in xs]
        wide = [
            jnp.concatenate(
                [
                    part
                    for m in range(micro)
                    for part in (hidden_ref[m, x].astype(jnp.float32), filler)
                ],
                axis=0,
            )
            for x in xs
        ]
        v_wide = [v.astype(jnp.float32) for v in vs]
        ws = [(gate * v).astype(jnp.bfloat16) for gate, v in zip(gates_x, v_wide)]
        las = [
            lax.dot_general(
                w, held.astype(jnp.bfloat16), contract_first, preferred_element_type=jnp.float32
            )
            for w, held in zip(ws, wide)
        ]
        routed = [
            jnp.sum(main * held, axis=1, keepdims=True)
            + adapter_scale
            * jnp.sum(u_ref[p, :, lanes].astype(jnp.float32) * v, axis=1, keepdims=True)
            for main, held, v, (_, p, lanes) in zip(mains, wide, v_wide, picked)
        ]
        grads = [
            (gate * (main + adapter_scale * low)).astype(jnp.bfloat16)
            for gate, main, low in zip(gates_x, mains, lows)
        ]
        for x, grad, la, back in zip(xs, grads, las, routed):
            for m in range(micro):
                hg_ref[m, x] = grad[m * padded : m * padded + slots]
                for h, (low, high) in enumerate(windows):
                    hit = code_s[m, h, pl.ds(x, 1), :] == slot_of[h]
                    rows = back[m * padded + low : m * padded + high]
                    back_s[m, h, pl.ds(x, 1), :] = jnp.sum(
                        jnp.where(hit, rows, 0.0), axis=0, keepdims=True
                    )
            for k in range(group_count):
                la_s[k, x] = (adapter_scale * la[:, k * share : (k + 1) * share]).astype(
                    la_s.dtype
                )
        return carry

    lax.fori_loop(0, half // batch, small_steps, 0)

    group = lax.axis_index("dp")
    la_copies = [
        pltpu.make_async_copy(
            la_s.at[lax.rem(group + s, group_count)], la_outs[s], la_sem.at[s]
        )
        for s in range(group_count)
    ]
    for copy in la_copies:
        copy.start()
    number = lax.broadcasted_iota(jnp.int32, (experts, span), 0).astype(jnp.float32) + first
    for j in range(shards):
        h, k = j // (shards // 2), j % (shards // 2)
        back = jnp.concatenate(
            [back_s[m, h, :, k * block : (k + 1) * block] for m in range(micro)], axis=1
        )
        found = [
            jnp.sum(jnp.where(name == number, back, 0.0), axis=0, keepdims=True)
            for name in names[j][0]
        ]
        rk_ref[j] = jnp.concatenate(found, axis=0)
    for copy in la_copies:
        copy.wait()


def adapter_kernel(capacity, micro, span, top, group_count, shards, *refs):
    pairs = shards // 2
    early = pairs // 2
    owners_ref = refs[0]
    early_refs = refs[1 : 1 + early]
    late_ref, swapped_ref = refs[1 + early : 3 + early]
    u_refs = refs[3 + early : 3 + early + group_count]
    lb_ref, tok_s, q_s, sem = refs[3 + early + group_count :]
    experts, rank, share = lb_ref.shape
    tall = u_refs[0].shape[1]
    padded = tall // micro
    block = span // micro
    first = (lax.axis_index("expert") * experts).astype(jnp.float32)
    group = lax.axis_index("dp")
    copies = []
    for g in range(group_count):
        home = lax.rem(group - g + group_count, group_count)
        for i in range(shards):
            far, k = i // pairs, i % pairs
            if k < early:
                source = early_refs[k].at[home, far]
            else:
                source = (swapped_ref if far else late_ref).at[home, k - early]
            copies.append(pltpu.make_async_copy(source, tok_s.at[g, owners_ref[i]], sem.at[g, i]))
    for copy in copies:
        copy.start()
    slots = capacity * shards
    windows = slot_windows(slots)
    slot_of = [slot_iota(window, shards // 2 * block) for window in windows]
    for g in range(group_count):
        for i in range(shards):
            copies[g * shards + i].wait()
        names = [read_names(tok_s[g, i, span:, :], span, top) for i in range(shards)]
        codes, gates = slot_codes(names, first, capacity, experts, micro)
        for m in range(micro):
            parts = []
            for h in range(2):
                picks = jnp.concatenate(
                    [
                        jnp.where(
                            codes[m][h][x : x + 1, :] == slot_of[h],
                            gates[m][h][x : x + 1, :],
                            0.0,
                        )
                        for x in range(experts)
                    ],
                    axis=0,
                ).astype(jnp.bfloat16)
                tokens = jnp.concatenate(
                    [
                        tok_s[g, j, m * block : (m + 1) * block, :]
                        for j in range(h * shards // 2, (h + 1) * shards // 2)
                    ],
                    axis=0,
                )
                rows = jnp.dot(picks, tokens, preferred_element_type=jnp.float32)
                parts.append(rows.reshape(experts, -1, share))
            q = join_windows(parts[0], parts[1], windows, padded, 1).astype(jnp.bfloat16)
            at = g * tall + m * padded
            q_s[:, at : at + padded, :] = q
    half = experts // 2
    for x in range(half):
        both = jnp.concatenate([u_refs[g][x] for g in range(group_count)], axis=0)
        lb_ref[x] = adapter_scale * lax.dot_general(
            both[:, :rank], q_s[x], contract_first, preferred_element_type=jnp.float32
        )
        lb_ref[x + half] = adapter_scale * lax.dot_general(
            both[:, rank:], q_s[x + half], contract_first, preferred_element_type=jnp.float32
        )


def ring_order(count):
    return list(range(0, count, 2)) + list(range(1, count, 2))[::-1]


def local_by_tokens(
    output_gradient,
    chosen_expert_index,
    routing_gate_weight,
    hidden,
    frozen_down_weight,
    adapter_input_map,
    adapter_output_map,
):
    sources = lax.axis_size("expert")
    group_count = lax.axis_size("dp")
    micro, experts, slots, units = hidden.shape
    span, top = chosen_expert_index.shape
    width = output_gradient.shape[1]
    rank = adapter_input_map.shape[2]
    capacity = slots // sources
    block = span // micro
    padded = pad_rows(slots)
    share = width // group_count
    pairs = sources // 2
    me = lax.axis_index("expert")
    group = lax.axis_index("dp")

    order = ring_order(pairs)
    place = {z: i for i, z in enumerate(order)}
    ring = [
        (2 * z + c, 2 * order[(place[z] + 1) % pairs] + c) for z in range(pairs) for c in range(2)
    ]
    swap = [(e, e ^ 1) for e in range(sources)]
    owner_table = [
        [
            2 * order[(place[e // 2] - i) % pairs] + (e % 2 if near else 1 - e % 2)
            for near in (True, False)
            for i in range(pairs)
        ]
        for e in range(sources)
    ]
    owners = jnp.asarray(owner_table, jnp.int32)[me]

    amap = jnp.swapaxes(adapter_input_map, 1, 2)
    u = jnp.einsum("mesk,exk->emsx", hidden, amap, preferred_element_type=jnp.float32)
    u = u.astype(jnp.bfloat16)
    u = jnp.pad(u, ((0, 0), (0, 0), (0, padded - slots), (0, 0))).reshape(
        2, experts // 2, micro * padded, rank
    )
    u = jnp.concatenate([u[0], u[1]], axis=-1)

    def shift_groups(array, by):
        return lax.ppermute(
            array, "dp", [(d, (d + by) % group_count) for d in range(group_count)]
        )

    def swap_partners(array):
        return lax.ppermute(array, "expert", swap)

    def exchange_columns(chosen):
        parts = [
            jnp.stack([piece[:, g * share : (g + 1) * share] for piece in chosen])
            for g in range(group_count)
        ]
        return jnp.stack(parts)

    def across_groups(array):
        return lax.all_to_all(array, "dp", split_axis=0, concat_axis=0, tiled=True)

    others = range(1, group_count)
    names = jnp.concatenate(
        [chosen_expert_index.T.astype(jnp.bfloat16), routing_gate_weight.T], axis=0
    )
    lines = 2 * top * span // share
    names = jnp.tile(names.reshape(lines, share), (1, group_count))
    extra = -(-lines // 8) * 8
    sent = jnp.concatenate(
        [output_gradient, jnp.pad(names, ((0, extra - lines), (0, 0)))], axis=0
    )

    early = pairs // 2
    near, far = [sent], []
    for step in range(pairs - 1):
        near.append(lax.ppermute(near[-1], "expert", ring))
        far.append(swap_partners(near[step]))
    early_columns = []
    for k in range(early):
        columns = exchange_columns([near[k], far[k]])
        if early_columns:
            columns, early_columns[-1] = lax.optimization_barrier((columns, early_columns[-1]))
        early_columns.append(across_groups(columns))
    u, early_columns[-1] = lax.optimization_barrier((u, early_columns[-1]))
    u_all = [u] + [shift_groups(u, s) for s in others]
    late_columns = exchange_columns(near[early:])
    late_columns, u_all = lax.optimization_barrier((late_columns, u_all))
    late_columns = across_groups(late_columns)
    far.append(swap_partners(near[-1]))
    pieces = near + far

    vmem = pl.BlockSpec(memory_space=pltpu.VMEM)
    smem = pl.BlockSpec(memory_space=pltpu.SMEM)
    anywhere = pl.BlockSpec(memory_space=pl.ANY)
    part_a = jax.ShapeDtypeStruct((experts, rank, units // group_count), jnp.bfloat16)
    hidden_grad, routed, *parts = pl.pallas_call(
        functools.partial(expert_kernel, capacity, group_count, sources),
        out_shape=(
            jax.ShapeDtypeStruct(hidden.shape, jnp.bfloat16),
            jax.ShapeDtypeStruct((sources, top, span), jnp.float32),
        )
        + (part_a,) * group_count,
        in_specs=[smem] + [anywhere] * sources + [vmem, vmem, anywhere, vmem, anywhere],
        out_specs=(vmem,) * 2 + (anywhere,) * group_count,
        scratch_shapes=[
            pltpu.VMEM((sources, span + extra, width), jnp.bfloat16),
            pltpu.VMEM((experts, units + rank, width), jnp.bfloat16),
            pltpu.VMEM((experts, micro * padded, width), jnp.bfloat16),
            pltpu.VMEM((experts, micro * padded, units + rank), jnp.float32),
            pltpu.VMEM((micro, 2, experts, sources // 2 * block), jnp.float32),
            pltpu.VMEM((experts, micro * padded, 1), jnp.float32),
            pltpu.VMEM((micro, 2, experts, sources // 2 * block), jnp.float32),
            pltpu.VMEM((group_count, experts, rank, units // group_count), jnp.bfloat16),
            pltpu.SemaphoreType.DMA((sources,)),
            pltpu.SemaphoreType.DMA((experts,)),
            pltpu.SemaphoreType.DMA((experts,)),
            pltpu.SemaphoreType.DMA((group_count,)),
        ],
        compiler_params=pltpu.CompilerParams(vmem_limit_bytes=58 * 1024 * 1024),
        cost_estimate=pl.CostEstimate(
            flops=2 * experts * micro * padded * width * (units + rank + sources * block),
            bytes_accessed=2 * experts * width * (units + rank) + 2 * sources * span * width,
            transcendentals=0,
        ),
        name="expert_rows",
    )(owners, *pieces, hidden, u, frozen_down_weight, amap, adapter_output_map)

    late_columns, parts, routed = lax.optimization_barrier((late_columns, parts, routed))
    swapped = swap_partners(late_columns)
    arrived = [shift_groups(parts[s], s) for s in others]
    home = lax.all_to_all(routed, "expert", split_axis=0, concat_axis=0, tiled=True)

    lora_b = pl.pallas_call(
        functools.partial(adapter_kernel, capacity, micro, span, top, group_count, sources),
        out_shape=jax.ShapeDtypeStruct((experts, rank, share), jnp.float32),
        in_specs=[smem] + [anywhere] * (early + 2) + [vmem] * group_count,
        out_specs=vmem,
        scratch_shapes=[
            pltpu.VMEM((group_count, sources, span + extra, share), jnp.bfloat16),
            pltpu.VMEM((experts, group_count * micro * padded, share), jnp.bfloat16),
            pltpu.SemaphoreType.DMA((group_count, sources)),
        ],
        compiler_params=pltpu.CompilerParams(vmem_limit_bytes=58 * 1024 * 1024),
        cost_estimate=pl.CostEstimate(
            flops=2 * experts * micro * padded * share * group_count * (rank + sources * block),
            bytes_accessed=2 * group_count * sources * span * share + 4 * experts * rank * share,
            transcendentals=0,
        ),
        name="adapter_columns",
    )(owners, *early_columns, late_columns, swapped, *u_all)

    home, arrived, lora_b = lax.optimization_barrier((home, arrived, lora_b))
    router_grad = jnp.sum(home, axis=0).T
    lora_a = parts[0].astype(jnp.float32)
    for part in arrived:
        lora_a = lora_a + part.astype(jnp.float32)
    return (hidden_grad, router_grad, lora_a, lora_b)


def local(*arrays):
    sources, groups = lax.axis_size("expert"), lax.axis_size("dp")
    span, width = arrays[0].shape
    top, (micro, experts, slots, units) = arrays[1].shape[1], arrays[3].shape
    even = sources % 4 == 0 and experts % 2 == 0 and width % (128 * groups) == 0 and units % groups == 0
    packs = 2 * top * span % (width // groups) == 0 and (width // groups) % span == 0
    exact = experts * sources <= 256
    if even and packs and exact and sources * span <= micro * experts * slots:
        return local_by_tokens(*arrays)
    return local_by_slots(*arrays)


def solution(mesh):
    in_specs = (
        P(("dp", "expert"), None),
        P(("dp", "expert"), None),
        P(("dp", "expert"), None),
        P(None, ("dp", "expert"), None, None),
        P("expert", None, None),
        P("expert", None, None),
        P("expert", None, None),
    )
    out_specs = (
        P(None, ("dp", "expert"), None, None),
        P(("dp", "expert"), None),
        P("expert", None, "dp"),
        P("expert", None, "dp"),
    )
    return jax.shard_map(local, mesh=mesh, in_specs=in_specs, out_specs=out_specs, check_vma=False)
```

```python
import functools

import jax
import jax.numpy as jnp
from jax import lax
from jax.experimental import pallas as pl
from jax.experimental.pallas import tpu as pltpu
from jax.sharding import PartitionSpec as P

adapter_scale = 2.0


def slot_rows(id_rows, experts, per_device, sources, capacity):
    onehot = (id_rows[:, :, None] == jnp.arange(experts, dtype=jnp.int32)[None, None, :]).astype(
        jnp.int32
    )
    before = jnp.sum(jnp.cumsum(onehot, axis=1) * onehot, axis=2) - 1
    target_dev = id_rows // per_device
    target_slot = id_rows % per_device
    return (target_slot * sources + target_dev) * capacity + before


def pick_rows(source, indices):
    return source[indices]


def dispatch_buffers(grad_rows, weight_rows, send_rows, top_count, buffer_len):
    entry_count = send_rows.shape[1]
    token_count = grad_rows.shape[1]
    filler = jnp.full((buffer_len,), entry_count, jnp.int32)

    def invert(rows):
        return filler.at[rows].set(jnp.arange(entry_count, dtype=jnp.int32))

    table = jax.vmap(invert)(send_rows)
    padded_grad = jnp.concatenate(
        [grad_rows, jnp.zeros((grad_rows.shape[0], 1, grad_rows.shape[2]), grad_rows.dtype)], axis=1
    )
    padded_weight = jnp.concatenate(
        [weight_rows, jnp.zeros((weight_rows.shape[0], 1), weight_rows.dtype)], axis=1
    )
    token_pick = jnp.where(table < entry_count, table // top_count, token_count)
    sent_grad = jax.vmap(pick_rows)(padded_grad, token_pick)
    sent_weight = jax.vmap(pick_rows)(padded_weight, table)
    return (sent_grad, sent_weight)


def expert_rows_view(
    received_gradient,
    received_weight,
    retained_rows,
    frozen_down_weight,
    adapter_input_map,
    adapter_output_map,
):
    frozen_term = jnp.einsum(
        "mesd,efd->mesf", received_gradient, frozen_down_weight, preferred_element_type=jnp.float32
    )
    across_product = jnp.einsum(
        "hati,aki->hatk", received_gradient, adapter_output_map, preferred_element_type=jnp.float32
    ).astype(jnp.bfloat16)
    low_rank_state = jnp.einsum(
        "ptqv,tgv->ptqg", across_product, adapter_input_map, preferred_element_type=jnp.float32
    )
    capacity_slot_weight = received_weight.astype(jnp.float32)[..., None]
    hidden_state_gradient = (
        capacity_slot_weight * (frozen_term + adapter_scale * low_rank_state)
    ).astype(jnp.bfloat16)
    down_mapping = jnp.einsum(
        "lkgu,kup->lkgp", retained_rows, adapter_input_map, preferred_element_type=jnp.float32
    ).astype(jnp.bfloat16)
    complete_term = jnp.sum(frozen_term * retained_rows.astype(jnp.float32), axis=-1)
    adapter_term = jnp.einsum(
        "mesr,mesr->mes", down_mapping, across_product, preferred_element_type=jnp.float32
    )
    routing_rows = complete_term + adapter_scale * adapter_term
    scaled_gradient = (capacity_slot_weight * received_gradient).astype(jnp.bfloat16)
    scaled_across_product = (capacity_slot_weight * across_product.astype(jnp.float32)).astype(
        jnp.bfloat16
    )
    adapter_output_gradient = adapter_scale * jnp.einsum(
        "mesr,mesd->erd", down_mapping, scaled_gradient, preferred_element_type=jnp.float32
    )
    adapter_input_gradient = adapter_scale * jnp.einsum(
        "mesr,mesf->erf", scaled_across_product, retained_rows, preferred_element_type=jnp.float32
    )
    return (hidden_state_gradient, routing_rows, adapter_input_gradient, adapter_output_gradient)


def local_by_slots(
    output_gradient,
    chosen_expert_index,
    routing_gate_weight,
    hidden,
    frozen_down_weight,
    adapter_input_map,
    adapter_output_map,
):
    sources = lax.axis_size("expert")
    per_device = frozen_down_weight.shape[0]
    experts = per_device * sources
    micro_count = hidden.shape[0]
    slot_count = hidden.shape[2]
    capacity = slot_count // sources
    top_count = chosen_expert_index.shape[1]
    model_width = output_gradient.shape[1]
    buffer_len = experts * capacity
    grad_rows = output_gradient.reshape(micro_count, -1, model_width)
    id_rows = chosen_expert_index.reshape(micro_count, -1)
    weight_rows = routing_gate_weight.reshape(micro_count, -1)
    send_rows = slot_rows(id_rows, experts, per_device, sources, capacity)
    sent_grad, sent_weight = dispatch_buffers(
        grad_rows, weight_rows, send_rows, top_count, buffer_len
    )
    sent_grad = sent_grad.reshape(micro_count, per_device, sources, capacity, model_width)
    sent_weight = sent_weight.reshape(micro_count, per_device, sources, capacity)
    received_gradient, received_weight = (
        lax.all_to_all(sent_grad, "expert", split_axis=2, concat_axis=2, tiled=True),
        lax.all_to_all(sent_weight, "expert", split_axis=2, concat_axis=2, tiled=True),
    )
    received_gradient = received_gradient.reshape(micro_count, per_device, slot_count, model_width)
    received_weight = received_weight.reshape(micro_count, per_device, slot_count)
    hidden_grad, routing_rows, adapter_input_gradient, adapter_output_gradient = expert_rows_view(
        received_gradient,
        received_weight,
        hidden,
        frozen_down_weight,
        adapter_input_map,
        adapter_output_map,
    )
    router_home = lax.all_to_all(
        routing_rows.reshape(micro_count, per_device, sources, capacity),
        "expert",
        split_axis=2,
        concat_axis=2,
        tiled=True,
    )
    router_flat = router_home.reshape(micro_count, buffer_len)
    router_grad = jax.vmap(pick_rows)(router_flat, send_rows).reshape(-1, top_count)
    share_a, share_b = (
        lax.psum_scatter(adapter_input_gradient, "dp", scatter_dimension=2, tiled=True),
        lax.psum_scatter(adapter_output_gradient, "dp", scatter_dimension=2, tiled=True),
    )
    return (hidden_grad, router_grad, share_a, share_b)


def pad_rows(count):
    return -(-count // 16) * 16


def read_names(rows, span, top):
    wide = rows.astype(jnp.float32)
    per = wide.shape[1] // span
    lines = [
        wide[k // per : k // per + 1, (k % per) * span : (k % per + 1) * span]
        for k in range(2 * top)
    ]
    return lines[:top], lines[top:]


def slot_codes(names, first, capacity, experts, micro):
    sources = len(names)
    span = names[0][0][0].shape[1]
    block = span // micro
    number = lax.broadcasted_iota(jnp.int32, (experts, span), 0).astype(jnp.float32) + first
    from_row = lax.broadcasted_iota(jnp.int32, (span, span), 0)
    to_row = lax.broadcasted_iota(jnp.int32, (span, span), 1)
    earlier = jnp.where(
        (from_row // block == to_row // block) & (from_row < to_row), 1.0, 0.0
    ).astype(jnp.bfloat16)
    codes, gates = [], []
    for j in range(sources):
        named = jnp.zeros((experts, span), jnp.float32)
        gate = jnp.zeros((experts, span), jnp.float32)
        for name, weight in zip(*names[j]):
            hit = name == number
            named = jnp.where(hit, 1.0, named)
            gate = jnp.where(hit, weight, gate)
        before = jnp.dot(named.astype(jnp.bfloat16), earlier, preferred_element_type=jnp.float32)
        codes.append(jnp.where(named > 0.0, before + float(j * capacity), -1.0))
        gates.append(gate)

    def arrange(values):
        half = sources // 2
        return [
            [
                jnp.concatenate(
                    [c[:, m * block : (m + 1) * block] for c in values[h * half : (h + 1) * half]],
                    axis=1,
                )
                for h in range(2)
            ]
            for m in range(micro)
        ]

    return arrange(codes), arrange(gates)


def slot_windows(slots):
    half = slots // 2
    return [(h * half // 8 * 8, -(-(h + 1) * half // 8) * 8) for h in range(2)]


def slot_iota(window, lanes):
    shape = (window[1] - window[0], lanes)
    return lax.broadcasted_iota(jnp.int32, shape, 0).astype(jnp.float32) + float(window[0])


def join_windows(first_part, second_part, windows, padded, axis):
    (_, end), (start, last) = windows

    def rows(values, low, high):
        return lax.slice_in_dim(values, low, high, axis=axis)

    parts = [rows(first_part, 0, start)]
    if end > start:
        parts.append(rows(first_part, start, end) + rows(second_part, 0, end - start))
    parts.append(rows(second_part, end - start, last - start))
    if padded > last:
        shape = list(first_part.shape)
        shape[axis] = padded - last
        parts.append(jnp.zeros(shape, first_part.dtype))
    return jnp.concatenate(parts, axis=axis)


contract_last = (((1,), (1,)), ((), ()))
contract_first = (((0,), (0,)), ((), ()))


def expert_kernel(capacity, group_count, shards, chunks, *refs):
    owners_ref = refs[0]
    token_refs = refs[1 : 1 + shards * chunks]
    refs = refs[shards * (chunks - 1) :]
    hidden_ref, u_ref, weight_hbm, amap_ref, bmap_hbm = refs[1 + shards : 6 + shards]
    hg_ref, rk_ref = refs[6 + shards : 8 + shards]
    la_outs = refs[8 + shards : 8 + shards + group_count]
    scratch = refs[8 + shards + group_count :]
    dy_s, wb_s, rows_s, y_s, code_s, gate_s, back_s, la_s = scratch[:8]
    dy_sem, w_sem, b_sem, la_sem = scratch[8:]
    top, span = rk_ref.shape[1:]
    micro, experts, slots, units = hidden_ref.shape
    rank = amap_ref.shape[1]
    width = dy_s.shape[2]
    block = span // micro
    padded = rows_s.shape[1] // micro
    first = (lax.axis_index("expert") * experts).astype(jnp.float32)

    part = width // chunks
    token_copies = [
        pltpu.make_async_copy(
            token_refs[i * chunks + c],
            dy_s.at[owners_ref[i], :, pl.ds(c * part, part)],
            dy_sem.at[i, c],
        )
        for i in range(shards)
        for c in range(chunks)
    ]
    for copy in token_copies:
        copy.start()

    def weight_copies(x):
        return (
            pltpu.make_async_copy(weight_hbm.at[x], wb_s.at[x, pl.ds(0, units)], w_sem.at[x]),
            pltpu.make_async_copy(bmap_hbm.at[x], wb_s.at[x, pl.ds(units, rank)], b_sem.at[x]),
        )

    for x in range(experts):
        for copy in weight_copies(x):
            copy.start()

    for copy in token_copies:
        copy.wait()
    names = [
        read_names(dy_s[i, span:, : width // group_count], span, top) for i in range(shards)
    ]
    codes, gates = slot_codes(names, first, capacity, experts, micro)
    windows = slot_windows(slots)
    lanes_of = shards // 2 * block
    slot_of = [slot_iota(window, lanes_of) for window in windows]
    picks = []
    for m in range(micro):
        chosen = [[], []]
        for h in range(2):
            code_s[m, h] = codes[m][h]
        for x in range(experts):
            sums = []
            for h in range(2):
                hit = codes[m][h][x : x + 1, :] == slot_of[h]
                chosen[h].append(jnp.where(hit, 1.0, 0.0))
                sums.append(
                    jnp.sum(
                        jnp.where(hit, gates[m][h][x : x + 1, :], 0.0), axis=1, keepdims=True
                    )
                )
            gate_s[x, m * padded : (m + 1) * padded, :] = join_windows(
                sums[0], sums[1], windows, padded, 0
            )
        picks.append([jnp.concatenate(c, axis=0).astype(jnp.bfloat16) for c in chosen])

    tile = 512 if width % 512 == 0 else width
    for m in range(micro):
        for n in range(width // tile):
            cols = slice(n * tile, (n + 1) * tile)
            parts = []
            for h in range(2):
                tokens = jnp.concatenate(
                    [
                        dy_s[j, m * block : (m + 1) * block, cols]
                        for j in range(h * shards // 2, (h + 1) * shards // 2)
                    ],
                    axis=0,
                )
                rows = jnp.dot(picks[m][h], tokens, preferred_element_type=jnp.float32)
                parts.append(rows.reshape(experts, -1, tile))
            rows_s[:, m * padded : (m + 1) * padded, cols] = join_windows(
                parts[0], parts[1], windows, padded, 1
            ).astype(jnp.bfloat16)

    half = experts // 2

    def main_products(x, carry):
        for copy in weight_copies(2 * x) + weight_copies(2 * x + 1):
            copy.wait()
        for i in range(2):
            y_s[2 * x + i] = lax.dot_general(
                rows_s[2 * x + i],
                wb_s[2 * x + i],
                contract_last,
                preferred_element_type=jnp.float32,
            )
        return carry

    lax.fori_loop(0, half, main_products, 0)

    share = units // group_count
    filler = jnp.zeros((padded - slots, units), jnp.float32)
    batch = 2 if half % 2 == 0 else 1

    def small_steps(step, carry):
        at = [step * batch + i for i in range(batch)]
        picked = [(p, p, slice(0, rank)) for p in at]
        picked += [(p + half, p, slice(rank, 2 * rank)) for p in at]
        xs = [x for x, _, _ in picked]
        mains = [y_s[x, :, :units] for x in xs]
        vs = [y_s[x, :, units:].astype(jnp.bfloat16) for x in xs]
        lows = [
            jnp.dot(v, amap_ref[x], preferred_element_type=jnp.float32) for v, x in zip(vs, xs)
        ]
        gates_x = [gate_s[x] for x in xs]
        wide = [
            jnp.concatenate(
                [
                    part
                    for m in range(micro)
                    for part in (hidden_ref[m, x].astype(jnp.float32), filler)
                ],
                axis=0,
            )
            for x in xs
        ]
        v_wide = [v.astype(jnp.float32) for v in vs]
        ws = [(gate * v).astype(jnp.bfloat16) for gate, v in zip(gates_x, v_wide)]
        las = [
            lax.dot_general(
                w, held.astype(jnp.bfloat16), contract_first, preferred_element_type=jnp.float32
            )
            for w, held in zip(ws, wide)
        ]
        routed = [
            jnp.sum(main * held, axis=1, keepdims=True)
            + adapter_scale
            * jnp.sum(u_ref[p, :, lanes].astype(jnp.float32) * v, axis=1, keepdims=True)
            for main, held, v, (_, p, lanes) in zip(mains, wide, v_wide, picked)
        ]
        grads = [
            (gate * (main + adapter_scale * low)).astype(jnp.bfloat16)
            for gate, main, low in zip(gates_x, mains, lows)
        ]
        for x, grad, la, back in zip(xs, grads, las, routed):
            for m in range(micro):
                hg_ref[m, x] = grad[m * padded : m * padded + slots]
                for h, (low, high) in enumerate(windows):
                    hit = code_s[m, h, pl.ds(x, 1), :] == slot_of[h]
                    rows = back[m * padded + low : m * padded + high]
                    back_s[m, h, pl.ds(x, 1), :] = jnp.sum(
                        jnp.where(hit, rows, 0.0), axis=0, keepdims=True
                    )
            for k in range(group_count):
                la_s[k, x] = (adapter_scale * la[:, k * share : (k + 1) * share]).astype(
                    la_s.dtype
                )
        return carry

    lax.fori_loop(0, half // batch, small_steps, 0)

    group = lax.axis_index("dp")
    la_copies = [
        pltpu.make_async_copy(
            la_s.at[lax.rem(group + s, group_count)], la_outs[s], la_sem.at[s]
        )
        for s in range(group_count)
    ]
    for copy in la_copies:
        copy.start()
    number = lax.broadcasted_iota(jnp.int32, (experts, span), 0).astype(jnp.float32) + first
    for j in range(shards):
        h, k = j // (shards // 2), j % (shards // 2)
        back = jnp.concatenate(
            [back_s[m, h, :, k * block : (k + 1) * block] for m in range(micro)], axis=1
        )
        found = [
            jnp.sum(jnp.where(name == number, back, 0.0), axis=0, keepdims=True)
            for name in names[j][0]
        ]
        rk_ref[j] = jnp.concatenate(found, axis=0)
    for copy in la_copies:
        copy.wait()


def adapter_kernel(capacity, micro, span, top, group_count, shards, *refs):
    pairs = shards // 2
    owners_ref, near_ref, far_ref = refs[:3]
    u_refs = refs[3 : 3 + group_count]
    lb_ref, tok_s, q_s, sem = refs[3 + group_count :]
    experts, rank, share = lb_ref.shape
    tall = u_refs[0].shape[1]
    padded = tall // micro
    block = span // micro
    first = (lax.axis_index("expert") * experts).astype(jnp.float32)
    group = lax.axis_index("dp")
    copies = []
    for g in range(group_count):
        home = lax.rem(group - g + group_count, group_count)
        for i in range(shards):
            source = (far_ref if i >= pairs else near_ref).at[home, i % pairs]
            copies.append(pltpu.make_async_copy(source, tok_s.at[g, owners_ref[i]], sem.at[g, i]))
    for copy in copies:
        copy.start()
    slots = capacity * shards
    windows = slot_windows(slots)
    slot_of = [slot_iota(window, shards // 2 * block) for window in windows]
    for g in range(group_count):
        for i in range(shards):
            copies[g * shards + i].wait()
        names = [read_names(tok_s[g, i, span:, :], span, top) for i in range(shards)]
        codes, gates = slot_codes(names, first, capacity, experts, micro)
        for m in range(micro):
            parts = []
            for h in range(2):
                picks = jnp.concatenate(
                    [
                        jnp.where(
                            codes[m][h][x : x + 1, :] == slot_of[h],
                            gates[m][h][x : x + 1, :],
                            0.0,
                        )
                        for x in range(experts)
                    ],
                    axis=0,
                ).astype(jnp.bfloat16)
                tokens = jnp.concatenate(
                    [
                        tok_s[g, j, m * block : (m + 1) * block, :]
                        for j in range(h * shards // 2, (h + 1) * shards // 2)
                    ],
                    axis=0,
                )
                rows = jnp.dot(picks, tokens, preferred_element_type=jnp.float32)
                parts.append(rows.reshape(experts, -1, share))
            q = join_windows(parts[0], parts[1], windows, padded, 1).astype(jnp.bfloat16)
            at = g * tall + m * padded
            q_s[:, at : at + padded, :] = q
    half = experts // 2
    for x in range(half):
        both = jnp.concatenate([u_refs[g][x] for g in range(group_count)], axis=0)
        lb_ref[x] = adapter_scale * lax.dot_general(
            both[:, :rank], q_s[x], contract_first, preferred_element_type=jnp.float32
        )
        lb_ref[x + half] = adapter_scale * lax.dot_general(
            both[:, rank:], q_s[x + half], contract_first, preferred_element_type=jnp.float32
        )


def ring_order(count):
    return list(range(0, count, 2)) + list(range(1, count, 2))[::-1]


def local_by_tokens(
    output_gradient,
    chosen_expert_index,
    routing_gate_weight,
    hidden,
    frozen_down_weight,
    adapter_input_map,
    adapter_output_map,
):
    sources = lax.axis_size("expert")
    group_count = lax.axis_size("dp")
    micro, experts, slots, units = hidden.shape
    span, top = chosen_expert_index.shape
    width = output_gradient.shape[1]
    rank = adapter_input_map.shape[2]
    capacity = slots // sources
    block = span // micro
    padded = pad_rows(slots)
    share = width // group_count
    pairs = sources // 2
    me = lax.axis_index("expert")
    group = lax.axis_index("dp")

    order = ring_order(pairs)
    place = {z: i for i, z in enumerate(order)}
    ring = [
        (2 * z + c, 2 * order[(place[z] + 1) % pairs] + c) for z in range(pairs) for c in range(2)
    ]
    swap = [(e, e ^ 1) for e in range(sources)]
    owner_table = [
        [
            2 * order[(place[e // 2] - i) % pairs] + (e % 2 if near else 1 - e % 2)
            for near in (True, False)
            for i in range(pairs)
        ]
        for e in range(sources)
    ]
    owners = jnp.asarray(owner_table, jnp.int32)[me]

    amap = jnp.swapaxes(adapter_input_map, 1, 2)
    u = jnp.einsum("mesk,exk->emsx", hidden, amap, preferred_element_type=jnp.float32)
    u = u.astype(jnp.bfloat16)
    u = jnp.pad(u, ((0, 0), (0, 0), (0, padded - slots), (0, 0))).reshape(
        2, experts // 2, micro * padded, rank
    )
    u = jnp.concatenate([u[0], u[1]], axis=-1)

    def shift_groups(array, by):
        return lax.ppermute(
            array, "dp", [(d, (d + by) % group_count) for d in range(group_count)]
        )

    def swap_partners(array):
        return lax.ppermute(array, "expert", swap)

    chunks = 2 if group_count % 2 == 0 else 1
    part = width // chunks

    def exchange_columns(chosen):
        def columns(pieces, g):
            at = g * share % part
            return pieces[g * share // part][:, at : at + share]

        return jnp.stack(
            [jnp.stack([columns(pieces, g) for pieces in chosen]) for g in range(group_count)]
        )

    def across_groups(array):
        return lax.all_to_all(array, "dp", split_axis=0, concat_axis=0, tiled=True)

    others = range(1, group_count)
    names = jnp.concatenate(
        [chosen_expert_index.T.astype(jnp.bfloat16), routing_gate_weight.T], axis=0
    )
    lines = 2 * top * span // share
    names = jnp.tile(names.reshape(lines, share), (1, group_count))
    extra = -(-lines // 8) * 8
    sent = jnp.concatenate(
        [output_gradient, jnp.pad(names, ((0, extra - lines), (0, 0)))], axis=0
    )

    near, far = [[sent[:, c * part : (c + 1) * part] for c in range(chunks)]], []
    for step in range(pairs - 1):
        if step:
            tied = [lax.optimization_barrier(pair) for pair in zip(near[step], far[-1])]
            near[step], far[-1] = [a for a, _ in tied], [b for _, b in tied]
        near.append([lax.ppermute(piece, "expert", ring) for piece in near[step]])
        far.append([swap_partners(piece) for piece in near[step]])
    u_all = [u] + [shift_groups(u, s) for s in others]
    columns = exchange_columns(near)
    columns, u_all, far[-1] = lax.optimization_barrier((columns, u_all, far[-1]))
    columns = across_groups(columns)
    far.append([swap_partners(piece) for piece in near[-1]])
    pieces = [piece for shard in near + far for piece in shard]

    vmem = pl.BlockSpec(memory_space=pltpu.VMEM)
    smem = pl.BlockSpec(memory_space=pltpu.SMEM)
    anywhere = pl.BlockSpec(memory_space=pl.ANY)
    part_a = jax.ShapeDtypeStruct((experts, rank, units // group_count), jnp.bfloat16)
    hidden_grad, routed, *parts = pl.pallas_call(
        functools.partial(expert_kernel, capacity, group_count, sources, chunks),
        out_shape=(
            jax.ShapeDtypeStruct(hidden.shape, jnp.bfloat16),
            jax.ShapeDtypeStruct((sources, top, span), jnp.float32),
        )
        + (part_a,) * group_count,
        in_specs=[smem] + [anywhere] * (sources * chunks) + [vmem, vmem, anywhere, vmem, anywhere],
        out_specs=(vmem,) * 2 + (anywhere,) * group_count,
        scratch_shapes=[
            pltpu.VMEM((sources, span + extra, width), jnp.bfloat16),
            pltpu.VMEM((experts, units + rank, width), jnp.bfloat16),
            pltpu.VMEM((experts, micro * padded, width), jnp.bfloat16),
            pltpu.VMEM((experts, micro * padded, units + rank), jnp.float32),
            pltpu.VMEM((micro, 2, experts, sources // 2 * block), jnp.float32),
            pltpu.VMEM((experts, micro * padded, 1), jnp.float32),
            pltpu.VMEM((micro, 2, experts, sources // 2 * block), jnp.float32),
            pltpu.VMEM((group_count, experts, rank, units // group_count), jnp.bfloat16),
            pltpu.SemaphoreType.DMA((sources, chunks)),
            pltpu.SemaphoreType.DMA((experts,)),
            pltpu.SemaphoreType.DMA((experts,)),
            pltpu.SemaphoreType.DMA((group_count,)),
        ],
        compiler_params=pltpu.CompilerParams(vmem_limit_bytes=58 * 1024 * 1024),
        cost_estimate=pl.CostEstimate(
            flops=2 * experts * micro * padded * width * (units + rank + sources * block),
            bytes_accessed=2 * experts * width * (units + rank) + 2 * sources * span * width,
            transcendentals=0,
        ),
        name="expert_rows",
    )(owners, *pieces, hidden, u, frozen_down_weight, amap, adapter_output_map)

    columns, parts, routed = lax.optimization_barrier((columns, parts, routed))
    swapped = swap_partners(columns)
    arrived = [shift_groups(parts[s], s) for s in others]
    home = lax.all_to_all(routed, "expert", split_axis=0, concat_axis=0, tiled=True)

    lora_b = pl.pallas_call(
        functools.partial(adapter_kernel, capacity, micro, span, top, group_count, sources),
        out_shape=jax.ShapeDtypeStruct((experts, rank, share), jnp.float32),
        in_specs=[smem] + [anywhere] * 2 + [vmem] * group_count,
        out_specs=vmem,
        scratch_shapes=[
            pltpu.VMEM((group_count, sources, span + extra, share), jnp.bfloat16),
            pltpu.VMEM((experts, group_count * micro * padded, share), jnp.bfloat16),
            pltpu.SemaphoreType.DMA((group_count, sources)),
        ],
        compiler_params=pltpu.CompilerParams(vmem_limit_bytes=58 * 1024 * 1024),
        cost_estimate=pl.CostEstimate(
            flops=2 * experts * micro * padded * share * group_count * (rank + sources * block),
            bytes_accessed=2 * group_count * sources * span * share + 4 * experts * rank * share,
            transcendentals=0,
        ),
        name="adapter_columns",
    )(owners, columns, swapped, *u_all)

    home, arrived, lora_b = lax.optimization_barrier((home, arrived, lora_b))
    router_grad = jnp.sum(home, axis=0).T
    lora_a = parts[0].astype(jnp.float32)
    for part in arrived:
        lora_a = lora_a + part.astype(jnp.float32)
    return (hidden_grad, router_grad, lora_a, lora_b)


def local(*arrays):
    sources, groups = lax.axis_size("expert"), lax.axis_size("dp")
    span, width = arrays[0].shape
    top, (micro, experts, slots, units) = arrays[1].shape[1], arrays[3].shape
    even = sources % 2 == 0 and experts % 2 == 0 and width % (128 * groups) == 0 and units % groups == 0
    packs = 2 * top * span % (width // groups) == 0 and (width // groups) % span == 0
    exact = experts * sources <= 256
    if even and packs and exact and sources * span <= micro * experts * slots:
        return local_by_tokens(*arrays)
    return local_by_slots(*arrays)


def solution(mesh):
    in_specs = (
        P(("dp", "expert"), None),
        P(("dp", "expert"), None),
        P(("dp", "expert"), None),
        P(None, ("dp", "expert"), None, None),
        P("expert", None, None),
        P("expert", None, None),
        P("expert", None, None),
    )
    out_specs = (
        P(None, ("dp", "expert"), None, None),
        P(("dp", "expert"), None),
        P("expert", None, "dp"),
        P("expert", None, "dp"),
    )
    return jax.shard_map(local, mesh=mesh, in_specs=in_specs, out_specs=out_specs, check_vma=False)
```

```python
import functools

import jax
import jax.numpy as jnp
from jax import lax
from jax.experimental import pallas as pl
from jax.experimental.pallas import tpu as pltpu
from jax.sharding import PartitionSpec as P

adapter_scale = 2.0


def slot_rows(id_rows, experts, per_device, sources, capacity):
    onehot = (id_rows[:, :, None] == jnp.arange(experts, dtype=jnp.int32)[None, None, :]).astype(
        jnp.int32
    )
    before = jnp.sum(jnp.cumsum(onehot, axis=1) * onehot, axis=2) - 1
    target_dev = id_rows // per_device
    target_slot = id_rows % per_device
    return (target_slot * sources + target_dev) * capacity + before


def pick_rows(source, indices):
    return source[indices]


def dispatch_buffers(grad_rows, weight_rows, send_rows, top_count, buffer_len):
    entry_count = send_rows.shape[1]
    token_count = grad_rows.shape[1]
    filler = jnp.full((buffer_len,), entry_count, jnp.int32)

    def invert(rows):
        return filler.at[rows].set(jnp.arange(entry_count, dtype=jnp.int32))

    table = jax.vmap(invert)(send_rows)
    padded_grad = jnp.concatenate(
        [grad_rows, jnp.zeros((grad_rows.shape[0], 1, grad_rows.shape[2]), grad_rows.dtype)], axis=1
    )
    padded_weight = jnp.concatenate(
        [weight_rows, jnp.zeros((weight_rows.shape[0], 1), weight_rows.dtype)], axis=1
    )
    token_pick = jnp.where(table < entry_count, table // top_count, token_count)
    sent_grad = jax.vmap(pick_rows)(padded_grad, token_pick)
    sent_weight = jax.vmap(pick_rows)(padded_weight, table)
    return (sent_grad, sent_weight)


def expert_rows_view(
    received_gradient,
    received_weight,
    retained_rows,
    frozen_down_weight,
    adapter_input_map,
    adapter_output_map,
):
    frozen_term = jnp.einsum(
        "mesd,efd->mesf", received_gradient, frozen_down_weight, preferred_element_type=jnp.float32
    )
    across_product = jnp.einsum(
        "hati,aki->hatk", received_gradient, adapter_output_map, preferred_element_type=jnp.float32
    ).astype(jnp.bfloat16)
    low_rank_state = jnp.einsum(
        "ptqv,tgv->ptqg", across_product, adapter_input_map, preferred_element_type=jnp.float32
    )
    capacity_slot_weight = received_weight.astype(jnp.float32)[..., None]
    hidden_state_gradient = (
        capacity_slot_weight * (frozen_term + adapter_scale * low_rank_state)
    ).astype(jnp.bfloat16)
    down_mapping = jnp.einsum(
        "lkgu,kup->lkgp", retained_rows, adapter_input_map, preferred_element_type=jnp.float32
    ).astype(jnp.bfloat16)
    complete_term = jnp.sum(frozen_term * retained_rows.astype(jnp.float32), axis=-1)
    adapter_term = jnp.einsum(
        "mesr,mesr->mes", down_mapping, across_product, preferred_element_type=jnp.float32
    )
    routing_rows = complete_term + adapter_scale * adapter_term
    scaled_gradient = (capacity_slot_weight * received_gradient).astype(jnp.bfloat16)
    scaled_across_product = (capacity_slot_weight * across_product.astype(jnp.float32)).astype(
        jnp.bfloat16
    )
    adapter_output_gradient = adapter_scale * jnp.einsum(
        "mesr,mesd->erd", down_mapping, scaled_gradient, preferred_element_type=jnp.float32
    )
    adapter_input_gradient = adapter_scale * jnp.einsum(
        "mesr,mesf->erf", scaled_across_product, retained_rows, preferred_element_type=jnp.float32
    )
    return (hidden_state_gradient, routing_rows, adapter_input_gradient, adapter_output_gradient)


def local_by_slots(
    output_gradient,
    chosen_expert_index,
    routing_gate_weight,
    hidden,
    frozen_down_weight,
    adapter_input_map,
    adapter_output_map,
):
    sources = lax.axis_size("expert")
    per_device = frozen_down_weight.shape[0]
    experts = per_device * sources
    micro_count = hidden.shape[0]
    slot_count = hidden.shape[2]
    capacity = slot_count // sources
    top_count = chosen_expert_index.shape[1]
    model_width = output_gradient.shape[1]
    buffer_len = experts * capacity
    grad_rows = output_gradient.reshape(micro_count, -1, model_width)
    id_rows = chosen_expert_index.reshape(micro_count, -1)
    weight_rows = routing_gate_weight.reshape(micro_count, -1)
    send_rows = slot_rows(id_rows, experts, per_device, sources, capacity)
    sent_grad, sent_weight = dispatch_buffers(
        grad_rows, weight_rows, send_rows, top_count, buffer_len
    )
    sent_grad = sent_grad.reshape(micro_count, per_device, sources, capacity, model_width)
    sent_weight = sent_weight.reshape(micro_count, per_device, sources, capacity)
    received_gradient, received_weight = (
        lax.all_to_all(sent_grad, "expert", split_axis=2, concat_axis=2, tiled=True),
        lax.all_to_all(sent_weight, "expert", split_axis=2, concat_axis=2, tiled=True),
    )
    received_gradient = received_gradient.reshape(micro_count, per_device, slot_count, model_width)
    received_weight = received_weight.reshape(micro_count, per_device, slot_count)
    hidden_grad, routing_rows, adapter_input_gradient, adapter_output_gradient = expert_rows_view(
        received_gradient,
        received_weight,
        hidden,
        frozen_down_weight,
        adapter_input_map,
        adapter_output_map,
    )
    router_home = lax.all_to_all(
        routing_rows.reshape(micro_count, per_device, sources, capacity),
        "expert",
        split_axis=2,
        concat_axis=2,
        tiled=True,
    )
    router_flat = router_home.reshape(micro_count, buffer_len)
    router_grad = jax.vmap(pick_rows)(router_flat, send_rows).reshape(-1, top_count)
    share_a, share_b = (
        lax.psum_scatter(adapter_input_gradient, "dp", scatter_dimension=2, tiled=True),
        lax.psum_scatter(adapter_output_gradient, "dp", scatter_dimension=2, tiled=True),
    )
    return (hidden_grad, router_grad, share_a, share_b)


def pad_rows(count):
    return -(-count // 16) * 16


def read_names(rows, span, top):
    wide = rows.astype(jnp.float32)
    per = wide.shape[1] // span
    lines = [
        wide[k // per : k // per + 1, (k % per) * span : (k % per + 1) * span]
        for k in range(2 * top)
    ]
    return lines[:top], lines[top:]


def slot_codes(names, first, capacity, experts, micro):
    sources = len(names)
    span = names[0][0][0].shape[1]
    block = span // micro
    number = lax.broadcasted_iota(jnp.int32, (experts, span), 0).astype(jnp.float32) + first
    from_row = lax.broadcasted_iota(jnp.int32, (span, span), 0)
    to_row = lax.broadcasted_iota(jnp.int32, (span, span), 1)
    earlier = jnp.where(
        (from_row // block == to_row // block) & (from_row < to_row), 1.0, 0.0
    ).astype(jnp.bfloat16)
    codes, gates = [], []
    for j in range(sources):
        named = jnp.zeros((experts, span), jnp.float32)
        gate = jnp.zeros((experts, span), jnp.float32)
        for name, weight in zip(*names[j]):
            hit = name == number
            named = jnp.where(hit, 1.0, named)
            gate = jnp.where(hit, weight, gate)
        before = jnp.dot(named.astype(jnp.bfloat16), earlier, preferred_element_type=jnp.float32)
        codes.append(jnp.where(named > 0.0, before + float(j * capacity), -1.0))
        gates.append(gate)

    def arrange(values):
        half = sources // 2
        return [
            [
                jnp.concatenate(
                    [c[:, m * block : (m + 1) * block] for c in values[h * half : (h + 1) * half]],
                    axis=1,
                )
                for h in range(2)
            ]
            for m in range(micro)
        ]

    return arrange(codes), arrange(gates)


def slot_windows(slots):
    half = slots // 2
    return [(h * half // 8 * 8, -(-(h + 1) * half // 8) * 8) for h in range(2)]


def slot_iota(window, lanes):
    shape = (window[1] - window[0], lanes)
    return lax.broadcasted_iota(jnp.int32, shape, 0).astype(jnp.float32) + float(window[0])


def join_windows(first_part, second_part, windows, padded, axis):
    (_, end), (start, last) = windows

    def rows(values, low, high):
        return lax.slice_in_dim(values, low, high, axis=axis)

    parts = [rows(first_part, 0, start)]
    if end > start:
        parts.append(rows(first_part, start, end) + rows(second_part, 0, end - start))
    parts.append(rows(second_part, end - start, last - start))
    if padded > last:
        shape = list(first_part.shape)
        shape[axis] = padded - last
        parts.append(jnp.zeros(shape, first_part.dtype))
    return jnp.concatenate(parts, axis=axis)


contract_last = (((1,), (1,)), ((), ()))
contract_first = (((0,), (0,)), ((), ()))


def shard_owner(index, sources):
    pairs = sources // 2
    me = lax.axis_index("expert")
    column, core = me // 2, lax.rem(me, 2)
    place = jnp.where(lax.rem(column, 2) == 0, column // 2, pairs - 1 - column // 2)
    place = lax.rem(place - index % pairs + pairs, pairs)
    column = jnp.where(2 * place < pairs, 2 * place, 2 * (pairs - 1 - place) + 1)
    return 2 * column + (core if index < pairs else 1 - core)


def expert_kernel(capacity, group_count, shards, chunks, *refs):
    token_refs = refs[: shards * chunks]
    refs = refs[shards * chunks :]
    hidden_ref, u_ref, weight_hbm, amap_ref, bmap_hbm, hg_ref, rk_ref = refs[:7]
    la_outs = refs[7 : 7 + group_count]
    scratch = refs[7 + group_count :]
    dy_s, wb_s, rows_s, y_s, code_s, gate_s, back_s, la_s = scratch[:8]
    dy_sem, w_sem, b_sem, la_sem = scratch[8:]
    top, span = rk_ref.shape[1:]
    micro, experts, slots, units = hidden_ref.shape
    rank = amap_ref.shape[1]
    width = dy_s.shape[2]
    block = span // micro
    padded = rows_s.shape[1] // micro
    first = (lax.axis_index("expert") * experts).astype(jnp.float32)

    part = width // chunks
    owners = [shard_owner(i, shards) for i in range(shards)]
    token_copies = [
        pltpu.make_async_copy(
            token_refs[i * chunks + c],
            dy_s.at[owners[i], :, pl.ds(c * part, part)],
            dy_sem.at[i, c],
        )
        for i in range(shards)
        for c in range(chunks)
    ]
    for copy in token_copies:
        copy.start()

    def weight_copies(x):
        return (
            pltpu.make_async_copy(weight_hbm.at[x], wb_s.at[x, pl.ds(0, units)], w_sem.at[x]),
            pltpu.make_async_copy(bmap_hbm.at[x], wb_s.at[x, pl.ds(units, rank)], b_sem.at[x]),
        )

    half = experts // 2
    batch = 2 if half % 2 == 0 else 1
    groups = half // batch

    def members(step):
        at = [step * batch + i for i in range(batch)]
        picked = [(p, p, slice(0, rank)) for p in at]
        return picked + [(p + half, p, slice(rank, 2 * rank)) for p in at]

    def request_weights(step):
        for x, _, _ in members(step):
            for copy in weight_copies(x):
                copy.start()

    for step in range(min(2, groups)):
        request_weights(step)

    for copy in token_copies:
        copy.wait()
    names = [
        read_names(dy_s[i, span:, width - width // group_count :], span, top) for i in range(shards)
    ]
    codes, gates = slot_codes(names, first, capacity, experts, micro)
    windows = slot_windows(slots)
    lanes_of = shards // 2 * block
    slot_of = [slot_iota(window, lanes_of) for window in windows]
    picks = []
    for m in range(micro):
        chosen = [[], []]
        for h in range(2):
            code_s[m, h] = codes[m][h]
        for x in range(experts):
            sums = []
            for h in range(2):
                hit = codes[m][h][x : x + 1, :] == slot_of[h]
                chosen[h].append(jnp.where(hit, 1.0, 0.0))
                sums.append(
                    jnp.sum(
                        jnp.where(hit, gates[m][h][x : x + 1, :], 0.0), axis=1, keepdims=True
                    )
                )
            gate_s[x, m * padded : (m + 1) * padded, :] = join_windows(
                sums[0], sums[1], windows, padded, 0
            )
        picks.append([jnp.concatenate(c, axis=0).astype(jnp.bfloat16) for c in chosen])

    tile = 512 if width % 512 == 0 else width
    for m in range(micro):
        for n in range(width // tile):
            cols = slice(n * tile, (n + 1) * tile)
            parts = []
            for h in range(2):
                tokens = jnp.concatenate(
                    [
                        dy_s[j, m * block : (m + 1) * block, cols]
                        for j in range(h * shards // 2, (h + 1) * shards // 2)
                    ],
                    axis=0,
                )
                rows = jnp.dot(picks[m][h], tokens, preferred_element_type=jnp.float32)
                parts.append(rows.reshape(experts, -1, tile))
            rows_s[:, m * padded : (m + 1) * padded, cols] = join_windows(
                parts[0], parts[1], windows, padded, 1
            ).astype(jnp.bfloat16)

    def main_products(step):
        xs = [x for x, _, _ in members(step)]
        for x in xs:
            for copy in weight_copies(x):
                copy.wait()

        @pl.when(step + 2 < groups)
        def _():
            request_weights(step + 2)

        return [
            lax.dot_general(rows_s[x], wb_s[x], contract_last, preferred_element_type=jnp.float32)
            for x in xs
        ]

    def keep_products(step, products):
        for (x, _, _), product in zip(members(step), products):
            y_s[x] = product

    share = units // group_count
    filler = jnp.zeros((padded - slots, units), jnp.float32)

    def small_steps(step):
        picked = members(step)
        xs = [x for x, _, _ in picked]
        mains = [y_s[x, :, :units] for x in xs]
        vs = [y_s[x, :, units:].astype(jnp.bfloat16) for x in xs]
        lows = [
            jnp.dot(v, amap_ref[x], preferred_element_type=jnp.float32) for v, x in zip(vs, xs)
        ]
        gates_x = [gate_s[x] for x in xs]
        wide = [
            jnp.concatenate(
                [
                    part
                    for m in range(micro)
                    for part in (hidden_ref[m, x].astype(jnp.float32), filler)
                ],
                axis=0,
            )
            for x in xs
        ]
        v_wide = [v.astype(jnp.float32) for v in vs]
        ws = [(gate * v).astype(jnp.bfloat16) for gate, v in zip(gates_x, v_wide)]
        las = [
            lax.dot_general(
                w, held.astype(jnp.bfloat16), contract_first, preferred_element_type=jnp.float32
            )
            for w, held in zip(ws, wide)
        ]
        routed = [
            jnp.sum(main * held, axis=1, keepdims=True)
            + adapter_scale
            * jnp.sum(u_ref[p, :, lanes].astype(jnp.float32) * v, axis=1, keepdims=True)
            for main, held, v, (_, p, lanes) in zip(mains, wide, v_wide, picked)
        ]
        grads = [
            (gate * (main + adapter_scale * low)).astype(jnp.bfloat16)
            for gate, main, low in zip(gates_x, mains, lows)
        ]
        for x, grad, la, back in zip(xs, grads, las, routed):
            for m in range(micro):
                hg_ref[m, x] = grad[m * padded : m * padded + slots]
                for h, (low, high) in enumerate(windows):
                    hit = code_s[m, h, pl.ds(x, 1), :] == slot_of[h]
                    rows = back[m * padded + low : m * padded + high]
                    back_s[m, h, pl.ds(x, 1), :] = jnp.sum(
                        jnp.where(hit, rows, 0.0), axis=0, keepdims=True
                    )
            for k in range(group_count):
                la_s[k, x] = (adapter_scale * la[:, k * share : (k + 1) * share]).astype(
                    la_s.dtype
                )

    def both_steps(step, carry):
        products = main_products(step)
        small_steps(step - 1)
        keep_products(step, products)
        return carry

    keep_products(0, main_products(0))
    lax.fori_loop(1, groups, both_steps, 0)
    small_steps(groups - 1)

    group = lax.axis_index("dp")
    la_copies = [
        pltpu.make_async_copy(
            la_s.at[lax.rem(group + s, group_count)], la_outs[s], la_sem.at[s]
        )
        for s in range(group_count)
    ]
    for copy in la_copies:
        copy.start()
    number = lax.broadcasted_iota(jnp.int32, (experts, span), 0).astype(jnp.float32) + first
    for j in range(shards):
        h, k = j // (shards // 2), j % (shards // 2)
        back = jnp.concatenate(
            [back_s[m, h, :, k * block : (k + 1) * block] for m in range(micro)], axis=1
        )
        found = [
            jnp.sum(jnp.where(name == number, back, 0.0), axis=0, keepdims=True)
            for name in names[j][0]
        ]
        rk_ref[j] = jnp.concatenate(found, axis=0)
    for copy in la_copies:
        copy.wait()


def adapter_kernel(capacity, micro, span, top, group_count, shards, *refs):
    pairs = shards // 2
    near_ref, far_ref = refs[:2]
    u_hbm = refs[2 : 2 + group_count]
    lb_ref, tok_s, q_s, u_refs, sem, u_sem = refs[2 + group_count :]
    experts, rank, share = lb_ref.shape
    tall = u_refs.shape[2]
    padded = tall // micro
    block = span // micro
    first = (lax.axis_index("expert") * experts).astype(jnp.float32)
    group = lax.axis_index("dp")
    owners = [shard_owner(i, shards) for i in range(shards)]
    u_copies = [
        pltpu.make_async_copy(u_hbm[g], u_refs.at[g], u_sem.at[g]) for g in range(group_count)
    ]
    copies = []
    for g in range(group_count):
        home = lax.rem(group - g + group_count, group_count)
        for i in range(shards):
            source = (far_ref if i >= pairs else near_ref).at[home, i % pairs]
            copies.append(pltpu.make_async_copy(source, tok_s.at[g, owners[i]], sem.at[g, i]))
    for copy in copies + u_copies:
        copy.start()
    slots = capacity * shards
    windows = slot_windows(slots)
    slot_of = [slot_iota(window, shards // 2 * block) for window in windows]
    for g in range(group_count):
        for i in range(shards):
            copies[g * shards + i].wait()
        names = [read_names(tok_s[g, i, span:, :], span, top) for i in range(shards)]
        codes, gates = slot_codes(names, first, capacity, experts, micro)
        for m in range(micro):
            parts = []
            for h in range(2):
                picks = jnp.concatenate(
                    [
                        jnp.where(
                            codes[m][h][x : x + 1, :] == slot_of[h],
                            gates[m][h][x : x + 1, :],
                            0.0,
                        )
                        for x in range(experts)
                    ],
                    axis=0,
                ).astype(jnp.bfloat16)
                tokens = jnp.concatenate(
                    [
                        tok_s[g, j, m * block : (m + 1) * block, :]
                        for j in range(h * shards // 2, (h + 1) * shards // 2)
                    ],
                    axis=0,
                )
                rows = jnp.dot(picks, tokens, preferred_element_type=jnp.float32)
                parts.append(rows.reshape(experts, -1, share))
            q = join_windows(parts[0], parts[1], windows, padded, 1).astype(jnp.bfloat16)
            at = g * tall + m * padded
            q_s[:, at : at + padded, :] = q
    for copy in u_copies:
        copy.wait()
    half = experts // 2
    for x in range(half):
        both = jnp.concatenate([u_refs[g, x] for g in range(group_count)], axis=0)
        lb_ref[x] = adapter_scale * lax.dot_general(
            both[:, :rank], q_s[x], contract_first, preferred_element_type=jnp.float32
        )
        lb_ref[x + half] = adapter_scale * lax.dot_general(
            both[:, rank:], q_s[x + half], contract_first, preferred_element_type=jnp.float32
        )


def ring_order(count):
    return list(range(0, count, 2)) + list(range(1, count, 2))[::-1]


def local_by_tokens(
    output_gradient,
    chosen_expert_index,
    routing_gate_weight,
    hidden,
    frozen_down_weight,
    adapter_input_map,
    adapter_output_map,
):
    sources = lax.axis_size("expert")
    group_count = lax.axis_size("dp")
    micro, experts, slots, units = hidden.shape
    span, top = chosen_expert_index.shape
    width = output_gradient.shape[1]
    rank = adapter_input_map.shape[2]
    capacity = slots // sources
    block = span // micro
    padded = pad_rows(slots)
    share = width // group_count
    pairs = sources // 2
    chunks = 2 if group_count % 2 == 0 else 1
    part = width // chunks

    order = ring_order(pairs)
    place = {z: i for i, z in enumerate(order)}
    ring = [
        (2 * z + c, 2 * order[(place[z] + 1) % pairs] + c) for z in range(pairs) for c in range(2)
    ]
    swap = [(e, e ^ 1) for e in range(sources)]

    amap = jnp.swapaxes(adapter_input_map, 1, 2)
    u = jnp.einsum("mesk,exk->emsx", hidden, amap, preferred_element_type=jnp.float32)
    u = u.astype(jnp.bfloat16)
    u = jnp.pad(u, ((0, 0), (0, 0), (0, padded - slots), (0, 0))).reshape(
        2, experts // 2, micro * padded, rank
    )
    u = jnp.concatenate([u[0], u[1]], axis=-1)

    def shift_groups(array, by):
        return lax.ppermute(
            array, "dp", [(d, (d + by) % group_count) for d in range(group_count)]
        )

    def swap_partners(array):
        return lax.ppermute(array, "expert", swap)

    def exchange_columns(chosen):
        def columns(pieces, g):
            at = g * share % part
            return pieces[g * share // part][:, at : at + share]

        return jnp.stack(
            [jnp.stack([columns(pieces, g) for pieces in chosen]) for g in range(group_count)]
        )

    def across_groups(array):
        return lax.all_to_all(array, "dp", split_axis=0, concat_axis=0, tiled=True)

    others = range(1, group_count)
    names = jnp.concatenate(
        [chosen_expert_index.T.astype(jnp.bfloat16), routing_gate_weight.T], axis=0
    )
    lines = 2 * top * span // share
    names = jnp.tile(names.reshape(lines, share), (1, group_count))
    extra = -(-lines // 8) * 8
    sent = jnp.concatenate(
        [output_gradient, jnp.pad(names, ((0, extra - lines), (0, 0)))], axis=0
    )

    near, far = [[sent[:, c * part : (c + 1) * part] for c in range(chunks)]], []
    u_all = [shift_groups(u, s) for s in others]
    for step in range(pairs - 1):
        if step:
            tied = [lax.optimization_barrier(pair) for pair in zip(near[step], far[-1])]
            near[step], far[-1] = [a for a, _ in tied], [b for _, b in tied]
        if step == pairs - 2:
            near[step][0], u_all = lax.optimization_barrier((near[step][0], u_all))
        near.append([lax.ppermute(piece, "expert", ring) for piece in near[step]])
        far.append([swap_partners(piece) for piece in near[step]])
    columns = exchange_columns(near)
    columns, far[-1] = lax.optimization_barrier((columns, far[-1]))
    columns = across_groups(columns)
    far.append([swap_partners(piece) for piece in near[-1]])
    pieces = [piece for shard in near + far for piece in shard]

    vmem = pl.BlockSpec(memory_space=pltpu.VMEM)
    anywhere = pl.BlockSpec(memory_space=pl.ANY)
    part_a = jax.ShapeDtypeStruct((experts, rank, units // group_count), jnp.bfloat16)
    hidden_grad, routed, *parts = pl.pallas_call(
        functools.partial(expert_kernel, capacity, group_count, sources, chunks),
        out_shape=(
            jax.ShapeDtypeStruct(hidden.shape, jnp.bfloat16),
            jax.ShapeDtypeStruct((sources, top, span), jnp.float32),
        )
        + (part_a,) * group_count,
        in_specs=[anywhere] * (sources * chunks) + [vmem, vmem, anywhere, vmem, anywhere],
        out_specs=(vmem,) * 2 + (anywhere,) * group_count,
        scratch_shapes=[
            pltpu.VMEM((sources, span + extra, width), jnp.bfloat16),
            pltpu.VMEM((experts, units + rank, width), jnp.bfloat16),
            pltpu.VMEM((experts, micro * padded, width), jnp.bfloat16),
            pltpu.VMEM((experts, micro * padded, units + rank), jnp.float32),
            pltpu.VMEM((micro, 2, experts, sources // 2 * block), jnp.float32),
            pltpu.VMEM((experts, micro * padded, 1), jnp.float32),
            pltpu.VMEM((micro, 2, experts, sources // 2 * block), jnp.float32),
            pltpu.VMEM((group_count, experts, rank, units // group_count), jnp.bfloat16),
            pltpu.SemaphoreType.DMA((sources, chunks)),
            pltpu.SemaphoreType.DMA((experts,)),
            pltpu.SemaphoreType.DMA((experts,)),
            pltpu.SemaphoreType.DMA((group_count,)),
        ],
        compiler_params=pltpu.CompilerParams(vmem_limit_bytes=58 * 1024 * 1024),
        cost_estimate=pl.CostEstimate(
            flops=2 * experts * micro * padded * width * (units + rank + sources * block),
            bytes_accessed=2 * experts * width * (units + rank) + 2 * sources * span * width,
            transcendentals=0,
        ),
        name="expert_rows",
    )(*pieces, hidden, u, frozen_down_weight, amap, adapter_output_map)

    columns, parts, routed = lax.optimization_barrier((columns, parts, routed))
    swapped = swap_partners(columns)
    arrived = [shift_groups(parts[s], s) for s in others]
    home = lax.all_to_all(routed, "expert", split_axis=0, concat_axis=0, tiled=True)

    lora_b = pl.pallas_call(
        functools.partial(adapter_kernel, capacity, micro, span, top, group_count, sources),
        out_shape=jax.ShapeDtypeStruct((experts, rank, share), jnp.float32),
        in_specs=[anywhere] * (2 + group_count),
        out_specs=vmem,
        scratch_shapes=[
            pltpu.VMEM((group_count, sources, span + extra, share), jnp.bfloat16),
            pltpu.VMEM((experts, group_count * micro * padded, share), jnp.bfloat16),
            pltpu.VMEM((group_count,) + u.shape, jnp.bfloat16),
            pltpu.SemaphoreType.DMA((group_count, sources)),
            pltpu.SemaphoreType.DMA((group_count,)),
        ],
        compiler_params=pltpu.CompilerParams(vmem_limit_bytes=58 * 1024 * 1024),
        cost_estimate=pl.CostEstimate(
            flops=2 * experts * micro * padded * share * group_count * (rank + sources * block),
            bytes_accessed=2 * group_count * sources * span * share + 4 * experts * rank * share,
            transcendentals=0,
        ),
        name="adapter_columns",
    )(columns, swapped, u, *u_all)

    home, arrived, lora_b = lax.optimization_barrier((home, arrived, lora_b))
    router_grad = jnp.sum(home, axis=0).T
    lora_a = parts[0].astype(jnp.float32)
    for part in arrived:
        lora_a = lora_a + part.astype(jnp.float32)
    return (hidden_grad, router_grad, lora_a, lora_b)


def local(*arrays):
    sources, groups = lax.axis_size("expert"), lax.axis_size("dp")
    span, width = arrays[0].shape
    top, (micro, experts, slots, units) = arrays[1].shape[1], arrays[3].shape
    even = sources % 2 == 0 and experts % 2 == 0 and width % (128 * groups) == 0 and units % groups == 0
    packs = 2 * top * span % (width // groups) == 0 and (width // groups) % span == 0
    exact = experts * sources <= 256
    if even and packs and exact and sources * span <= micro * experts * slots:
        return local_by_tokens(*arrays)
    return local_by_slots(*arrays)


def solution(mesh):
    in_specs = (
        P(("dp", "expert"), None),
        P(("dp", "expert"), None),
        P(("dp", "expert"), None),
        P(None, ("dp", "expert"), None, None),
        P("expert", None, None),
        P("expert", None, None),
        P("expert", None, None),
    )
    out_specs = (
        P(None, ("dp", "expert"), None, None),
        P(("dp", "expert"), None),
        P("expert", None, "dp"),
        P("expert", None, "dp"),
    )
    return jax.shard_map(local, mesh=mesh, in_specs=in_specs, out_specs=out_specs, check_vma=False)
```

```python
import functools

import jax
import jax.numpy as jnp
from jax import lax
from jax.experimental import pallas as pl
from jax.experimental.pallas import tpu as pltpu
from jax.sharding import PartitionSpec as P

adapter_scale = 2.0


def slot_rows(id_rows, experts, per_device, sources, capacity):
    onehot = (id_rows[:, :, None] == jnp.arange(experts, dtype=jnp.int32)[None, None, :]).astype(
        jnp.int32
    )
    before = jnp.sum(jnp.cumsum(onehot, axis=1) * onehot, axis=2) - 1
    target_dev = id_rows // per_device
    target_slot = id_rows % per_device
    return (target_slot * sources + target_dev) * capacity + before


def pick_rows(source, indices):
    return source[indices]


def dispatch_buffers(grad_rows, weight_rows, send_rows, top_count, buffer_len):
    entry_count = send_rows.shape[1]
    token_count = grad_rows.shape[1]
    filler = jnp.full((buffer_len,), entry_count, jnp.int32)

    def invert(rows):
        return filler.at[rows].set(jnp.arange(entry_count, dtype=jnp.int32))

    table = jax.vmap(invert)(send_rows)
    padded_grad = jnp.concatenate(
        [grad_rows, jnp.zeros((grad_rows.shape[0], 1, grad_rows.shape[2]), grad_rows.dtype)], axis=1
    )
    padded_weight = jnp.concatenate(
        [weight_rows, jnp.zeros((weight_rows.shape[0], 1), weight_rows.dtype)], axis=1
    )
    token_pick = jnp.where(table < entry_count, table // top_count, token_count)
    sent_grad = jax.vmap(pick_rows)(padded_grad, token_pick)
    sent_weight = jax.vmap(pick_rows)(padded_weight, table)
    return (sent_grad, sent_weight)


def expert_rows_view(
    received_gradient,
    received_weight,
    retained_rows,
    frozen_down_weight,
    adapter_input_map,
    adapter_output_map,
):
    frozen_term = jnp.einsum(
        "mesd,efd->mesf", received_gradient, frozen_down_weight, preferred_element_type=jnp.float32
    )
    across_product = jnp.einsum(
        "hati,aki->hatk", received_gradient, adapter_output_map, preferred_element_type=jnp.float32
    ).astype(jnp.bfloat16)
    low_rank_state = jnp.einsum(
        "ptqv,tgv->ptqg", across_product, adapter_input_map, preferred_element_type=jnp.float32
    )
    capacity_slot_weight = received_weight.astype(jnp.float32)[..., None]
    hidden_state_gradient = (
        capacity_slot_weight * (frozen_term + adapter_scale * low_rank_state)
    ).astype(jnp.bfloat16)
    down_mapping = jnp.einsum(
        "lkgu,kup->lkgp", retained_rows, adapter_input_map, preferred_element_type=jnp.float32
    ).astype(jnp.bfloat16)
    complete_term = jnp.sum(frozen_term * retained_rows.astype(jnp.float32), axis=-1)
    adapter_term = jnp.einsum(
        "mesr,mesr->mes", down_mapping, across_product, preferred_element_type=jnp.float32
    )
    routing_rows = complete_term + adapter_scale * adapter_term
    scaled_gradient = (capacity_slot_weight * received_gradient).astype(jnp.bfloat16)
    scaled_across_product = (capacity_slot_weight * across_product.astype(jnp.float32)).astype(
        jnp.bfloat16
    )
    adapter_output_gradient = adapter_scale * jnp.einsum(
        "mesr,mesd->erd", down_mapping, scaled_gradient, preferred_element_type=jnp.float32
    )
    adapter_input_gradient = adapter_scale * jnp.einsum(
        "mesr,mesf->erf", scaled_across_product, retained_rows, preferred_element_type=jnp.float32
    )
    return (hidden_state_gradient, routing_rows, adapter_input_gradient, adapter_output_gradient)


def local_by_slots(
    output_gradient,
    chosen_expert_index,
    routing_gate_weight,
    hidden,
    frozen_down_weight,
    adapter_input_map,
    adapter_output_map,
):
    sources = lax.axis_size("expert")
    per_device = frozen_down_weight.shape[0]
    experts = per_device * sources
    micro_count = hidden.shape[0]
    slot_count = hidden.shape[2]
    capacity = slot_count // sources
    top_count = chosen_expert_index.shape[1]
    model_width = output_gradient.shape[1]
    buffer_len = experts * capacity
    grad_rows = output_gradient.reshape(micro_count, -1, model_width)
    id_rows = chosen_expert_index.reshape(micro_count, -1)
    weight_rows = routing_gate_weight.reshape(micro_count, -1)
    send_rows = slot_rows(id_rows, experts, per_device, sources, capacity)
    sent_grad, sent_weight = dispatch_buffers(
        grad_rows, weight_rows, send_rows, top_count, buffer_len
    )
    sent_grad = sent_grad.reshape(micro_count, per_device, sources, capacity, model_width)
    sent_weight = sent_weight.reshape(micro_count, per_device, sources, capacity)
    received_gradient, received_weight = (
        lax.all_to_all(sent_grad, "expert", split_axis=2, concat_axis=2, tiled=True),
        lax.all_to_all(sent_weight, "expert", split_axis=2, concat_axis=2, tiled=True),
    )
    received_gradient = received_gradient.reshape(micro_count, per_device, slot_count, model_width)
    received_weight = received_weight.reshape(micro_count, per_device, slot_count)
    hidden_grad, routing_rows, adapter_input_gradient, adapter_output_gradient = expert_rows_view(
        received_gradient,
        received_weight,
        hidden,
        frozen_down_weight,
        adapter_input_map,
        adapter_output_map,
    )
    router_home = lax.all_to_all(
        routing_rows.reshape(micro_count, per_device, sources, capacity),
        "expert",
        split_axis=2,
        concat_axis=2,
        tiled=True,
    )
    router_flat = router_home.reshape(micro_count, buffer_len)
    router_grad = jax.vmap(pick_rows)(router_flat, send_rows).reshape(-1, top_count)
    share_a, share_b = (
        lax.psum_scatter(adapter_input_gradient, "dp", scatter_dimension=2, tiled=True),
        lax.psum_scatter(adapter_output_gradient, "dp", scatter_dimension=2, tiled=True),
    )
    return (hidden_grad, router_grad, share_a, share_b)


def pad_rows(count):
    return -(-count // 16) * 16


def read_names(rows, span, top):
    wide = rows.astype(jnp.float32)
    per = wide.shape[1] // span
    lines = [
        wide[k // per : k // per + 1, (k % per) * span : (k % per + 1) * span]
        for k in range(2 * top)
    ]
    return lines[:top], lines[top:]


def slot_codes(names, first, capacity, experts, micro):
    sources = len(names)
    span = names[0][0][0].shape[1]
    block = span // micro
    number = lax.broadcasted_iota(jnp.int32, (experts, span), 0).astype(jnp.float32) + first
    from_row = lax.broadcasted_iota(jnp.int32, (span, span), 0)
    to_row = lax.broadcasted_iota(jnp.int32, (span, span), 1)
    earlier = jnp.where(
        (from_row // block == to_row // block) & (from_row < to_row), 1.0, 0.0
    ).astype(jnp.bfloat16)
    codes, gates = [], []
    for j in range(sources):
        named = jnp.zeros((experts, span), jnp.float32)
        gate = jnp.zeros((experts, span), jnp.float32)
        for name, weight in zip(*names[j]):
            hit = name == number
            named = jnp.where(hit, 1.0, named)
            gate = jnp.where(hit, weight, gate)
        before = jnp.dot(named.astype(jnp.bfloat16), earlier, preferred_element_type=jnp.float32)
        codes.append(jnp.where(named > 0.0, before + float(j * capacity), -1.0))
        gates.append(gate)

    def arrange(values):
        half = sources // 2
        return [
            [
                jnp.concatenate(
                    [c[:, m * block : (m + 1) * block] for c in values[h * half : (h + 1) * half]],
                    axis=1,
                )
                for h in range(2)
            ]
            for m in range(micro)
        ]

    return arrange(codes), arrange(gates)


def slot_windows(slots):
    half = slots // 2
    return [(h * half // 8 * 8, -(-(h + 1) * half // 8) * 8) for h in range(2)]


def slot_iota(window, lanes):
    shape = (window[1] - window[0], lanes)
    return lax.broadcasted_iota(jnp.int32, shape, 0).astype(jnp.float32) + float(window[0])


def join_windows(first_part, second_part, windows, padded, axis):
    (_, end), (start, last) = windows

    def rows(values, low, high):
        return lax.slice_in_dim(values, low, high, axis=axis)

    parts = [rows(first_part, 0, start)]
    if end > start:
        parts.append(rows(first_part, start, end) + rows(second_part, 0, end - start))
    parts.append(rows(second_part, end - start, last - start))
    if padded > last:
        shape = list(first_part.shape)
        shape[axis] = padded - last
        parts.append(jnp.zeros(shape, first_part.dtype))
    return jnp.concatenate(parts, axis=axis)


contract_last = (((1,), (1,)), ((), ()))
contract_first = (((0,), (0,)), ((), ()))


def shard_owner(index, sources):
    pairs = sources // 2
    me = lax.axis_index("expert")
    column, core = me // 2, lax.rem(me, 2)
    place = jnp.where(lax.rem(column, 2) == 0, column // 2, pairs - 1 - column // 2)
    place = lax.rem(place - index % pairs + pairs, pairs)
    column = jnp.where(2 * place < pairs, 2 * place, 2 * (pairs - 1 - place) + 1)
    return 2 * column + (core if index < pairs else 1 - core)


def expert_kernel(capacity, group_count, shards, chunks, *refs):
    token_refs = refs[: shards * chunks]
    refs = refs[shards * chunks :]
    hidden_ref, u_ref, weight_hbm, amap_ref, bmap_hbm, hg_ref, rk_ref = refs[:7]
    la_outs = refs[7 : 7 + group_count]
    scratch = refs[7 + group_count :]
    dy_s, wb_s, rows_s, y_s, code_s, gate_s, back_s, la_s = scratch[:8]
    dy_sem, w_sem, b_sem, la_sem = scratch[8:]
    top, span = rk_ref.shape[1:]
    micro, experts, slots, units = hidden_ref.shape
    rank = amap_ref.shape[1]
    width = dy_s.shape[2]
    block = span // micro
    padded = rows_s.shape[1] // micro
    first = (lax.axis_index("expert") * experts).astype(jnp.float32)

    part = width // chunks
    owners = [shard_owner(i, shards) for i in range(shards)]
    token_copies = [
        pltpu.make_async_copy(
            token_refs[i * chunks + c],
            dy_s.at[owners[i], :, pl.ds(c * part, part)],
            dy_sem.at[i, c],
        )
        for i in range(shards)
        for c in range(chunks)
    ]
    for copy in token_copies:
        copy.start()

    def weight_copies(x):
        return (
            pltpu.make_async_copy(weight_hbm.at[x], wb_s.at[x, pl.ds(0, units)], w_sem.at[x]),
            pltpu.make_async_copy(bmap_hbm.at[x], wb_s.at[x, pl.ds(units, rank)], b_sem.at[x]),
        )

    half = experts // 2
    batch = 2 if half % 2 == 0 else 1
    groups = half // batch

    def members(step):
        at = [step * batch + i for i in range(batch)]
        picked = [(p, p, slice(0, rank)) for p in at]
        return picked + [(p + half, p, slice(rank, 2 * rank)) for p in at]

    def request_weights(step):
        for x, _, _ in members(step):
            for copy in weight_copies(x):
                copy.start()

    for step in range(min(2, groups)):
        request_weights(step)

    for copy in token_copies:
        copy.wait()
    names = [
        read_names(dy_s[i, span:, width - width // group_count :], span, top) for i in range(shards)
    ]
    codes, gates = slot_codes(names, first, capacity, experts, micro)
    windows = slot_windows(slots)
    lanes_of = shards // 2 * block
    slot_of = [slot_iota(window, lanes_of) for window in windows]
    picks = []
    for m in range(micro):
        chosen = [[], []]
        for h in range(2):
            code_s[m, h] = codes[m][h]
        for x in range(experts):
            sums = []
            for h in range(2):
                hit = codes[m][h][x : x + 1, :] == slot_of[h]
                chosen[h].append(jnp.where(hit, 1.0, 0.0))
                sums.append(
                    jnp.sum(
                        jnp.where(hit, gates[m][h][x : x + 1, :], 0.0), axis=1, keepdims=True
                    )
                )
            gate_s[x, m * padded : (m + 1) * padded, :] = join_windows(
                sums[0], sums[1], windows, padded, 0
            )
        picks.append([jnp.concatenate(c, axis=0).astype(jnp.bfloat16) for c in chosen])

    tile = 512 if width % 512 == 0 else width
    for m in range(micro):
        for n in range(width // tile):
            cols = slice(n * tile, (n + 1) * tile)
            parts = []
            for h in range(2):
                tokens = jnp.concatenate(
                    [
                        dy_s[j, m * block : (m + 1) * block, cols]
                        for j in range(h * shards // 2, (h + 1) * shards // 2)
                    ],
                    axis=0,
                )
                rows = jnp.dot(picks[m][h], tokens, preferred_element_type=jnp.float32)
                parts.append(rows.reshape(experts, -1, tile))
            rows_s[:, m * padded : (m + 1) * padded, cols] = join_windows(
                parts[0], parts[1], windows, padded, 1
            ).astype(jnp.bfloat16)

    def main_products(step):
        xs = [x for x, _, _ in members(step)]
        for x in xs:
            for copy in weight_copies(x):
                copy.wait()

        @pl.when(step + 2 < groups)
        def _():
            request_weights(step + 2)

        return [
            lax.dot_general(rows_s[x], wb_s[x], contract_last, preferred_element_type=jnp.float32)
            for x in xs
        ]

    def keep_products(step, products):
        for (x, _, _), product in zip(members(step), products):
            y_s[x] = product

    share = units // group_count
    filler = jnp.zeros((padded - slots, units), jnp.float32)

    def small_steps(step):
        picked = members(step)
        xs = [x for x, _, _ in picked]
        mains = [y_s[x, :, :units] for x in xs]
        vs = [y_s[x, :, units:].astype(jnp.bfloat16) for x in xs]
        lows = [
            jnp.dot(v, amap_ref[x], preferred_element_type=jnp.float32) for v, x in zip(vs, xs)
        ]
        gates_x = [gate_s[x] for x in xs]
        wide = [
            jnp.concatenate(
                [
                    part
                    for m in range(micro)
                    for part in (hidden_ref[m, x].astype(jnp.float32), filler)
                ],
                axis=0,
            )
            for x in xs
        ]
        v_wide = [v.astype(jnp.float32) for v in vs]
        ws = [(gate * v).astype(jnp.bfloat16) for gate, v in zip(gates_x, v_wide)]
        las = [
            lax.dot_general(
                w, held.astype(jnp.bfloat16), contract_first, preferred_element_type=jnp.float32
            )
            for w, held in zip(ws, wide)
        ]
        routed = [
            jnp.sum(main * held, axis=1, keepdims=True)
            + adapter_scale
            * jnp.sum(u_ref[p, :, lanes].astype(jnp.float32) * v, axis=1, keepdims=True)
            for main, held, v, (_, p, lanes) in zip(mains, wide, v_wide, picked)
        ]
        grads = [
            (gate * (main + adapter_scale * low)).astype(jnp.bfloat16)
            for gate, main, low in zip(gates_x, mains, lows)
        ]
        for x, grad, la, back in zip(xs, grads, las, routed):
            for m in range(micro):
                hg_ref[m, x] = grad[m * padded : m * padded + slots]
                for h, (low, high) in enumerate(windows):
                    hit = code_s[m, h, pl.ds(x, 1), :] == slot_of[h]
                    rows = back[m * padded + low : m * padded + high]
                    back_s[m, h, pl.ds(x, 1), :] = jnp.sum(
                        jnp.where(hit, rows, 0.0), axis=0, keepdims=True
                    )
            for k in range(group_count):
                la_s[k, x] = (adapter_scale * la[:, k * share : (k + 1) * share]).astype(
                    la_s.dtype
                )

    def both_steps(step, carry):
        products = main_products(step)
        small_steps(step - 1)
        keep_products(step, products)
        return carry

    keep_products(0, main_products(0))
    lax.fori_loop(1, groups, both_steps, 0)
    small_steps(groups - 1)

    group = lax.axis_index("dp")
    la_copies = [
        pltpu.make_async_copy(
            la_s.at[lax.rem(group + s, group_count)], la_outs[s], la_sem.at[s]
        )
        for s in range(group_count)
    ]
    for copy in la_copies:
        copy.start()
    number = lax.broadcasted_iota(jnp.int32, (experts, span), 0).astype(jnp.float32) + first
    for j in range(shards):
        h, k = j // (shards // 2), j % (shards // 2)
        back = jnp.concatenate(
            [back_s[m, h, :, k * block : (k + 1) * block] for m in range(micro)], axis=1
        )
        found = [
            jnp.sum(jnp.where(name == number, back, 0.0), axis=0, keepdims=True)
            for name in names[j][0]
        ]
        rk_ref[j] = jnp.concatenate(found, axis=0)
    for copy in la_copies:
        copy.wait()


def adapter_kernel(capacity, micro, span, top, group_count, shards, *refs):
    pairs = shards // 2
    near_ref, far_ref = refs[:2]
    u_hbm = refs[2 : 2 + group_count]
    lb_ref, tok_s, q_s, u_refs, sem, u_sem = refs[2 + group_count :]
    experts, rank, share = lb_ref.shape
    tall = u_refs.shape[2]
    padded = tall // micro
    block = span // micro
    first = (lax.axis_index("expert") * experts).astype(jnp.float32)
    group = lax.axis_index("dp")
    owners = [shard_owner(i, shards) for i in range(shards)]
    u_copies = [
        pltpu.make_async_copy(u_hbm[g], u_refs.at[g], u_sem.at[g]) for g in range(group_count)
    ]
    copies = []
    for g in range(group_count):
        home = lax.rem(group - g + group_count, group_count)
        for i in range(shards):
            source = (far_ref if i >= pairs else near_ref).at[home, i % pairs]
            copies.append(pltpu.make_async_copy(source, tok_s.at[g, owners[i]], sem.at[g, i]))
    for copy in copies + u_copies:
        copy.start()
    slots = capacity * shards
    windows = slot_windows(slots)
    slot_of = [slot_iota(window, shards // 2 * block) for window in windows]
    for g in range(group_count):
        for i in range(shards):
            copies[g * shards + i].wait()
        names = [read_names(tok_s[g, i, span:, :], span, top) for i in range(shards)]
        codes, gates = slot_codes(names, first, capacity, experts, micro)
        for m in range(micro):
            parts = []
            for h in range(2):
                picks = jnp.concatenate(
                    [
                        jnp.where(
                            codes[m][h][x : x + 1, :] == slot_of[h],
                            gates[m][h][x : x + 1, :],
                            0.0,
                        )
                        for x in range(experts)
                    ],
                    axis=0,
                ).astype(jnp.bfloat16)
                tokens = jnp.concatenate(
                    [
                        tok_s[g, j, m * block : (m + 1) * block, :]
                        for j in range(h * shards // 2, (h + 1) * shards // 2)
                    ],
                    axis=0,
                )
                rows = jnp.dot(picks, tokens, preferred_element_type=jnp.float32)
                parts.append(rows.reshape(experts, -1, share))
            q = join_windows(parts[0], parts[1], windows, padded, 1).astype(jnp.bfloat16)
            at = g * tall + m * padded
            q_s[:, at : at + padded, :] = q
    for copy in u_copies:
        copy.wait()
    half = experts // 2
    for x in range(half):
        both = jnp.concatenate([u_refs[g, x] for g in range(group_count)], axis=0)
        lb_ref[x] = adapter_scale * lax.dot_general(
            both[:, :rank], q_s[x], contract_first, preferred_element_type=jnp.float32
        )
        lb_ref[x + half] = adapter_scale * lax.dot_general(
            both[:, rank:], q_s[x + half], contract_first, preferred_element_type=jnp.float32
        )


def ring_order(count):
    return list(range(0, count, 2)) + list(range(1, count, 2))[::-1]


def local_by_tokens(
    output_gradient,
    chosen_expert_index,
    routing_gate_weight,
    hidden,
    frozen_down_weight,
    adapter_input_map,
    adapter_output_map,
):
    sources = lax.axis_size("expert")
    group_count = lax.axis_size("dp")
    micro, experts, slots, units = hidden.shape
    span, top = chosen_expert_index.shape
    width = output_gradient.shape[1]
    rank = adapter_input_map.shape[2]
    capacity = slots // sources
    block = span // micro
    padded = pad_rows(slots)
    share = width // group_count
    pairs = sources // 2
    chunks = 2 if group_count % 2 == 0 else 1
    part = width // chunks

    order = ring_order(pairs)
    place = {z: i for i, z in enumerate(order)}
    ring = [
        (2 * z + c, 2 * order[(place[z] + 1) % pairs] + c) for z in range(pairs) for c in range(2)
    ]
    swap = [(e, e ^ 1) for e in range(sources)]

    amap = jnp.swapaxes(adapter_input_map, 1, 2)
    u = jnp.einsum("mesk,exk->emsx", hidden, amap, preferred_element_type=jnp.float32)
    u = u.astype(jnp.bfloat16)
    u = jnp.pad(u, ((0, 0), (0, 0), (0, padded - slots), (0, 0))).reshape(
        2, experts // 2, micro * padded, rank
    )
    u = jnp.concatenate([u[0], u[1]], axis=-1)

    def shift_groups(array, by):
        return lax.ppermute(
            array, "dp", [(d, (d + by) % group_count) for d in range(group_count)]
        )

    def swap_partners(array):
        return lax.ppermute(array, "expert", swap)

    def exchange_columns(chosen):
        def columns(pieces, g):
            at = g * share % part
            own = pieces[g * share // part][:, at : at + share]
            line = lax.broadcasted_iota(jnp.int32, own.shape, 0)
            return jnp.where(line < span, own, pieces[-1][:, :share])

        return jnp.stack(
            [jnp.stack([columns(pieces, g) for pieces in chosen]) for g in range(group_count)]
        )

    def across_groups(array):
        return lax.all_to_all(array, "dp", split_axis=0, concat_axis=0, tiled=True)

    others = range(1, group_count)
    lines = 2 * top * span // share
    extra = -(-lines // 8) * 8
    part_rows, chosen_expert_index = lax.optimization_barrier(
        (
            jnp.pad(output_gradient[:, :part], ((0, extra), (0, 0))),
            chosen_expert_index,
        )
    )
    names = jnp.concatenate(
        [chosen_expert_index.T.astype(jnp.bfloat16), routing_gate_weight.T], axis=0
    )
    names = jnp.tile(names.reshape(lines, share), (1, group_count // chunks))
    below = jnp.pad(names, ((0, extra - lines), (0, 0)))
    last = jnp.concatenate([output_gradient[:, width - part :], below], axis=0)
    sent = [part_rows, last] if chunks == 2 else [last]

    near, far = [sent], []
    u_all = [shift_groups(u, s) for s in others]
    halves = [(step, c) for step in range(1, pairs - 1) for c in range(chunks)][1:]
    moments = [halves[min(k, len(halves) - 1)] for k in range(len(u_all)) if halves]
    for step in range(pairs - 1):
        here = near[step]
        if step > 1:
            tied = [
                lax.optimization_barrier((here[c], [shard[c] for shard in far]))
                for c in range(chunks)
            ]
            here = [a for a, _ in tied]
            far = [[b[k] for _, b in tied] for k in range(len(far))]
        for k, (at, c) in enumerate(moments):
            if at == step:
                here[c], u_all[k] = lax.optimization_barrier((here[c], u_all[k]))
        near[step] = here
        near.append([lax.ppermute(piece, "expert", ring) for piece in here])
        if step:
            far.append([swap_partners(piece) for piece in here])
        else:
            tied = [lax.optimization_barrier(pair) for pair in zip(here, near[1])]
            near[1] = [b for _, b in tied]
            far.append([swap_partners(a) for a, _ in tied])
    far.append([swap_partners(piece) for piece in near[-1]])
    columns = exchange_columns(near)
    columns, far[-2:] = lax.optimization_barrier((columns, far[-2:]))
    columns = across_groups(columns)
    pieces = [piece for shard in near + far for piece in shard]

    vmem = pl.BlockSpec(memory_space=pltpu.VMEM)
    anywhere = pl.BlockSpec(memory_space=pl.ANY)
    part_a = jax.ShapeDtypeStruct((experts, rank, units // group_count), jnp.bfloat16)
    hidden_grad, routed, *parts = pl.pallas_call(
        functools.partial(expert_kernel, capacity, group_count, sources, chunks),
        out_shape=(
            jax.ShapeDtypeStruct(hidden.shape, jnp.bfloat16),
            jax.ShapeDtypeStruct((sources, top, span), jnp.float32),
        )
        + (part_a,) * group_count,
        in_specs=[anywhere] * (sources * chunks) + [vmem, vmem, anywhere, vmem, anywhere],
        out_specs=(vmem,) * 2 + (anywhere,) * group_count,
        scratch_shapes=[
            pltpu.VMEM((sources, span + extra, width), jnp.bfloat16),
            pltpu.VMEM((experts, units + rank, width), jnp.bfloat16),
            pltpu.VMEM((experts, micro * padded, width), jnp.bfloat16),
            pltpu.VMEM((experts, micro * padded, units + rank), jnp.float32),
            pltpu.VMEM((micro, 2, experts, sources // 2 * block), jnp.float32),
            pltpu.VMEM((experts, micro * padded, 1), jnp.float32),
            pltpu.VMEM((micro, 2, experts, sources // 2 * block), jnp.float32),
            pltpu.VMEM((group_count, experts, rank, units // group_count), jnp.bfloat16),
            pltpu.SemaphoreType.DMA((sources, chunks)),
            pltpu.SemaphoreType.DMA((experts,)),
            pltpu.SemaphoreType.DMA((experts,)),
            pltpu.SemaphoreType.DMA((group_count,)),
        ],
        compiler_params=pltpu.CompilerParams(vmem_limit_bytes=52 * 1024 * 1024),
        cost_estimate=pl.CostEstimate(
            flops=2 * experts * micro * padded * width * (units + rank + sources * block),
            bytes_accessed=2 * experts * width * (units + rank) + 2 * sources * span * width,
            transcendentals=0,
        ),
        name="expert_rows",
    )(*pieces, hidden, u, frozen_down_weight, amap, adapter_output_map)

    columns, parts, routed = lax.optimization_barrier((columns, parts, routed))
    swapped = swap_partners(columns)
    arrived = [shift_groups(parts[s], s) for s in others]
    home = lax.all_to_all(routed, "expert", split_axis=0, concat_axis=0, tiled=True)

    lora_b = pl.pallas_call(
        functools.partial(adapter_kernel, capacity, micro, span, top, group_count, sources),
        out_shape=jax.ShapeDtypeStruct((experts, rank, share), jnp.float32),
        in_specs=[anywhere] * (2 + group_count),
        out_specs=vmem,
        scratch_shapes=[
            pltpu.VMEM((group_count, sources, span + extra, share), jnp.bfloat16),
            pltpu.VMEM((experts, group_count * micro * padded, share), jnp.bfloat16),
            pltpu.VMEM((group_count,) + u.shape, jnp.bfloat16),
            pltpu.SemaphoreType.DMA((group_count, sources)),
            pltpu.SemaphoreType.DMA((group_count,)),
        ],
        compiler_params=pltpu.CompilerParams(vmem_limit_bytes=58 * 1024 * 1024),
        cost_estimate=pl.CostEstimate(
            flops=2 * experts * micro * padded * share * group_count * (rank + sources * block),
            bytes_accessed=2 * group_count * sources * span * share + 4 * experts * rank * share,
            transcendentals=0,
        ),
        name="adapter_columns",
    )(columns, swapped, u, *u_all)

    home, arrived, lora_b = lax.optimization_barrier((home, arrived, lora_b))
    router_grad = jnp.sum(home, axis=0).T
    lora_a = parts[0].astype(jnp.float32)
    for part in arrived:
        lora_a = lora_a + part.astype(jnp.float32)
    return (hidden_grad, router_grad, lora_a, lora_b)


def local(*arrays):
    sources, groups = lax.axis_size("expert"), lax.axis_size("dp")
    span, width = arrays[0].shape
    top, (micro, experts, slots, units) = arrays[1].shape[1], arrays[3].shape
    even = sources % 2 == 0 and experts % 2 == 0 and width % (128 * groups) == 0 and units % groups == 0
    packs = 2 * top * span % (width // groups) == 0 and (width // groups) % span == 0
    exact = experts * sources <= 256
    if even and packs and exact and sources * span <= micro * experts * slots:
        return local_by_tokens(*arrays)
    return local_by_slots(*arrays)


def solution(mesh):
    in_specs = (
        P(("dp", "expert"), None),
        P(("dp", "expert"), None),
        P(("dp", "expert"), None),
        P(None, ("dp", "expert"), None, None),
        P("expert", None, None),
        P("expert", None, None),
        P("expert", None, None),
    )
    out_specs = (
        P(None, ("dp", "expert"), None, None),
        P(("dp", "expert"), None),
        P("expert", None, "dp"),
        P("expert", None, "dp"),
    )
    return jax.shard_map(local, mesh=mesh, in_specs=in_specs, out_specs=out_specs, check_vma=False)
```

```python
import functools

import jax
import jax.numpy as jnp
from jax import lax
from jax.experimental import pallas as pl
from jax.experimental.pallas import tpu as pltpu
from jax.sharding import PartitionSpec as P

adapter_scale = 2.0


def slot_rows(id_rows, experts, per_device, sources, capacity):
    onehot = (id_rows[:, :, None] == jnp.arange(experts, dtype=jnp.int32)[None, None, :]).astype(
        jnp.int32
    )
    before = jnp.sum(jnp.cumsum(onehot, axis=1) * onehot, axis=2) - 1
    target_dev = id_rows // per_device
    target_slot = id_rows % per_device
    return (target_slot * sources + target_dev) * capacity + before


def pick_rows(source, indices):
    return source[indices]


def dispatch_buffers(grad_rows, weight_rows, send_rows, top_count, buffer_len):
    entry_count = send_rows.shape[1]
    token_count = grad_rows.shape[1]
    filler = jnp.full((buffer_len,), entry_count, jnp.int32)

    def invert(rows):
        return filler.at[rows].set(jnp.arange(entry_count, dtype=jnp.int32))

    table = jax.vmap(invert)(send_rows)
    padded_grad = jnp.concatenate(
        [grad_rows, jnp.zeros((grad_rows.shape[0], 1, grad_rows.shape[2]), grad_rows.dtype)], axis=1
    )
    padded_weight = jnp.concatenate(
        [weight_rows, jnp.zeros((weight_rows.shape[0], 1), weight_rows.dtype)], axis=1
    )
    token_pick = jnp.where(table < entry_count, table // top_count, token_count)
    sent_grad = jax.vmap(pick_rows)(padded_grad, token_pick)
    sent_weight = jax.vmap(pick_rows)(padded_weight, table)
    return (sent_grad, sent_weight)


def expert_rows_view(
    received_gradient,
    received_weight,
    retained_rows,
    frozen_down_weight,
    adapter_input_map,
    adapter_output_map,
):
    frozen_term = jnp.einsum(
        "mesd,efd->mesf", received_gradient, frozen_down_weight, preferred_element_type=jnp.float32
    )
    across_product = jnp.einsum(
        "hati,aki->hatk", received_gradient, adapter_output_map, preferred_element_type=jnp.float32
    ).astype(jnp.bfloat16)
    low_rank_state = jnp.einsum(
        "ptqv,tgv->ptqg", across_product, adapter_input_map, preferred_element_type=jnp.float32
    )
    capacity_slot_weight = received_weight.astype(jnp.float32)[..., None]
    hidden_state_gradient = (
        capacity_slot_weight * (frozen_term + adapter_scale * low_rank_state)
    ).astype(jnp.bfloat16)
    down_mapping = jnp.einsum(
        "lkgu,kup->lkgp", retained_rows, adapter_input_map, preferred_element_type=jnp.float32
    ).astype(jnp.bfloat16)
    complete_term = jnp.sum(frozen_term * retained_rows.astype(jnp.float32), axis=-1)
    adapter_term = jnp.einsum(
        "mesr,mesr->mes", down_mapping, across_product, preferred_element_type=jnp.float32
    )
    routing_rows = complete_term + adapter_scale * adapter_term
    scaled_gradient = (capacity_slot_weight * received_gradient).astype(jnp.bfloat16)
    scaled_across_product = (capacity_slot_weight * across_product.astype(jnp.float32)).astype(
        jnp.bfloat16
    )
    adapter_output_gradient = adapter_scale * jnp.einsum(
        "mesr,mesd->erd", down_mapping, scaled_gradient, preferred_element_type=jnp.float32
    )
    adapter_input_gradient = adapter_scale * jnp.einsum(
        "mesr,mesf->erf", scaled_across_product, retained_rows, preferred_element_type=jnp.float32
    )
    return (hidden_state_gradient, routing_rows, adapter_input_gradient, adapter_output_gradient)


def local_by_slots(
    output_gradient,
    chosen_expert_index,
    routing_gate_weight,
    hidden,
    frozen_down_weight,
    adapter_input_map,
    adapter_output_map,
):
    sources = lax.axis_size("expert")
    per_device = frozen_down_weight.shape[0]
    experts = per_device * sources
    micro_count = hidden.shape[0]
    slot_count = hidden.shape[2]
    capacity = slot_count // sources
    top_count = chosen_expert_index.shape[1]
    model_width = output_gradient.shape[1]
    buffer_len = experts * capacity
    grad_rows = output_gradient.reshape(micro_count, -1, model_width)
    id_rows = chosen_expert_index.reshape(micro_count, -1)
    weight_rows = routing_gate_weight.reshape(micro_count, -1)
    send_rows = slot_rows(id_rows, experts, per_device, sources, capacity)
    sent_grad, sent_weight = dispatch_buffers(
        grad_rows, weight_rows, send_rows, top_count, buffer_len
    )
    sent_grad = sent_grad.reshape(micro_count, per_device, sources, capacity, model_width)
    sent_weight = sent_weight.reshape(micro_count, per_device, sources, capacity)
    received_gradient, received_weight = (
        lax.all_to_all(sent_grad, "expert", split_axis=2, concat_axis=2, tiled=True),
        lax.all_to_all(sent_weight, "expert", split_axis=2, concat_axis=2, tiled=True),
    )
    received_gradient = received_gradient.reshape(micro_count, per_device, slot_count, model_width)
    received_weight = received_weight.reshape(micro_count, per_device, slot_count)
    hidden_grad, routing_rows, adapter_input_gradient, adapter_output_gradient = expert_rows_view(
        received_gradient,
        received_weight,
        hidden,
        frozen_down_weight,
        adapter_input_map,
        adapter_output_map,
    )
    router_home = lax.all_to_all(
        routing_rows.reshape(micro_count, per_device, sources, capacity),
        "expert",
        split_axis=2,
        concat_axis=2,
        tiled=True,
    )
    router_flat = router_home.reshape(micro_count, buffer_len)
    router_grad = jax.vmap(pick_rows)(router_flat, send_rows).reshape(-1, top_count)
    share_a, share_b = (
        lax.psum_scatter(adapter_input_gradient, "dp", scatter_dimension=2, tiled=True),
        lax.psum_scatter(adapter_output_gradient, "dp", scatter_dimension=2, tiled=True),
    )
    return (hidden_grad, router_grad, share_a, share_b)


def pad_rows(count):
    return -(-count // 16) * 16


def read_names(rows, span, top):
    wide = rows.astype(jnp.float32)
    per = wide.shape[1] // span
    lines = [
        wide[k // per : k // per + 1, (k % per) * span : (k % per + 1) * span]
        for k in range(2 * top)
    ]
    return lines[:top], lines[top:]


def slot_codes(names, first, capacity, experts, micro):
    sources = len(names)
    span = names[0][0][0].shape[1]
    block = span // micro
    number = lax.broadcasted_iota(jnp.int32, (experts, span), 0).astype(jnp.float32) + first
    from_row = lax.broadcasted_iota(jnp.int32, (span, span), 0)
    to_row = lax.broadcasted_iota(jnp.int32, (span, span), 1)
    earlier = jnp.where(
        (from_row // block == to_row // block) & (from_row < to_row), 1.0, 0.0
    ).astype(jnp.bfloat16)
    codes, gates = [], []
    for j in range(sources):
        named = jnp.zeros((experts, span), jnp.float32)
        gate = jnp.zeros((experts, span), jnp.float32)
        for name, weight in zip(*names[j]):
            hit = name == number
            named = jnp.where(hit, 1.0, named)
            gate = jnp.where(hit, weight, gate)
        before = jnp.dot(named.astype(jnp.bfloat16), earlier, preferred_element_type=jnp.float32)
        codes.append(jnp.where(named > 0.0, before + float(j * capacity), -1.0))
        gates.append(gate)

    def arrange(values):
        half = sources // 2
        return [
            [
                jnp.concatenate(
                    [c[:, m * block : (m + 1) * block] for c in values[h * half : (h + 1) * half]],
                    axis=1,
                )
                for h in range(2)
            ]
            for m in range(micro)
        ]

    return arrange(codes), arrange(gates)


def slot_windows(slots):
    half = slots // 2
    return [(h * half // 8 * 8, -(-(h + 1) * half // 8) * 8) for h in range(2)]


def slot_iota(window, lanes):
    shape = (window[1] - window[0], lanes)
    return lax.broadcasted_iota(jnp.int32, shape, 0).astype(jnp.float32) + float(window[0])


def join_windows(first_part, second_part, windows, padded, axis):
    (_, end), (start, last) = windows

    def rows(values, low, high):
        return lax.slice_in_dim(values, low, high, axis=axis)

    parts = [rows(first_part, 0, start)]
    if end > start:
        parts.append(rows(first_part, start, end) + rows(second_part, 0, end - start))
    parts.append(rows(second_part, end - start, last - start))
    if padded > last:
        shape = list(first_part.shape)
        shape[axis] = padded - last
        parts.append(jnp.zeros(shape, first_part.dtype))
    return jnp.concatenate(parts, axis=axis)


contract_last = (((1,), (1,)), ((), ()))
contract_first = (((0,), (0,)), ((), ()))


def shard_owner(index, sources):
    pairs = sources // 2
    me = lax.axis_index("expert")
    column, core = me // 2, lax.rem(me, 2)
    place = jnp.where(lax.rem(column, 2) == 0, column // 2, pairs - 1 - column // 2)
    place = lax.rem(place - index % pairs + pairs, pairs)
    column = jnp.where(2 * place < pairs, 2 * place, 2 * (pairs - 1 - place) + 1)
    return 2 * column + (core if index < pairs else 1 - core)


def expert_kernel(capacity, group_count, shards, chunks, *refs):
    token_refs = refs[: shards * chunks]
    refs = refs[shards * chunks :]
    hidden_ref, u_ref, weight_hbm, amap_ref, bmap_hbm, hg_ref, rk_ref = refs[:7]
    la_outs = refs[7 : 7 + group_count]
    scratch = refs[7 + group_count :]
    dy_s, wb_s, rows_s, y_s, code_s, gate_s, back_s, la_s = scratch[:8]
    dy_sem, w_sem, b_sem, la_sem = scratch[8:]
    top, span = rk_ref.shape[1:]
    micro, experts, slots, units = hidden_ref.shape
    rank = amap_ref.shape[1]
    width = dy_s.shape[2]
    block = span // micro
    padded = rows_s.shape[1] // micro
    first = (lax.axis_index("expert") * experts).astype(jnp.float32)

    part = width // chunks
    owners = [shard_owner(i, shards) for i in range(shards)]
    token_copies = [
        pltpu.make_async_copy(
            token_refs[i * chunks + c],
            dy_s.at[owners[i], :, pl.ds(c * part, part)],
            dy_sem.at[i, c],
        )
        for i in range(shards)
        for c in range(chunks)
    ]
    for copy in token_copies:
        copy.start()

    def weight_copies(x):
        return (
            pltpu.make_async_copy(weight_hbm.at[x], wb_s.at[x, pl.ds(0, units)], w_sem.at[x]),
            pltpu.make_async_copy(bmap_hbm.at[x], wb_s.at[x, pl.ds(units, rank)], b_sem.at[x]),
        )

    half = experts // 2
    batch = 2 if half % 2 == 0 else 1
    groups = half // batch

    def members(step):
        at = [step * batch + i for i in range(batch)]
        picked = [(p, p, slice(0, rank)) for p in at]
        return picked + [(p + half, p, slice(rank, 2 * rank)) for p in at]

    def request_weights(step):
        for x, _, _ in members(step):
            for copy in weight_copies(x):
                copy.start()

    for step in range(min(2, groups)):
        request_weights(step)

    for copy in token_copies:
        copy.wait()
    names = [
        read_names(dy_s[i, span:, width - width // group_count :], span, top) for i in range(shards)
    ]
    codes, gates = slot_codes(names, first, capacity, experts, micro)
    windows = slot_windows(slots)
    lanes_of = shards // 2 * block
    slot_of = [slot_iota(window, lanes_of) for window in windows]
    picks = []
    for m in range(micro):
        chosen = [[], []]
        for h in range(2):
            code_s[m, h] = codes[m][h]
        for x in range(experts):
            sums = []
            for h in range(2):
                hit = codes[m][h][x : x + 1, :] == slot_of[h]
                chosen[h].append(jnp.where(hit, 1.0, 0.0))
                sums.append(
                    jnp.sum(
                        jnp.where(hit, gates[m][h][x : x + 1, :], 0.0), axis=1, keepdims=True
                    )
                )
            gate_s[x, m * padded : (m + 1) * padded, :] = join_windows(
                sums[0], sums[1], windows, padded, 0
            )
        picks.append([jnp.concatenate(c, axis=0).astype(jnp.bfloat16) for c in chosen])

    tile = 512 if width % 512 == 0 else width
    for m in range(micro):
        for n in range(width // tile):
            cols = slice(n * tile, (n + 1) * tile)
            parts = []
            for h in range(2):
                tokens = jnp.concatenate(
                    [
                        dy_s[j, m * block : (m + 1) * block, cols]
                        for j in range(h * shards // 2, (h + 1) * shards // 2)
                    ],
                    axis=0,
                )
                rows = jnp.dot(picks[m][h], tokens, preferred_element_type=jnp.float32)
                parts.append(rows.reshape(experts, -1, tile))
            rows_s[:, m * padded : (m + 1) * padded, cols] = join_windows(
                parts[0], parts[1], windows, padded, 1
            ).astype(jnp.bfloat16)

    def main_products(step):
        xs = [x for x, _, _ in members(step)]
        for x in xs:
            for copy in weight_copies(x):
                copy.wait()

        @pl.when(step + 2 < groups)
        def _():
            request_weights(step + 2)

        return [
            lax.dot_general(rows_s[x], wb_s[x], contract_last, preferred_element_type=jnp.float32)
            for x in xs
        ]

    def keep_products(step, products):
        for (x, _, _), product in zip(members(step), products):
            y_s[x] = product

    share = units // group_count
    filler = jnp.zeros((padded - slots, units), jnp.float32)

    def small_steps(step):
        picked = members(step)
        xs = [x for x, _, _ in picked]
        mains = [y_s[x, :, :units] for x in xs]
        vs = [y_s[x, :, units:].astype(jnp.bfloat16) for x in xs]
        lows = [
            jnp.dot(v, amap_ref[x], preferred_element_type=jnp.float32) for v, x in zip(vs, xs)
        ]
        gates_x = [gate_s[x] for x in xs]
        wide = [
            jnp.concatenate(
                [
                    part
                    for m in range(micro)
                    for part in (hidden_ref[m, x].astype(jnp.float32), filler)
                ],
                axis=0,
            )
            for x in xs
        ]
        v_wide = [v.astype(jnp.float32) for v in vs]
        ws = [(gate * v).astype(jnp.bfloat16) for gate, v in zip(gates_x, v_wide)]
        las = [
            lax.dot_general(
                w, held.astype(jnp.bfloat16), contract_first, preferred_element_type=jnp.float32
            )
            for w, held in zip(ws, wide)
        ]
        routed = [
            jnp.sum(main * held, axis=1, keepdims=True)
            + adapter_scale
            * jnp.sum(u_ref[p, :, lanes].astype(jnp.float32) * v, axis=1, keepdims=True)
            for main, held, v, (_, p, lanes) in zip(mains, wide, v_wide, picked)
        ]
        grads = [
            (gate * (main + adapter_scale * low)).astype(jnp.bfloat16)
            for gate, main, low in zip(gates_x, mains, lows)
        ]
        for x, grad, la, back in zip(xs, grads, las, routed):
            for m in range(micro):
                hg_ref[m, x] = grad[m * padded : m * padded + slots]
                for h, (low, high) in enumerate(windows):
                    hit = code_s[m, h, pl.ds(x, 1), :] == slot_of[h]
                    rows = back[m * padded + low : m * padded + high]
                    back_s[m, h, pl.ds(x, 1), :] = jnp.sum(
                        jnp.where(hit, rows, 0.0), axis=0, keepdims=True
                    )
            for k in range(group_count):
                la_s[k, x] = (adapter_scale * la[:, k * share : (k + 1) * share]).astype(
                    la_s.dtype
                )

    def both_steps(step, carry):
        products = main_products(step)
        small_steps(step - 1)
        keep_products(step, products)
        return carry

    keep_products(0, main_products(0))
    lax.fori_loop(1, groups, both_steps, 0)
    small_steps(groups - 1)

    group = lax.axis_index("dp")
    la_copies = [
        pltpu.make_async_copy(
            la_s.at[lax.rem(group + s, group_count)], la_outs[s], la_sem.at[s]
        )
        for s in range(group_count)
    ]
    for copy in la_copies:
        copy.start()
    number = lax.broadcasted_iota(jnp.int32, (experts, span), 0).astype(jnp.float32) + first
    for j in range(shards):
        h, k = j // (shards // 2), j % (shards // 2)
        back = jnp.concatenate(
            [back_s[m, h, :, k * block : (k + 1) * block] for m in range(micro)], axis=1
        )
        found = [
            jnp.sum(jnp.where(name == number, back, 0.0), axis=0, keepdims=True)
            for name in names[j][0]
        ]
        rk_ref[j] = jnp.concatenate(found, axis=0)
    for copy in la_copies:
        copy.wait()


def adapter_kernel(capacity, micro, span, top, group_count, shards, *refs):
    pairs = shards // 2
    early_ref, early_far_ref, near_ref, far_ref = refs[:4]
    lb_ref, tok_s, q_s, u_refs, sem, u_sem = refs[4:]
    experts, rank, share = lb_ref.shape
    blocks, tall = u_refs.shape[1:3]
    padded = tall // micro
    block = span // micro
    first = (lax.axis_index("expert") * experts).astype(jnp.float32)
    group = lax.axis_index("dp")
    owners = [shard_owner(i, shards) for i in range(shards)]
    copies, u_copies = [], []
    for g in range(group_count):
        home = lax.rem(group - g + group_count, group_count)
        for i in range(shards):
            if i % pairs:
                source = (far_ref if i >= pairs else near_ref).at[home, i % pairs - 1]
            elif i:
                source = early_far_ref.at[home]
            else:
                source = early_ref.at[home, pl.ds(blocks * tall, tok_s.shape[2])]
            copies.append(pltpu.make_async_copy(source, tok_s.at[g, owners[i]], sem.at[g, i]))
        for k in range(blocks):
            source = early_ref.at[home, pl.ds(k * tall, tall)]
            u_copies.append(pltpu.make_async_copy(source, u_refs.at[g, k], u_sem.at[g, k]))
    for copy in copies + u_copies:
        copy.start()
    slots = capacity * shards
    windows = slot_windows(slots)
    slot_of = [slot_iota(window, shards // 2 * block) for window in windows]
    for g in range(group_count):
        for i in range(shards):
            copies[g * shards + i].wait()
        names = [read_names(tok_s[g, i, span:, :], span, top) for i in range(shards)]
        codes, gates = slot_codes(names, first, capacity, experts, micro)
        for m in range(micro):
            parts = []
            for h in range(2):
                picks = jnp.concatenate(
                    [
                        jnp.where(
                            codes[m][h][x : x + 1, :] == slot_of[h],
                            gates[m][h][x : x + 1, :],
                            0.0,
                        )
                        for x in range(experts)
                    ],
                    axis=0,
                ).astype(jnp.bfloat16)
                tokens = jnp.concatenate(
                    [
                        tok_s[g, j, m * block : (m + 1) * block, :]
                        for j in range(h * shards // 2, (h + 1) * shards // 2)
                    ],
                    axis=0,
                )
                rows = jnp.dot(picks, tokens, preferred_element_type=jnp.float32)
                parts.append(rows.reshape(experts, -1, share))
            q = join_windows(parts[0], parts[1], windows, padded, 1).astype(jnp.bfloat16)
            at = g * tall + m * padded
            q_s[:, at : at + padded, :] = q
    for copy in u_copies:
        copy.wait()
    half = experts // 2
    for x in range(half):
        lane = x // blocks * 2 * rank
        both = jnp.concatenate(
            [u_refs[g, x % blocks, :, lane : lane + 2 * rank] for g in range(group_count)], axis=0
        )
        lb_ref[x] = adapter_scale * lax.dot_general(
            both[:, :rank], q_s[x], contract_first, preferred_element_type=jnp.float32
        )
        lb_ref[x + half] = adapter_scale * lax.dot_general(
            both[:, rank:], q_s[x + half], contract_first, preferred_element_type=jnp.float32
        )


def ring_order(count):
    return list(range(0, count, 2)) + list(range(1, count, 2))[::-1]


def local_by_tokens(
    output_gradient,
    chosen_expert_index,
    routing_gate_weight,
    hidden,
    frozen_down_weight,
    adapter_input_map,
    adapter_output_map,
):
    sources = lax.axis_size("expert")
    group_count = lax.axis_size("dp")
    micro, experts, slots, units = hidden.shape
    span, top = chosen_expert_index.shape
    width = output_gradient.shape[1]
    rank = adapter_input_map.shape[2]
    capacity = slots // sources
    block = span // micro
    padded = pad_rows(slots)
    share = width // group_count
    pairs = sources // 2
    chunks = 2 if group_count % 2 == 0 else 1
    part = width // chunks

    order = ring_order(pairs)
    place = {z: i for i, z in enumerate(order)}
    ring = [
        (2 * z + c, 2 * order[(place[z] + 1) % pairs] + c) for z in range(pairs) for c in range(2)
    ]
    swap = [(e, e ^ 1) for e in range(sources)]

    amap = jnp.swapaxes(adapter_input_map, 1, 2)
    u = jnp.einsum("mesk,exk->emsx", hidden, amap, preferred_element_type=jnp.float32)
    u = u.astype(jnp.bfloat16)
    u = jnp.pad(u, ((0, 0), (0, 0), (0, padded - slots), (0, 0))).reshape(
        2, experts // 2, micro * padded, rank
    )
    u = jnp.concatenate([u[0], u[1]], axis=-1)

    def shift_groups(array, by):
        return lax.ppermute(
            array, "dp", [(d, (d + by) % group_count) for d in range(group_count)]
        )

    def swap_partners(array):
        return lax.ppermute(array, "expert", swap)

    def exchange_columns(chosen):
        def columns(pieces, g):
            at = g * share % part
            return pieces[g * share // part][:, at : at + share]

        return jnp.stack(
            [jnp.stack([columns(pieces, g) for pieces in chosen]) for g in range(group_count)]
        )

    def across_groups(array):
        return lax.all_to_all(array, "dp", split_axis=0, concat_axis=0, tiled=True)

    others = range(1, group_count)
    names = jnp.concatenate(
        [chosen_expert_index.T.astype(jnp.bfloat16), routing_gate_weight.T], axis=0
    )
    lines = 2 * top * span // share
    names = jnp.tile(names.reshape(lines, share), (1, group_count))
    extra = -(-lines // 8) * 8
    sent = jnp.concatenate(
        [output_gradient, jnp.pad(names, ((0, extra - lines), (0, 0)))], axis=0
    )

    near, far = [[sent[:, c * part : (c + 1) * part] for c in range(chunks)]], []
    blocks = experts // 2 * 2 * rank // share
    packed = jnp.concatenate(
        [u[k * blocks : (k + 1) * blocks] for k in range(experts // 2 // blocks)], axis=-1
    ).reshape(blocks * micro * padded, share)
    early = jnp.stack(
        [
            jnp.concatenate([packed, sent[:, g * share : (g + 1) * share]], axis=0)
            for g in range(group_count)
        ]
    )
    early = across_groups(early)
    early_far = swap_partners(early[:, blocks * micro * padded :])
    for step in range(pairs - 1):
        if step > 1:
            tied = [
                lax.optimization_barrier((near[step][c], [shard[c] for shard in far]))
                for c in range(chunks)
            ]
            near[step] = [a for a, _ in tied]
            far = [[b[k] for _, b in tied] for k in range(len(far))]
        near.append([lax.ppermute(piece, "expert", ring) for piece in near[step]])
        far.append([swap_partners(piece) for piece in near[step]])
    far.append([swap_partners(piece) for piece in near[-1]])
    columns = exchange_columns(near[1:])
    columns, early, early_far, far[-2:] = lax.optimization_barrier(
        (columns, early, early_far, far[-2:])
    )
    columns = across_groups(columns)
    pieces = [piece for shard in near + far for piece in shard]

    vmem = pl.BlockSpec(memory_space=pltpu.VMEM)
    anywhere = pl.BlockSpec(memory_space=pl.ANY)
    part_a = jax.ShapeDtypeStruct((experts, rank, units // group_count), jnp.bfloat16)
    hidden_grad, routed, *parts = pl.pallas_call(
        functools.partial(expert_kernel, capacity, group_count, sources, chunks),
        out_shape=(
            jax.ShapeDtypeStruct(hidden.shape, jnp.bfloat16),
            jax.ShapeDtypeStruct((sources, top, span), jnp.float32),
        )
        + (part_a,) * group_count,
        in_specs=[anywhere] * (sources * chunks) + [vmem, vmem, anywhere, vmem, anywhere],
        out_specs=(vmem,) * 2 + (anywhere,) * group_count,
        scratch_shapes=[
            pltpu.VMEM((sources, span + extra, width), jnp.bfloat16),
            pltpu.VMEM((experts, units + rank, width), jnp.bfloat16),
            pltpu.VMEM((experts, micro * padded, width), jnp.bfloat16),
            pltpu.VMEM((experts, micro * padded, units + rank), jnp.float32),
            pltpu.VMEM((micro, 2, experts, sources // 2 * block), jnp.float32),
            pltpu.VMEM((experts, micro * padded, 1), jnp.float32),
            pltpu.VMEM((micro, 2, experts, sources // 2 * block), jnp.float32),
            pltpu.VMEM((group_count, experts, rank, units // group_count), jnp.bfloat16),
            pltpu.SemaphoreType.DMA((sources, chunks)),
            pltpu.SemaphoreType.DMA((experts,)),
            pltpu.SemaphoreType.DMA((experts,)),
            pltpu.SemaphoreType.DMA((group_count,)),
        ],
        compiler_params=pltpu.CompilerParams(vmem_limit_bytes=52 * 1024 * 1024),
        cost_estimate=pl.CostEstimate(
            flops=2 * experts * micro * padded * width * (units + rank + sources * block),
            bytes_accessed=2 * experts * width * (units + rank) + 2 * sources * span * width,
            transcendentals=0,
        ),
        name="expert_rows",
    )(*pieces, hidden, u, frozen_down_weight, amap, adapter_output_map)

    columns, parts, routed = lax.optimization_barrier((columns, parts, routed))
    swapped = swap_partners(columns)
    arrived = [shift_groups(parts[s], s) for s in others]
    home = lax.all_to_all(routed, "expert", split_axis=0, concat_axis=0, tiled=True)

    lora_b = pl.pallas_call(
        functools.partial(adapter_kernel, capacity, micro, span, top, group_count, sources),
        out_shape=jax.ShapeDtypeStruct((experts, rank, share), jnp.float32),
        in_specs=[anywhere] * 4,
        out_specs=vmem,
        scratch_shapes=[
            pltpu.VMEM((group_count, sources, span + extra, share), jnp.bfloat16),
            pltpu.VMEM((experts, group_count * micro * padded, share), jnp.bfloat16),
            pltpu.VMEM((group_count, blocks, micro * padded, share), jnp.bfloat16),
            pltpu.SemaphoreType.DMA((group_count, sources)),
            pltpu.SemaphoreType.DMA((group_count, blocks)),
        ],
        compiler_params=pltpu.CompilerParams(vmem_limit_bytes=58 * 1024 * 1024),
        cost_estimate=pl.CostEstimate(
            flops=2 * experts * micro * padded * share * group_count * (rank + sources * block),
            bytes_accessed=2 * group_count * sources * span * share + 4 * experts * rank * share,
            transcendentals=0,
        ),
        name="adapter_columns",
    )(early, early_far, columns, swapped)

    home, arrived, lora_b = lax.optimization_barrier((home, arrived, lora_b))
    router_grad = jnp.sum(home, axis=0).T
    lora_a = parts[0].astype(jnp.float32)
    for part in arrived:
        lora_a = lora_a + part.astype(jnp.float32)
    return (hidden_grad, router_grad, lora_a, lora_b)


def local(*arrays):
    sources, groups = lax.axis_size("expert"), lax.axis_size("dp")
    span, width = arrays[0].shape
    top, (micro, experts, slots, units) = arrays[1].shape[1], arrays[3].shape
    even = sources % 4 == 0 and experts % 2 == 0 and width % (128 * groups) == 0 and units % groups == 0
    rank = arrays[5].shape[2]
    packs = width // groups % (2 * rank) == 0 and experts * rank % (width // groups) == 0
    packs = packs and 2 * top * span % (width // groups) == 0 and (width // groups) % span == 0
    exact = experts * sources <= 256
    if even and packs and exact and sources * span <= micro * experts * slots:
        return local_by_tokens(*arrays)
    return local_by_slots(*arrays)


def solution(mesh):
    in_specs = (
        P(("dp", "expert"), None),
        P(("dp", "expert"), None),
        P(("dp", "expert"), None),
        P(None, ("dp", "expert"), None, None),
        P("expert", None, None),
        P("expert", None, None),
        P("expert", None, None),
    )
    out_specs = (
        P(None, ("dp", "expert"), None, None),
        P(("dp", "expert"), None),
        P("expert", None, "dp"),
        P("expert", None, "dp"),
    )
    return jax.shard_map(local, mesh=mesh, in_specs=in_specs, out_specs=out_specs, check_vma=False)
```

```python
import functools

import jax
import jax.numpy as jnp
from jax import lax
from jax.experimental import pallas as pl
from jax.experimental.pallas import tpu as pltpu
from jax.sharding import PartitionSpec as P

adapter_scale = 2.0


def slot_rows(id_rows, experts, per_device, sources, capacity):
    onehot = (id_rows[:, :, None] == jnp.arange(experts, dtype=jnp.int32)[None, None, :]).astype(
        jnp.int32
    )
    before = jnp.sum(jnp.cumsum(onehot, axis=1) * onehot, axis=2) - 1
    target_dev = id_rows // per_device
    target_slot = id_rows % per_device
    return (target_slot * sources + target_dev) * capacity + before


def pick_rows(source, indices):
    return source[indices]


def dispatch_buffers(grad_rows, weight_rows, send_rows, top_count, buffer_len):
    entry_count = send_rows.shape[1]
    token_count = grad_rows.shape[1]
    filler = jnp.full((buffer_len,), entry_count, jnp.int32)

    def invert(rows):
        return filler.at[rows].set(jnp.arange(entry_count, dtype=jnp.int32))

    table = jax.vmap(invert)(send_rows)
    padded_grad = jnp.concatenate(
        [grad_rows, jnp.zeros((grad_rows.shape[0], 1, grad_rows.shape[2]), grad_rows.dtype)], axis=1
    )
    padded_weight = jnp.concatenate(
        [weight_rows, jnp.zeros((weight_rows.shape[0], 1), weight_rows.dtype)], axis=1
    )
    token_pick = jnp.where(table < entry_count, table // top_count, token_count)
    sent_grad = jax.vmap(pick_rows)(padded_grad, token_pick)
    sent_weight = jax.vmap(pick_rows)(padded_weight, table)
    return (sent_grad, sent_weight)


def expert_rows_view(
    received_gradient,
    received_weight,
    retained_rows,
    frozen_down_weight,
    adapter_input_map,
    adapter_output_map,
):
    frozen_term = jnp.einsum(
        "mesd,efd->mesf", received_gradient, frozen_down_weight, preferred_element_type=jnp.float32
    )
    across_product = jnp.einsum(
        "hati,aki->hatk", received_gradient, adapter_output_map, preferred_element_type=jnp.float32
    ).astype(jnp.bfloat16)
    low_rank_state = jnp.einsum(
        "ptqv,tgv->ptqg", across_product, adapter_input_map, preferred_element_type=jnp.float32
    )
    capacity_slot_weight = received_weight.astype(jnp.float32)[..., None]
    hidden_state_gradient = (
        capacity_slot_weight * (frozen_term + adapter_scale * low_rank_state)
    ).astype(jnp.bfloat16)
    down_mapping = jnp.einsum(
        "lkgu,kup->lkgp", retained_rows, adapter_input_map, preferred_element_type=jnp.float32
    ).astype(jnp.bfloat16)
    complete_term = jnp.sum(frozen_term * retained_rows.astype(jnp.float32), axis=-1)
    adapter_term = jnp.einsum(
        "mesr,mesr->mes", down_mapping, across_product, preferred_element_type=jnp.float32
    )
    routing_rows = complete_term + adapter_scale * adapter_term
    scaled_gradient = (capacity_slot_weight * received_gradient).astype(jnp.bfloat16)
    scaled_across_product = (capacity_slot_weight * across_product.astype(jnp.float32)).astype(
        jnp.bfloat16
    )
    adapter_output_gradient = adapter_scale * jnp.einsum(
        "mesr,mesd->erd", down_mapping, scaled_gradient, preferred_element_type=jnp.float32
    )
    adapter_input_gradient = adapter_scale * jnp.einsum(
        "mesr,mesf->erf", scaled_across_product, retained_rows, preferred_element_type=jnp.float32
    )
    return (hidden_state_gradient, routing_rows, adapter_input_gradient, adapter_output_gradient)


def local_by_slots(
    output_gradient,
    chosen_expert_index,
    routing_gate_weight,
    hidden,
    frozen_down_weight,
    adapter_input_map,
    adapter_output_map,
):
    sources = lax.axis_size("expert")
    per_device = frozen_down_weight.shape[0]
    experts = per_device * sources
    micro_count = hidden.shape[0]
    slot_count = hidden.shape[2]
    capacity = slot_count // sources
    top_count = chosen_expert_index.shape[1]
    model_width = output_gradient.shape[1]
    buffer_len = experts * capacity
    grad_rows = output_gradient.reshape(micro_count, -1, model_width)
    id_rows = chosen_expert_index.reshape(micro_count, -1)
    weight_rows = routing_gate_weight.reshape(micro_count, -1)
    send_rows = slot_rows(id_rows, experts, per_device, sources, capacity)
    sent_grad, sent_weight = dispatch_buffers(
        grad_rows, weight_rows, send_rows, top_count, buffer_len
    )
    sent_grad = sent_grad.reshape(micro_count, per_device, sources, capacity, model_width)
    sent_weight = sent_weight.reshape(micro_count, per_device, sources, capacity)
    received_gradient, received_weight = (
        lax.all_to_all(sent_grad, "expert", split_axis=2, concat_axis=2, tiled=True),
        lax.all_to_all(sent_weight, "expert", split_axis=2, concat_axis=2, tiled=True),
    )
    received_gradient = received_gradient.reshape(micro_count, per_device, slot_count, model_width)
    received_weight = received_weight.reshape(micro_count, per_device, slot_count)
    hidden_grad, routing_rows, adapter_input_gradient, adapter_output_gradient = expert_rows_view(
        received_gradient,
        received_weight,
        hidden,
        frozen_down_weight,
        adapter_input_map,
        adapter_output_map,
    )
    router_home = lax.all_to_all(
        routing_rows.reshape(micro_count, per_device, sources, capacity),
        "expert",
        split_axis=2,
        concat_axis=2,
        tiled=True,
    )
    router_flat = router_home.reshape(micro_count, buffer_len)
    router_grad = jax.vmap(pick_rows)(router_flat, send_rows).reshape(-1, top_count)
    share_a, share_b = (
        lax.psum_scatter(adapter_input_gradient, "dp", scatter_dimension=2, tiled=True),
        lax.psum_scatter(adapter_output_gradient, "dp", scatter_dimension=2, tiled=True),
    )
    return (hidden_grad, router_grad, share_a, share_b)


def pad_rows(count):
    return -(-count // 16) * 16


def read_names(rows, span, top):
    wide = rows.astype(jnp.float32)
    per = wide.shape[1] // span
    lines = [
        wide[k // per : k // per + 1, (k % per) * span : (k % per + 1) * span]
        for k in range(2 * top)
    ]
    return lines[:top], lines[top:]


def slot_codes(names, first, capacity, experts, micro):
    sources = len(names)
    span = names[0][0][0].shape[1]
    block = span // micro
    number = lax.broadcasted_iota(jnp.int32, (experts, span), 0).astype(jnp.float32) + first
    from_row = lax.broadcasted_iota(jnp.int32, (span, span), 0)
    to_row = lax.broadcasted_iota(jnp.int32, (span, span), 1)
    earlier = jnp.where(
        (from_row // block == to_row // block) & (from_row < to_row), 1.0, 0.0
    ).astype(jnp.bfloat16)
    codes, gates = [], []
    for j in range(sources):
        named = jnp.zeros((experts, span), jnp.float32)
        gate = jnp.zeros((experts, span), jnp.float32)
        for name, weight in zip(*names[j]):
            hit = name == number
            named = jnp.where(hit, 1.0, named)
            gate = jnp.where(hit, weight, gate)
        before = jnp.dot(named.astype(jnp.bfloat16), earlier, preferred_element_type=jnp.float32)
        codes.append(jnp.where(named > 0.0, before + float(j * capacity), -1.0))
        gates.append(gate)

    def arrange(values):
        half = sources // 2
        return [
            [
                jnp.concatenate(
                    [c[:, m * block : (m + 1) * block] for c in values[h * half : (h + 1) * half]],
                    axis=1,
                )
                for h in range(2)
            ]
            for m in range(micro)
        ]

    return arrange(codes), arrange(gates)


def slot_windows(slots):
    half = slots // 2
    return [(h * half // 8 * 8, -(-(h + 1) * half // 8) * 8) for h in range(2)]


def slot_iota(window, lanes):
    shape = (window[1] - window[0], lanes)
    return lax.broadcasted_iota(jnp.int32, shape, 0).astype(jnp.float32) + float(window[0])


def join_windows(first_part, second_part, windows, padded, axis):
    (_, end), (start, last) = windows

    def rows(values, low, high):
        return lax.slice_in_dim(values, low, high, axis=axis)

    parts = [rows(first_part, 0, start)]
    if end > start:
        parts.append(rows(first_part, start, end) + rows(second_part, 0, end - start))
    parts.append(rows(second_part, end - start, last - start))
    if padded > last:
        shape = list(first_part.shape)
        shape[axis] = padded - last
        parts.append(jnp.zeros(shape, first_part.dtype))
    return jnp.concatenate(parts, axis=axis)


contract_last = (((1,), (1,)), ((), ()))
contract_first = (((0,), (0,)), ((), ()))


def shard_owner(index, sources):
    pairs = sources // 2
    me = lax.axis_index("expert")
    column, core = me // 2, lax.rem(me, 2)
    place = jnp.where(lax.rem(column, 2) == 0, column // 2, pairs - 1 - column // 2)
    place = lax.rem(place - index % pairs + pairs, pairs)
    column = jnp.where(2 * place < pairs, 2 * place, 2 * (pairs - 1 - place) + 1)
    return 2 * column + (core if index < pairs else 1 - core)


def payload_kernel(share, dy_ref, index_ref, gate_ref, *outs):
    top, span = index_ref.shape
    part = outs[0].shape[1]
    per = share // span
    names, gates = index_ref[...].astype(jnp.float32), gate_ref[...].astype(jnp.float32)
    lines = [names[k : k + 1] for k in range(top)] + [gates[k : k + 1] for k in range(top)]
    rows = [jnp.concatenate(lines[k : k + per], axis=1) for k in range(0, 2 * top, per)]
    spare = outs[0].shape[0] - span - len(rows)
    if spare:
        rows.append(jnp.zeros((spare, share), jnp.float32))
    below = jnp.concatenate(rows, axis=0).astype(jnp.bfloat16)
    for c, out in enumerate(outs):
        out[:span] = dy_ref[:, c * part : (c + 1) * part]
        for at in range(0, part, share):
            out[span:, at : at + share] = below


def expert_kernel(capacity, group_count, shards, chunks, *refs):
    token_refs = refs[: shards * chunks]
    refs = refs[shards * chunks :]
    hidden_ref, u_ref, weight_hbm, amap_ref, bmap_hbm, hg_ref, rk_ref = refs[:7]
    la_outs = refs[7 : 7 + group_count]
    scratch = refs[7 + group_count :]
    dy_s, wb_s, rows_s, y_s, code_s, gate_s, back_s, la_s = scratch[:8]
    dy_sem, w_sem, b_sem, la_sem = scratch[8:]
    top, span = rk_ref.shape[1:]
    micro, experts, slots, units = hidden_ref.shape
    rank = amap_ref.shape[1]
    width = dy_s.shape[2]
    block = span // micro
    padded = rows_s.shape[1] // micro
    first = (lax.axis_index("expert") * experts).astype(jnp.float32)

    part = width // chunks
    owners = [shard_owner(i, shards) for i in range(shards)]
    token_copies = [
        pltpu.make_async_copy(
            token_refs[i * chunks + c],
            dy_s.at[owners[i], :, pl.ds(c * part, part)],
            dy_sem.at[i, c],
        )
        for i in range(shards)
        for c in range(chunks)
    ]
    for copy in token_copies:
        copy.start()

    def weight_copies(x, slot):
        return (
            pltpu.make_async_copy(weight_hbm.at[x], wb_s.at[slot, pl.ds(0, units)], w_sem.at[x]),
            pltpu.make_async_copy(bmap_hbm.at[x], wb_s.at[slot, pl.ds(units, rank)], b_sem.at[x]),
        )

    half = experts // 2
    batch = 2 if half % 2 == 0 else 1
    groups = half // batch

    def members(step):
        at = [step * batch + i for i in range(batch)]
        picked = [(p, p, slice(0, rank)) for p in at]
        return picked + [(p + half, p, slice(rank, 2 * rank)) for p in at]

    def slot_at(step, i):
        return lax.rem(step, wb_s.shape[0] // (2 * batch)) * 2 * batch + i

    def request_weights(step):
        for i, (x, _, _) in enumerate(members(step)):
            for copy in weight_copies(x, slot_at(step, i)):
                copy.start()

    for step in range(min(2, groups)):
        request_weights(step)

    for copy in token_copies:
        copy.wait()
    names = [
        read_names(dy_s[i, span:, width - width // group_count :], span, top) for i in range(shards)
    ]
    codes, gates = slot_codes(names, first, capacity, experts, micro)
    windows = slot_windows(slots)
    lanes_of = shards // 2 * block
    slot_of = [slot_iota(window, lanes_of) for window in windows]
    picks = []
    for m in range(micro):
        chosen = [[], []]
        for h in range(2):
            code_s[m, h] = codes[m][h]
        for x in range(experts):
            sums = []
            for h in range(2):
                hit = codes[m][h][x : x + 1, :] == slot_of[h]
                chosen[h].append(jnp.where(hit, 1.0, 0.0))
                sums.append(
                    jnp.sum(
                        jnp.where(hit, gates[m][h][x : x + 1, :], 0.0), axis=1, keepdims=True
                    )
                )
            gate_s[x, m * padded : (m + 1) * padded, :] = join_windows(
                sums[0], sums[1], windows, padded, 0
            )
        picks.append([jnp.concatenate(c, axis=0).astype(jnp.bfloat16) for c in chosen])

    tile = 512 if width % 512 == 0 else width
    for m in range(micro):
        for n in range(width // tile):
            cols = slice(n * tile, (n + 1) * tile)
            parts = []
            for h in range(2):
                tokens = jnp.concatenate(
                    [
                        dy_s[j, m * block : (m + 1) * block, cols]
                        for j in range(h * shards // 2, (h + 1) * shards // 2)
                    ],
                    axis=0,
                )
                rows = jnp.dot(picks[m][h], tokens, preferred_element_type=jnp.float32)
                parts.append(rows.reshape(experts, -1, tile))
            rows_s[:, m * padded : (m + 1) * padded, cols] = join_windows(
                parts[0], parts[1], windows, padded, 1
            ).astype(jnp.bfloat16)

    def main_products(step):
        xs = [x for x, _, _ in members(step)]
        for i, x in enumerate(xs):
            for copy in weight_copies(x, slot_at(step, i)):
                copy.wait()

        @pl.when(step + 2 < groups)
        def _():
            request_weights(step + 2)

        return [
            lax.dot_general(
                rows_s[x],
                wb_s[slot_at(step, i)],
                contract_last,
                preferred_element_type=jnp.float32,
            )
            for i, x in enumerate(xs)
        ]

    def keep_products(step, products):
        for (x, _, _), product in zip(members(step), products):
            y_s[x] = product

    share = units // group_count
    filler = jnp.zeros((padded - slots, units), jnp.float32)

    def small_steps(step):
        picked = members(step)
        xs = [x for x, _, _ in picked]
        mains = [y_s[x, :, :units] for x in xs]
        vs = [y_s[x, :, units:].astype(jnp.bfloat16) for x in xs]
        lows = [
            jnp.dot(v, amap_ref[x], preferred_element_type=jnp.float32) for v, x in zip(vs, xs)
        ]
        gates_x = [gate_s[x] for x in xs]
        wide = [
            jnp.concatenate(
                [
                    part
                    for m in range(micro)
                    for part in (hidden_ref[m, x].astype(jnp.float32), filler)
                ],
                axis=0,
            )
            for x in xs
        ]
        v_wide = [v.astype(jnp.float32) for v in vs]
        ws = [(gate * v).astype(jnp.bfloat16) for gate, v in zip(gates_x, v_wide)]
        las = [
            lax.dot_general(
                w, held.astype(jnp.bfloat16), contract_first, preferred_element_type=jnp.float32
            )
            for w, held in zip(ws, wide)
        ]
        routed = [
            jnp.sum(main * held, axis=1, keepdims=True)
            + adapter_scale
            * jnp.sum(u_ref[p, :, lanes].astype(jnp.float32) * v, axis=1, keepdims=True)
            for main, held, v, (_, p, lanes) in zip(mains, wide, v_wide, picked)
        ]
        grads = [
            (gate * (main + adapter_scale * low)).astype(jnp.bfloat16)
            for gate, main, low in zip(gates_x, mains, lows)
        ]
        for x, grad, la, back in zip(xs, grads, las, routed):
            for m in range(micro):
                hg_ref[m, x] = grad[m * padded : m * padded + slots]
                for h, (low, high) in enumerate(windows):
                    hit = code_s[m, h, pl.ds(x, 1), :] == slot_of[h]
                    rows = back[m * padded + low : m * padded + high]
                    back_s[m, h, pl.ds(x, 1), :] = jnp.sum(
                        jnp.where(hit, rows, 0.0), axis=0, keepdims=True
                    )
            for k in range(group_count):
                la_s[k, x] = (adapter_scale * la[:, k * share : (k + 1) * share]).astype(
                    la_s.dtype
                )

    def both_steps(step, carry):
        products = main_products(step)
        small_steps(step - 1)
        keep_products(step, products)
        return carry

    keep_products(0, main_products(0))
    lax.fori_loop(1, groups, both_steps, 0)
    small_steps(groups - 1)

    group = lax.axis_index("dp")
    la_copies = [
        pltpu.make_async_copy(
            la_s.at[lax.rem(group + s, group_count)], la_outs[s], la_sem.at[s]
        )
        for s in range(group_count)
    ]
    for copy in la_copies:
        copy.start()
    number = lax.broadcasted_iota(jnp.int32, (experts, span), 0).astype(jnp.float32) + first
    for j in range(shards):
        h, k = j // (shards // 2), j % (shards // 2)
        back = jnp.concatenate(
            [back_s[m, h, :, k * block : (k + 1) * block] for m in range(micro)], axis=1
        )
        found = [
            jnp.sum(jnp.where(name == number, back, 0.0), axis=0, keepdims=True)
            for name in names[j][0]
        ]
        rk_ref[j] = jnp.concatenate(found, axis=0)
    for copy in la_copies:
        copy.wait()


def adapter_kernel(capacity, micro, span, top, group_count, shards, *refs):
    pairs = shards // 2
    early_ref, early_far_ref, near_ref, far_ref = refs[:4]
    lb_hbm, tok_s, q_s, u_refs, lb_ref, sem, u_sem, lb_sem = refs[4:]
    experts, rank, share = lb_ref.shape
    lb_copies = [
        pltpu.make_async_copy(lb_ref.at[x], lb_hbm.at[x], lb_sem.at[x]) for x in range(experts)
    ]
    blocks, tall = u_refs.shape[1:3]
    padded = tall // micro
    block = span // micro
    first = (lax.axis_index("expert") * experts).astype(jnp.float32)
    group = lax.axis_index("dp")
    owners = [shard_owner(i, shards) for i in range(shards)]
    copies, u_copies = [], []
    for g in range(group_count):
        home = lax.rem(group - g + group_count, group_count)
        for i in range(shards):
            if i % pairs:
                source = (far_ref if i >= pairs else near_ref).at[home, i % pairs - 1]
            elif i:
                source = early_far_ref.at[home]
            else:
                source = early_ref.at[home, pl.ds(blocks * tall, tok_s.shape[2])]
            copies.append(pltpu.make_async_copy(source, tok_s.at[g, owners[i]], sem.at[g, i]))
        for k in range(blocks):
            source = early_ref.at[home, pl.ds(k * tall, tall)]
            u_copies.append(pltpu.make_async_copy(source, u_refs.at[g, k], u_sem.at[g, k]))
    for copy in copies + u_copies:
        copy.start()
    slots = capacity * shards
    windows = slot_windows(slots)
    slot_of = [slot_iota(window, shards // 2 * block) for window in windows]
    for g in range(group_count):
        for i in range(shards):
            copies[g * shards + i].wait()
        names = [read_names(tok_s[g, i, span:, :], span, top) for i in range(shards)]
        codes, gates = slot_codes(names, first, capacity, experts, micro)
        for m in range(micro):
            parts = []
            for h in range(2):
                picks = jnp.concatenate(
                    [
                        jnp.where(
                            codes[m][h][x : x + 1, :] == slot_of[h],
                            gates[m][h][x : x + 1, :],
                            0.0,
                        )
                        for x in range(experts)
                    ],
                    axis=0,
                ).astype(jnp.bfloat16)
                tokens = jnp.concatenate(
                    [
                        tok_s[g, j, m * block : (m + 1) * block, :]
                        for j in range(h * shards // 2, (h + 1) * shards // 2)
                    ],
                    axis=0,
                )
                rows = jnp.dot(picks, tokens, preferred_element_type=jnp.float32)
                parts.append(rows.reshape(experts, -1, share))
            q = join_windows(parts[0], parts[1], windows, padded, 1).astype(jnp.bfloat16)
            at = g * tall + m * padded
            q_s[:, at : at + padded, :] = q
    for copy in u_copies:
        copy.wait()
    half = experts // 2
    for x in range(half):
        lane = x // blocks * 2 * rank
        both = jnp.concatenate(
            [u_refs[g, x % blocks, :, lane : lane + 2 * rank] for g in range(group_count)], axis=0
        )
        lb_ref[x] = adapter_scale * lax.dot_general(
            both[:, :rank], q_s[x], contract_first, preferred_element_type=jnp.float32
        )
        lb_ref[x + half] = adapter_scale * lax.dot_general(
            both[:, rank:], q_s[x + half], contract_first, preferred_element_type=jnp.float32
        )
        lb_copies[x].start()
        lb_copies[x + half].start()
    for copy in lb_copies:
        copy.wait()


def ring_order(count):
    return list(range(0, count, 2)) + list(range(1, count, 2))[::-1]


def local_by_tokens(
    output_gradient,
    chosen_expert_index,
    routing_gate_weight,
    hidden,
    frozen_down_weight,
    adapter_input_map,
    adapter_output_map,
):
    sources = lax.axis_size("expert")
    group_count = lax.axis_size("dp")
    micro, experts, slots, units = hidden.shape
    span, top = chosen_expert_index.shape
    width = output_gradient.shape[1]
    rank = adapter_input_map.shape[2]
    capacity = slots // sources
    block = span // micro
    padded = pad_rows(slots)
    share = width // group_count
    pairs = sources // 2
    chunks = 2 if group_count % 2 == 0 else 1
    part = width // chunks

    order = ring_order(pairs)
    place = {z: i for i, z in enumerate(order)}
    ring = [
        (2 * z + c, 2 * order[(place[z] + 1) % pairs] + c) for z in range(pairs) for c in range(2)
    ]
    swap = [(e, e ^ 1) for e in range(sources)]

    amap = jnp.swapaxes(adapter_input_map, 1, 2)
    u = jnp.einsum("mesk,exk->emsx", hidden, amap, preferred_element_type=jnp.float32)
    u = u.astype(jnp.bfloat16)
    u = jnp.pad(u, ((0, 0), (0, 0), (0, padded - slots), (0, 0))).reshape(
        2, experts // 2, micro * padded, rank
    )
    u = jnp.concatenate([u[0], u[1]], axis=-1)

    def shift_groups(array, by):
        return lax.ppermute(
            array, "dp", [(d, (d + by) % group_count) for d in range(group_count)]
        )

    def swap_partners(array):
        return lax.ppermute(array, "expert", swap)

    def exchange_columns(chosen):
        def columns(pieces, g):
            at = g * share % part
            return pieces[g * share // part][:, at : at + share]

        return jnp.stack(
            [jnp.stack([columns(pieces, g) for pieces in chosen]) for g in range(group_count)]
        )

    def across_groups(array):
        return lax.all_to_all(array, "dp", split_axis=0, concat_axis=0, tiled=True)

    others = range(1, group_count)
    lines = 2 * top * span // share
    extra = -(-lines // 8) * 8
    vmem = pl.BlockSpec(memory_space=pltpu.VMEM)
    sent = pl.pallas_call(
        functools.partial(payload_kernel, share),
        out_shape=[jax.ShapeDtypeStruct((span + extra, part), jnp.bfloat16)] * chunks,
        in_specs=[vmem] * 3,
        out_specs=[vmem] * chunks,
        compiler_params=pltpu.CompilerParams(vmem_limit_bytes=58 * 1024 * 1024),
        name="ring_payload",
    )(output_gradient, chosen_expert_index.T, routing_gate_weight.T)

    near, far = [list(sent)], []
    blocks = experts // 2 * 2 * rank // share
    packed = jnp.concatenate(
        [u[k * blocks : (k + 1) * blocks] for k in range(experts // 2 // blocks)], axis=-1
    ).reshape(blocks * micro * padded, share)
    early = jnp.stack(
        [
            jnp.concatenate(
                [packed, sent[g * share // part][:, g * share % part :][:, :share]], axis=0
            )
            for g in range(group_count)
        ]
    )
    early = across_groups(early)
    early_far = swap_partners(early[:, blocks * micro * padded :])
    for step in range(pairs - 1):
        if step > 1:
            tied = [
                lax.optimization_barrier((near[step][c], [shard[c] for shard in far]))
                for c in range(chunks)
            ]
            near[step] = [a for a, _ in tied]
            far = [[b[k] for _, b in tied] for k in range(len(far))]
        near.append([lax.ppermute(piece, "expert", ring) for piece in near[step]])
        far.append([swap_partners(piece) for piece in near[step]])
    far.append([swap_partners(piece) for piece in near[-1]])
    columns = exchange_columns(near[1:])
    columns, early, early_far, far[-2:] = lax.optimization_barrier(
        (columns, early, early_far, far[-2:])
    )
    columns = across_groups(columns)
    pieces = [piece for shard in near + far for piece in shard]

    anywhere = pl.BlockSpec(memory_space=pl.ANY)
    kept = 3 * (4 if experts % 4 == 0 else 2)
    part_a = jax.ShapeDtypeStruct((experts, rank, units // group_count), jnp.bfloat16)
    hidden_grad, routed, *parts = pl.pallas_call(
        functools.partial(expert_kernel, capacity, group_count, sources, chunks),
        out_shape=(
            jax.ShapeDtypeStruct(hidden.shape, jnp.bfloat16),
            jax.ShapeDtypeStruct((sources, top, span), jnp.float32),
        )
        + (part_a,) * group_count,
        in_specs=[anywhere] * (sources * chunks) + [vmem, vmem, anywhere, vmem, anywhere],
        out_specs=(vmem,) * 2 + (anywhere,) * group_count,
        scratch_shapes=[
            pltpu.VMEM((sources, span + extra, width), jnp.bfloat16),
            pltpu.VMEM((min(experts, kept), units + rank, width), jnp.bfloat16),
            pltpu.VMEM((experts, micro * padded, width), jnp.bfloat16),
            pltpu.VMEM((experts, micro * padded, units + rank), jnp.float32),
            pltpu.VMEM((micro, 2, experts, sources // 2 * block), jnp.float32),
            pltpu.VMEM((experts, micro * padded, 1), jnp.float32),
            pltpu.VMEM((micro, 2, experts, sources // 2 * block), jnp.float32),
            pltpu.VMEM((group_count, experts, rank, units // group_count), jnp.bfloat16),
            pltpu.SemaphoreType.DMA((sources, chunks)),
            pltpu.SemaphoreType.DMA((experts,)),
            pltpu.SemaphoreType.DMA((experts,)),
            pltpu.SemaphoreType.DMA((group_count,)),
        ],
        compiler_params=pltpu.CompilerParams(vmem_limit_bytes=45 * 1024 * 1024),
        cost_estimate=pl.CostEstimate(
            flops=2 * experts * micro * padded * width * (units + rank + sources * block),
            bytes_accessed=2 * experts * width * (units + rank) + 2 * sources * span * width,
            transcendentals=0,
        ),
        name="expert_rows",
    )(*pieces, hidden, u, frozen_down_weight, amap, adapter_output_map)

    columns, parts, routed = lax.optimization_barrier((columns, parts, routed))
    swapped = swap_partners(columns)
    arrived = [shift_groups(parts[s], s) for s in others]
    swapped, routed = lax.optimization_barrier((swapped, routed))
    home = lax.all_to_all(routed, "expert", split_axis=0, concat_axis=0, tiled=True)

    lora_b = pl.pallas_call(
        functools.partial(adapter_kernel, capacity, micro, span, top, group_count, sources),
        out_shape=jax.ShapeDtypeStruct((experts, rank, share), jnp.float32),
        in_specs=[anywhere] * 4,
        out_specs=anywhere,
        scratch_shapes=[
            pltpu.VMEM((group_count, sources, span + extra, share), jnp.bfloat16),
            pltpu.VMEM((experts, group_count * micro * padded, share), jnp.bfloat16),
            pltpu.VMEM((group_count, blocks, micro * padded, share), jnp.bfloat16),
            pltpu.VMEM((experts, rank, share), jnp.float32),
            pltpu.SemaphoreType.DMA((group_count, sources)),
            pltpu.SemaphoreType.DMA((group_count, blocks)),
            pltpu.SemaphoreType.DMA((experts,)),
        ],
        compiler_params=pltpu.CompilerParams(vmem_limit_bytes=58 * 1024 * 1024),
        cost_estimate=pl.CostEstimate(
            flops=2 * experts * micro * padded * share * group_count * (rank + sources * block),
            bytes_accessed=2 * group_count * sources * span * share + 4 * experts * rank * share,
            transcendentals=0,
        ),
        name="adapter_columns",
    )(early, early_far, columns, swapped)

    home, arrived, lora_b = lax.optimization_barrier((home, arrived, lora_b))
    router_grad = jnp.sum(home, axis=0).T
    lora_a = parts[0].astype(jnp.float32)
    for part in arrived:
        lora_a = lora_a + part.astype(jnp.float32)
    return (hidden_grad, router_grad, lora_a, lora_b)


def local(*arrays):
    sources, groups = lax.axis_size("expert"), lax.axis_size("dp")
    span, width = arrays[0].shape
    top, (micro, experts, slots, units) = arrays[1].shape[1], arrays[3].shape
    even = sources % 4 == 0 and experts % 2 == 0 and width % (128 * groups) == 0 and units % groups == 0
    rank = arrays[5].shape[2]
    packs = width // groups % (2 * rank) == 0 and experts * rank % (width // groups) == 0
    packs = packs and 2 * top * span % (width // groups) == 0 and (width // groups) % span == 0
    exact = experts * sources <= 256
    if even and packs and exact and sources * span <= micro * experts * slots:
        return local_by_tokens(*arrays)
    return local_by_slots(*arrays)


def solution(mesh):
    in_specs = (
        P(("dp", "expert"), None),
        P(("dp", "expert"), None),
        P(("dp", "expert"), None),
        P(None, ("dp", "expert"), None, None),
        P("expert", None, None),
        P("expert", None, None),
        P("expert", None, None),
    )
    out_specs = (
        P(None, ("dp", "expert"), None, None),
        P(("dp", "expert"), None),
        P("expert", None, "dp"),
        P("expert", None, "dp"),
    )
    return jax.shard_map(local, mesh=mesh, in_specs=in_specs, out_specs=out_specs, check_vma=False)
```

```python
import functools

import jax
import jax.numpy as jnp
from jax import lax
from jax.experimental import pallas as pl
from jax.experimental.pallas import tpu as pltpu
from jax.sharding import PartitionSpec as P

adapter_scale = 2.0


def slot_rows(id_rows, experts, per_device, sources, capacity):
    onehot = (id_rows[:, :, None] == jnp.arange(experts, dtype=jnp.int32)[None, None, :]).astype(
        jnp.int32
    )
    before = jnp.sum(jnp.cumsum(onehot, axis=1) * onehot, axis=2) - 1
    target_dev = id_rows // per_device
    target_slot = id_rows % per_device
    return (target_slot * sources + target_dev) * capacity + before


def pick_rows(source, indices):
    return source[indices]


def dispatch_buffers(grad_rows, weight_rows, send_rows, top_count, buffer_len):
    entry_count = send_rows.shape[1]
    token_count = grad_rows.shape[1]
    filler = jnp.full((buffer_len,), entry_count, jnp.int32)

    def invert(rows):
        return filler.at[rows].set(jnp.arange(entry_count, dtype=jnp.int32))

    table = jax.vmap(invert)(send_rows)
    padded_grad = jnp.concatenate(
        [grad_rows, jnp.zeros((grad_rows.shape[0], 1, grad_rows.shape[2]), grad_rows.dtype)], axis=1
    )
    padded_weight = jnp.concatenate(
        [weight_rows, jnp.zeros((weight_rows.shape[0], 1), weight_rows.dtype)], axis=1
    )
    token_pick = jnp.where(table < entry_count, table // top_count, token_count)
    sent_grad = jax.vmap(pick_rows)(padded_grad, token_pick)
    sent_weight = jax.vmap(pick_rows)(padded_weight, table)
    return (sent_grad, sent_weight)


def expert_rows_view(
    received_gradient,
    received_weight,
    retained_rows,
    frozen_down_weight,
    adapter_input_map,
    adapter_output_map,
):
    frozen_term = jnp.einsum(
        "mesd,efd->mesf", received_gradient, frozen_down_weight, preferred_element_type=jnp.float32
    )
    across_product = jnp.einsum(
        "hati,aki->hatk", received_gradient, adapter_output_map, preferred_element_type=jnp.float32
    ).astype(jnp.bfloat16)
    low_rank_state = jnp.einsum(
        "ptqv,tgv->ptqg", across_product, adapter_input_map, preferred_element_type=jnp.float32
    )
    capacity_slot_weight = received_weight.astype(jnp.float32)[..., None]
    hidden_state_gradient = (
        capacity_slot_weight * (frozen_term + adapter_scale * low_rank_state)
    ).astype(jnp.bfloat16)
    down_mapping = jnp.einsum(
        "lkgu,kup->lkgp", retained_rows, adapter_input_map, preferred_element_type=jnp.float32
    ).astype(jnp.bfloat16)
    complete_term = jnp.sum(frozen_term * retained_rows.astype(jnp.float32), axis=-1)
    adapter_term = jnp.einsum(
        "mesr,mesr->mes", down_mapping, across_product, preferred_element_type=jnp.float32
    )
    routing_rows = complete_term + adapter_scale * adapter_term
    scaled_gradient = (capacity_slot_weight * received_gradient).astype(jnp.bfloat16)
    scaled_across_product = (capacity_slot_weight * across_product.astype(jnp.float32)).astype(
        jnp.bfloat16
    )
    adapter_output_gradient = adapter_scale * jnp.einsum(
        "mesr,mesd->erd", down_mapping, scaled_gradient, preferred_element_type=jnp.float32
    )
    adapter_input_gradient = adapter_scale * jnp.einsum(
        "mesr,mesf->erf", scaled_across_product, retained_rows, preferred_element_type=jnp.float32
    )
    return (hidden_state_gradient, routing_rows, adapter_input_gradient, adapter_output_gradient)


def local_by_slots(
    output_gradient,
    chosen_expert_index,
    routing_gate_weight,
    hidden,
    frozen_down_weight,
    adapter_input_map,
    adapter_output_map,
):
    sources = lax.axis_size("expert")
    per_device = frozen_down_weight.shape[0]
    experts = per_device * sources
    micro_count = hidden.shape[0]
    slot_count = hidden.shape[2]
    capacity = slot_count // sources
    top_count = chosen_expert_index.shape[1]
    model_width = output_gradient.shape[1]
    buffer_len = experts * capacity
    grad_rows = output_gradient.reshape(micro_count, -1, model_width)
    id_rows = chosen_expert_index.reshape(micro_count, -1)
    weight_rows = routing_gate_weight.reshape(micro_count, -1)
    send_rows = slot_rows(id_rows, experts, per_device, sources, capacity)
    sent_grad, sent_weight = dispatch_buffers(
        grad_rows, weight_rows, send_rows, top_count, buffer_len
    )
    sent_grad = sent_grad.reshape(micro_count, per_device, sources, capacity, model_width)
    sent_weight = sent_weight.reshape(micro_count, per_device, sources, capacity)
    received_gradient, received_weight = (
        lax.all_to_all(sent_grad, "expert", split_axis=2, concat_axis=2, tiled=True),
        lax.all_to_all(sent_weight, "expert", split_axis=2, concat_axis=2, tiled=True),
    )
    received_gradient = received_gradient.reshape(micro_count, per_device, slot_count, model_width)
    received_weight = received_weight.reshape(micro_count, per_device, slot_count)
    hidden_grad, routing_rows, adapter_input_gradient, adapter_output_gradient = expert_rows_view(
        received_gradient,
        received_weight,
        hidden,
        frozen_down_weight,
        adapter_input_map,
        adapter_output_map,
    )
    router_home = lax.all_to_all(
        routing_rows.reshape(micro_count, per_device, sources, capacity),
        "expert",
        split_axis=2,
        concat_axis=2,
        tiled=True,
    )
    router_flat = router_home.reshape(micro_count, buffer_len)
    router_grad = jax.vmap(pick_rows)(router_flat, send_rows).reshape(-1, top_count)
    share_a, share_b = (
        lax.psum_scatter(adapter_input_gradient, "dp", scatter_dimension=2, tiled=True),
        lax.psum_scatter(adapter_output_gradient, "dp", scatter_dimension=2, tiled=True),
    )
    return (hidden_grad, router_grad, share_a, share_b)


def pad_rows(count):
    return -(-count // 16) * 16


def read_names(rows, span, top):
    wide = rows.astype(jnp.float32)
    per = wide.shape[1] // span
    lines = [
        wide[k // per : k // per + 1, (k % per) * span : (k % per + 1) * span]
        for k in range(2 * top)
    ]
    return lines[:top], lines[top:]


def slot_codes(names, first, capacity, experts, micro):
    sources = len(names)
    span = names[0][0][0].shape[1]
    block = span // micro
    number = lax.broadcasted_iota(jnp.int32, (experts, span), 0).astype(jnp.float32) + first
    from_row = lax.broadcasted_iota(jnp.int32, (span, span), 0)
    to_row = lax.broadcasted_iota(jnp.int32, (span, span), 1)
    earlier = jnp.where(
        (from_row // block == to_row // block) & (from_row < to_row), 1.0, 0.0
    ).astype(jnp.bfloat16)
    codes, gates = [], []
    for j in range(sources):
        named = jnp.zeros((experts, span), jnp.float32)
        gate = jnp.zeros((experts, span), jnp.float32)
        for name, weight in zip(*names[j]):
            hit = name == number
            named = jnp.where(hit, 1.0, named)
            gate = jnp.where(hit, weight, gate)
        before = jnp.dot(named.astype(jnp.bfloat16), earlier, preferred_element_type=jnp.float32)
        codes.append(jnp.where(named > 0.0, before + float(j * capacity), -1.0))
        gates.append(gate)

    def arrange(values):
        half = sources // 2
        return [
            [
                jnp.concatenate(
                    [c[:, m * block : (m + 1) * block] for c in values[h * half : (h + 1) * half]],
                    axis=1,
                )
                for h in range(2)
            ]
            for m in range(micro)
        ]

    return arrange(codes), arrange(gates)


def slot_windows(slots):
    half = slots // 2
    return [(h * half // 8 * 8, -(-(h + 1) * half // 8) * 8) for h in range(2)]


def slot_iota(window, lanes):
    shape = (window[1] - window[0], lanes)
    return lax.broadcasted_iota(jnp.int32, shape, 0).astype(jnp.float32) + float(window[0])


def join_windows(first_part, second_part, windows, padded, axis):
    (_, end), (start, last) = windows

    def rows(values, low, high):
        return lax.slice_in_dim(values, low, high, axis=axis)

    parts = [rows(first_part, 0, start)]
    if end > start:
        parts.append(rows(first_part, start, end) + rows(second_part, 0, end - start))
    parts.append(rows(second_part, end - start, last - start))
    if padded > last:
        shape = list(first_part.shape)
        shape[axis] = padded - last
        parts.append(jnp.zeros(shape, first_part.dtype))
    return jnp.concatenate(parts, axis=axis)


contract_last = (((1,), (1,)), ((), ()))
contract_first = (((0,), (0,)), ((), ()))


def shard_owner(index, sources):
    pairs = sources // 2
    me = lax.axis_index("expert")
    column, core = me // 2, lax.rem(me, 2)
    place = jnp.where(lax.rem(column, 2) == 0, column // 2, pairs - 1 - column // 2)
    place = lax.rem(place - index % pairs + pairs, pairs)
    column = jnp.where(2 * place < pairs, 2 * place, 2 * (pairs - 1 - place) + 1)
    return 2 * column + (core if index < pairs else 1 - core)


def payload_kernel(share, dy_ref, index_ref, gate_ref, *outs):
    top, span = index_ref.shape
    part = outs[0].shape[1]
    per = share // span
    names, gates = index_ref[...].astype(jnp.float32), gate_ref[...].astype(jnp.float32)
    lines = [names[k : k + 1] for k in range(top)] + [gates[k : k + 1] for k in range(top)]
    rows = [jnp.concatenate(lines[k : k + per], axis=1) for k in range(0, 2 * top, per)]
    spare = outs[0].shape[0] - span - len(rows)
    if spare:
        rows.append(jnp.zeros((spare, share), jnp.float32))
    below = jnp.concatenate(rows, axis=0).astype(jnp.bfloat16)
    for c, out in enumerate(outs):
        out[:span] = dy_ref[:, c * part : (c + 1) * part]
        for at in range(0, part, share):
            out[span:, at : at + share] = below


def expert_kernel(capacity, group_count, shards, chunks, *refs):
    token_refs = refs[: shards * chunks]
    refs = refs[shards * chunks :]
    hidden_hbm, u_hbm, weight_hbm, amap_hbm, bmap_hbm, hg_ref, rk_ref = refs[:7]
    la_outs = refs[7 : 7 + group_count]
    scratch = refs[7 + group_count :]
    dy_s, wb_s, rows_s, y_s, code_s, gate_s, back_s, la_s = scratch[:8]
    hidden_ref, u_ref, amap_ref, dy_sem, w_sem, b_sem, la_sem, in_sem = scratch[8:]
    top, span = rk_ref.shape[1:]
    micro, experts, slots, units = hidden_ref.shape
    rank = amap_ref.shape[1]
    width = dy_s.shape[2]
    block = span // micro
    padded = rows_s.shape[1] // micro
    first = (lax.axis_index("expert") * experts).astype(jnp.float32)

    part = width // chunks
    owners = [shard_owner(i, shards) for i in range(shards)]
    token_copies = [
        pltpu.make_async_copy(
            token_refs[i * chunks + c],
            dy_s.at[owners[i], :, pl.ds(c * part, part)],
            dy_sem.at[i, c],
        )
        for i in range(shards)
        for c in range(chunks)
    ]
    for copy in token_copies:
        copy.start()

    def weight_copies(x, slot):
        return (
            pltpu.make_async_copy(weight_hbm.at[x], wb_s.at[slot, pl.ds(0, units)], w_sem.at[x]),
            pltpu.make_async_copy(bmap_hbm.at[x], wb_s.at[slot, pl.ds(units, rank)], b_sem.at[x]),
        )

    half = experts // 2
    batch = 2 if half % 2 == 0 else 1
    groups = half // batch

    def members(step):
        at = [step * batch + i for i in range(batch)]
        picked = [(p, p, slice(0, rank)) for p in at]
        return picked + [(p + half, p, slice(rank, 2 * rank)) for p in at]

    def slot_at(step, i):
        return lax.rem(step, wb_s.shape[0] // (2 * batch)) * 2 * batch + i

    def request_weights(step):
        for i, (x, _, _) in enumerate(members(step)):
            for copy in weight_copies(x, slot_at(step, i)):
                copy.start()

    request_weights(0)
    late_copies = [
        pltpu.make_async_copy(source, target, in_sem.at[k])
        for k, (source, target) in enumerate(
            [(hidden_hbm, hidden_ref), (u_hbm, u_ref), (amap_hbm, amap_ref)]
        )
    ]
    for copy in late_copies:
        copy.start()
    if groups > 1:
        request_weights(1)

    for copy in token_copies:
        copy.wait()
    names = [
        read_names(dy_s[i, span:, width - width // group_count :], span, top) for i in range(shards)
    ]
    codes, gates = slot_codes(names, first, capacity, experts, micro)
    windows = slot_windows(slots)
    lanes_of = shards // 2 * block
    slot_of = [slot_iota(window, lanes_of) for window in windows]
    picks = []
    for m in range(micro):
        chosen = [[], []]
        for h in range(2):
            code_s[m, h] = codes[m][h]
        for x in range(experts):
            sums = []
            for h in range(2):
                hit = codes[m][h][x : x + 1, :] == slot_of[h]
                chosen[h].append(jnp.where(hit, 1.0, 0.0))
                sums.append(
                    jnp.sum(
                        jnp.where(hit, gates[m][h][x : x + 1, :], 0.0), axis=1, keepdims=True
                    )
                )
            gate_s[x, m * padded : (m + 1) * padded, :] = join_windows(
                sums[0], sums[1], windows, padded, 0
            )
        picks.append([jnp.concatenate(c, axis=0).astype(jnp.bfloat16) for c in chosen])

    tile = 512 if width % 512 == 0 else width
    for m in range(micro):
        for n in range(width // tile):
            cols = slice(n * tile, (n + 1) * tile)
            parts = []
            for h in range(2):
                tokens = jnp.concatenate(
                    [
                        dy_s[j, m * block : (m + 1) * block, cols]
                        for j in range(h * shards // 2, (h + 1) * shards // 2)
                    ],
                    axis=0,
                )
                rows = jnp.dot(picks[m][h], tokens, preferred_element_type=jnp.float32)
                parts.append(rows.reshape(experts, -1, tile))
            rows_s[:, m * padded : (m + 1) * padded, cols] = join_windows(
                parts[0], parts[1], windows, padded, 1
            ).astype(jnp.bfloat16)

    def main_products(step):
        xs = [x for x, _, _ in members(step)]
        for i, x in enumerate(xs):
            for copy in weight_copies(x, slot_at(step, i)):
                copy.wait()

        @pl.when(step + 2 < groups)
        def _():
            request_weights(step + 2)

        return [
            lax.dot_general(
                rows_s[x],
                wb_s[slot_at(step, i)],
                contract_last,
                preferred_element_type=jnp.float32,
            )
            for i, x in enumerate(xs)
        ]

    def keep_products(step, products):
        for (x, _, _), product in zip(members(step), products):
            y_s[x] = product

    share = units // group_count
    filler = jnp.zeros((padded - slots, units), jnp.float32)

    def small_steps(step):
        picked = members(step)
        xs = [x for x, _, _ in picked]
        mains = [y_s[x, :, :units] for x in xs]
        vs = [y_s[x, :, units:].astype(jnp.bfloat16) for x in xs]
        lows = [
            jnp.dot(v, amap_ref[x], preferred_element_type=jnp.float32) for v, x in zip(vs, xs)
        ]
        gates_x = [gate_s[x] for x in xs]
        wide = [
            jnp.concatenate(
                [
                    part
                    for m in range(micro)
                    for part in (hidden_ref[m, x].astype(jnp.float32), filler)
                ],
                axis=0,
            )
            for x in xs
        ]
        v_wide = [v.astype(jnp.float32) for v in vs]
        ws = [(gate * v).astype(jnp.bfloat16) for gate, v in zip(gates_x, v_wide)]
        las = [
            lax.dot_general(
                w, held.astype(jnp.bfloat16), contract_first, preferred_element_type=jnp.float32
            )
            for w, held in zip(ws, wide)
        ]
        routed = [
            jnp.sum(main * held, axis=1, keepdims=True)
            + adapter_scale
            * jnp.sum(u_ref[p, :, lanes].astype(jnp.float32) * v, axis=1, keepdims=True)
            for main, held, v, (_, p, lanes) in zip(mains, wide, v_wide, picked)
        ]
        grads = [
            (gate * (main + adapter_scale * low)).astype(jnp.bfloat16)
            for gate, main, low in zip(gates_x, mains, lows)
        ]
        for x, grad, la, back in zip(xs, grads, las, routed):
            for m in range(micro):
                hg_ref[m, x] = grad[m * padded : m * padded + slots]
                for h, (low, high) in enumerate(windows):
                    hit = code_s[m, h, pl.ds(x, 1), :] == slot_of[h]
                    rows = back[m * padded + low : m * padded + high]
                    back_s[m, h, pl.ds(x, 1), :] = jnp.sum(
                        jnp.where(hit, rows, 0.0), axis=0, keepdims=True
                    )
            for k in range(group_count):
                la_s[k, x] = (adapter_scale * la[:, k * share : (k + 1) * share]).astype(
                    la_s.dtype
                )

    def both_steps(step, carry):
        products = main_products(step)
        small_steps(step - 1)
        keep_products(step, products)
        return carry

    keep_products(0, main_products(0))
    for copy in late_copies:
        copy.wait()
    lax.fori_loop(1, groups, both_steps, 0)
    small_steps(groups - 1)

    group = lax.axis_index("dp")
    la_copies = [
        pltpu.make_async_copy(
            la_s.at[lax.rem(group + s, group_count)], la_outs[s], la_sem.at[s]
        )
        for s in range(group_count)
    ]
    for copy in la_copies:
        copy.start()
    number = lax.broadcasted_iota(jnp.int32, (experts, span), 0).astype(jnp.float32) + first
    for j in range(shards):
        h, k = j // (shards // 2), j % (shards // 2)
        back = jnp.concatenate(
            [back_s[m, h, :, k * block : (k + 1) * block] for m in range(micro)], axis=1
        )
        found = [
            jnp.sum(jnp.where(name == number, back, 0.0), axis=0, keepdims=True)
            for name in names[j][0]
        ]
        rk_ref[j] = jnp.concatenate(found, axis=0)
    for copy in la_copies:
        copy.wait()


def adapter_kernel(capacity, micro, span, top, group_count, shards, *refs):
    pairs = shards // 2
    early_ref, early_far_ref, near_ref, far_ref = refs[:4]
    lb_hbm, tok_s, q_s, u_refs, lb_ref, sem, u_sem, lb_sem = refs[4:]
    experts, rank, share = lb_ref.shape
    lb_copies = [
        pltpu.make_async_copy(lb_ref.at[x], lb_hbm.at[x], lb_sem.at[x]) for x in range(experts)
    ]
    blocks, tall = u_refs.shape[1:3]
    padded = tall // micro
    block = span // micro
    first = (lax.axis_index("expert") * experts).astype(jnp.float32)
    group = lax.axis_index("dp")
    owners = [shard_owner(i, shards) for i in range(shards)]
    copies, u_copies = [], []
    for g in range(group_count):
        home = lax.rem(group - g + group_count, group_count)
        for i in range(shards):
            if i % pairs:
                source = (far_ref if i >= pairs else near_ref).at[home, i % pairs - 1]
            elif i:
                source = early_far_ref.at[home]
            else:
                source = early_ref.at[home, pl.ds(blocks * tall, tok_s.shape[2])]
            copies.append(pltpu.make_async_copy(source, tok_s.at[g, owners[i]], sem.at[g, i]))
        for k in range(blocks):
            source = early_ref.at[home, pl.ds(k * tall, tall)]
            u_copies.append(pltpu.make_async_copy(source, u_refs.at[g, k], u_sem.at[g, k]))
    for copy in copies + u_copies:
        copy.start()
    slots = capacity * shards
    windows = slot_windows(slots)
    slot_of = [slot_iota(window, shards // 2 * block) for window in windows]
    for g in range(group_count):
        for i in range(shards):
            copies[g * shards + i].wait()
        names = [read_names(tok_s[g, i, span:, :], span, top) for i in range(shards)]
        codes, gates = slot_codes(names, first, capacity, experts, micro)
        for m in range(micro):
            parts = []
            for h in range(2):
                picks = jnp.concatenate(
                    [
                        jnp.where(
                            codes[m][h][x : x + 1, :] == slot_of[h],
                            gates[m][h][x : x + 1, :],
                            0.0,
                        )
                        for x in range(experts)
                    ],
                    axis=0,
                ).astype(jnp.bfloat16)
                tokens = jnp.concatenate(
                    [
                        tok_s[g, j, m * block : (m + 1) * block, :]
                        for j in range(h * shards // 2, (h + 1) * shards // 2)
                    ],
                    axis=0,
                )
                rows = jnp.dot(picks, tokens, preferred_element_type=jnp.float32)
                parts.append(rows.reshape(experts, -1, share))
            q = join_windows(parts[0], parts[1], windows, padded, 1).astype(jnp.bfloat16)
            at = g * tall + m * padded
            q_s[:, at : at + padded, :] = q
    for copy in u_copies:
        copy.wait()
    half = experts // 2
    for x in range(half):
        lane = x // blocks * 2 * rank
        both = jnp.concatenate(
            [u_refs[g, x % blocks, :, lane : lane + 2 * rank] for g in range(group_count)], axis=0
        )
        lb_ref[x] = adapter_scale * lax.dot_general(
            both[:, :rank], q_s[x], contract_first, preferred_element_type=jnp.float32
        )
        lb_ref[x + half] = adapter_scale * lax.dot_general(
            both[:, rank:], q_s[x + half], contract_first, preferred_element_type=jnp.float32
        )
        lb_copies[x].start()
        lb_copies[x + half].start()
    for copy in lb_copies:
        copy.wait()


def ring_order(count):
    return list(range(0, count, 2)) + list(range(1, count, 2))[::-1]


def local_by_tokens(
    output_gradient,
    chosen_expert_index,
    routing_gate_weight,
    hidden,
    frozen_down_weight,
    adapter_input_map,
    adapter_output_map,
):
    sources = lax.axis_size("expert")
    group_count = lax.axis_size("dp")
    micro, experts, slots, units = hidden.shape
    span, top = chosen_expert_index.shape
    width = output_gradient.shape[1]
    rank = adapter_input_map.shape[2]
    capacity = slots // sources
    block = span // micro
    padded = pad_rows(slots)
    share = width // group_count
    pairs = sources // 2
    chunks = 2 if group_count % 2 == 0 else 1
    part = width // chunks

    order = ring_order(pairs)
    place = {z: i for i, z in enumerate(order)}
    ring = [
        (2 * z + c, 2 * order[(place[z] + 1) % pairs] + c) for z in range(pairs) for c in range(2)
    ]
    swap = [(e, e ^ 1) for e in range(sources)]

    amap = jnp.swapaxes(adapter_input_map, 1, 2)
    u = jnp.einsum("mesk,exk->emsx", hidden, amap, preferred_element_type=jnp.float32)
    u = u.astype(jnp.bfloat16)
    u = jnp.pad(u, ((0, 0), (0, 0), (0, padded - slots), (0, 0))).reshape(
        2, experts // 2, micro * padded, rank
    )
    u = jnp.concatenate([u[0], u[1]], axis=-1)

    def shift_groups(array, by):
        return lax.ppermute(
            array, "dp", [(d, (d + by) % group_count) for d in range(group_count)]
        )

    def swap_partners(array):
        return lax.ppermute(array, "expert", swap)

    def exchange_columns(chosen):
        def columns(pieces, g):
            at = g * share % part
            return pieces[g * share // part][:, at : at + share]

        return jnp.stack(
            [jnp.stack([columns(pieces, g) for pieces in chosen]) for g in range(group_count)]
        )

    def across_groups(array):
        return lax.all_to_all(array, "dp", split_axis=0, concat_axis=0, tiled=True)

    others = range(1, group_count)
    lines = 2 * top * span // share
    extra = -(-lines // 8) * 8
    vmem = pl.BlockSpec(memory_space=pltpu.VMEM)
    sent = pl.pallas_call(
        functools.partial(payload_kernel, share),
        out_shape=[jax.ShapeDtypeStruct((span + extra, part), jnp.bfloat16)] * chunks,
        in_specs=[vmem] * 3,
        out_specs=[vmem] * chunks,
        compiler_params=pltpu.CompilerParams(vmem_limit_bytes=58 * 1024 * 1024),
        name="ring_payload",
    )(output_gradient, chosen_expert_index.T, routing_gate_weight.T)

    near, far = [list(sent)], []
    blocks = experts // 2 * 2 * rank // share
    packed = jnp.concatenate(
        [u[k * blocks : (k + 1) * blocks] for k in range(experts // 2 // blocks)], axis=-1
    ).reshape(blocks * micro * padded, share)
    early = jnp.stack(
        [
            jnp.concatenate(
                [packed, sent[g * share // part][:, g * share % part :][:, :share]], axis=0
            )
            for g in range(group_count)
        ]
    )
    early = across_groups(early)
    early_far = swap_partners(early[:, blocks * micro * padded :])
    for step in range(pairs - 1):
        if step > 1:
            tied = [
                lax.optimization_barrier((near[step][c], [shard[c] for shard in far]))
                for c in range(chunks)
            ]
            near[step] = [a for a, _ in tied]
            far = [[b[k] for _, b in tied] for k in range(len(far))]
        near.append([lax.ppermute(piece, "expert", ring) for piece in near[step]])
        far.append([swap_partners(piece) for piece in near[step]])
    far.append([swap_partners(piece) for piece in near[-1]])
    columns = exchange_columns(near[1:])
    columns, early, early_far, far[-2:] = lax.optimization_barrier(
        (columns, early, early_far, far[-2:])
    )
    columns = across_groups(columns)
    pieces = [piece for shard in near + far for piece in shard]

    anywhere = pl.BlockSpec(memory_space=pl.ANY)
    kept = 3 * (4 if experts % 4 == 0 else 2)
    part_a = jax.ShapeDtypeStruct((experts, rank, units // group_count), jnp.bfloat16)
    hidden_grad, routed, *parts = pl.pallas_call(
        functools.partial(expert_kernel, capacity, group_count, sources, chunks),
        out_shape=(
            jax.ShapeDtypeStruct(hidden.shape, jnp.bfloat16),
            jax.ShapeDtypeStruct((sources, top, span), jnp.float32),
        )
        + (part_a,) * group_count,
        in_specs=[anywhere] * (sources * chunks) + [anywhere] * 5,
        out_specs=(vmem,) * 2 + (anywhere,) * group_count,
        scratch_shapes=[
            pltpu.VMEM((sources, span + extra, width), jnp.bfloat16),
            pltpu.VMEM((min(experts, kept), units + rank, width), jnp.bfloat16),
            pltpu.VMEM((experts, micro * padded, width), jnp.bfloat16),
            pltpu.VMEM((experts, micro * padded, units + rank), jnp.float32),
            pltpu.VMEM((micro, 2, experts, sources // 2 * block), jnp.float32),
            pltpu.VMEM((experts, micro * padded, 1), jnp.float32),
            pltpu.VMEM((micro, 2, experts, sources // 2 * block), jnp.float32),
            pltpu.VMEM((group_count, experts, rank, units // group_count), jnp.bfloat16),
            pltpu.VMEM(hidden.shape, jnp.bfloat16),
            pltpu.VMEM(u.shape, jnp.bfloat16),
            pltpu.VMEM(amap.shape, jnp.bfloat16),
            pltpu.SemaphoreType.DMA((sources, chunks)),
            pltpu.SemaphoreType.DMA((experts,)),
            pltpu.SemaphoreType.DMA((experts,)),
            pltpu.SemaphoreType.DMA((group_count,)),
            pltpu.SemaphoreType.DMA((3,)),
        ],
        compiler_params=pltpu.CompilerParams(vmem_limit_bytes=58 * 1024 * 1024),
        cost_estimate=pl.CostEstimate(
            flops=2 * experts * micro * padded * width * (units + rank + sources * block),
            bytes_accessed=2 * experts * width * (units + rank) + 2 * sources * span * width,
            transcendentals=0,
        ),
        name="expert_rows",
    )(*pieces, hidden, u, frozen_down_weight, amap, adapter_output_map)

    columns, parts, routed = lax.optimization_barrier((columns, parts, routed))
    swapped = swap_partners(columns)
    arrived = [shift_groups(parts[s], s) for s in others]
    swapped, routed = lax.optimization_barrier((swapped, routed))
    home = lax.all_to_all(routed, "expert", split_axis=0, concat_axis=0, tiled=True)

    lora_b = pl.pallas_call(
        functools.partial(adapter_kernel, capacity, micro, span, top, group_count, sources),
        out_shape=jax.ShapeDtypeStruct((experts, rank, share), jnp.float32),
        in_specs=[anywhere] * 4,
        out_specs=anywhere,
        scratch_shapes=[
            pltpu.VMEM((group_count, sources, span + extra, share), jnp.bfloat16),
            pltpu.VMEM((experts, group_count * micro * padded, share), jnp.bfloat16),
            pltpu.VMEM((group_count, blocks, micro * padded, share), jnp.bfloat16),
            pltpu.VMEM((experts, rank, share), jnp.float32),
            pltpu.SemaphoreType.DMA((group_count, sources)),
            pltpu.SemaphoreType.DMA((group_count, blocks)),
            pltpu.SemaphoreType.DMA((experts,)),
        ],
        compiler_params=pltpu.CompilerParams(vmem_limit_bytes=58 * 1024 * 1024),
        cost_estimate=pl.CostEstimate(
            flops=2 * experts * micro * padded * share * group_count * (rank + sources * block),
            bytes_accessed=2 * group_count * sources * span * share + 4 * experts * rank * share,
            transcendentals=0,
        ),
        name="adapter_columns",
    )(early, early_far, columns, swapped)

    home, arrived, lora_b = lax.optimization_barrier((home, arrived, lora_b))
    router_grad = jnp.sum(home, axis=0).T
    lora_a = parts[0].astype(jnp.float32)
    for part in arrived:
        lora_a = lora_a + part.astype(jnp.float32)
    return (hidden_grad, router_grad, lora_a, lora_b)


def local(*arrays):
    sources, groups = lax.axis_size("expert"), lax.axis_size("dp")
    span, width = arrays[0].shape
    top, (micro, experts, slots, units) = arrays[1].shape[1], arrays[3].shape
    even = sources % 4 == 0 and experts % 2 == 0 and width % (128 * groups) == 0 and units % groups == 0
    rank = arrays[5].shape[2]
    packs = width // groups % (2 * rank) == 0 and experts * rank % (width // groups) == 0
    packs = packs and 2 * top * span % (width // groups) == 0 and (width // groups) % span == 0
    exact = experts * sources <= 256
    if even and packs and exact and sources * span <= micro * experts * slots:
        return local_by_tokens(*arrays)
    return local_by_slots(*arrays)


def solution(mesh):
    in_specs = (
        P(("dp", "expert"), None),
        P(("dp", "expert"), None),
        P(("dp", "expert"), None),
        P(None, ("dp", "expert"), None, None),
        P("expert", None, None),
        P("expert", None, None),
        P("expert", None, None),
    )
    out_specs = (
        P(None, ("dp", "expert"), None, None),
        P(("dp", "expert"), None),
        P("expert", None, "dp"),
        P("expert", None, "dp"),
    )
    return jax.shard_map(local, mesh=mesh, in_specs=in_specs, out_specs=out_specs, check_vma=False)
```

```python
import functools

import jax
import jax.numpy as jnp
from jax import lax
from jax.experimental import pallas as pl
from jax.experimental.pallas import tpu as pltpu
from jax.sharding import PartitionSpec as P

adapter_scale = 2.0


def slot_rows(id_rows, experts, per_device, sources, capacity):
    onehot = (id_rows[:, :, None] == jnp.arange(experts, dtype=jnp.int32)[None, None, :]).astype(
        jnp.int32
    )
    before = jnp.sum(jnp.cumsum(onehot, axis=1) * onehot, axis=2) - 1
    target_dev = id_rows // per_device
    target_slot = id_rows % per_device
    return (target_slot * sources + target_dev) * capacity + before


def pick_rows(source, indices):
    return source[indices]


def dispatch_buffers(grad_rows, weight_rows, send_rows, top_count, buffer_len):
    entry_count = send_rows.shape[1]
    token_count = grad_rows.shape[1]
    filler = jnp.full((buffer_len,), entry_count, jnp.int32)

    def invert(rows):
        return filler.at[rows].set(jnp.arange(entry_count, dtype=jnp.int32))

    table = jax.vmap(invert)(send_rows)
    padded_grad = jnp.concatenate(
        [grad_rows, jnp.zeros((grad_rows.shape[0], 1, grad_rows.shape[2]), grad_rows.dtype)], axis=1
    )
    padded_weight = jnp.concatenate(
        [weight_rows, jnp.zeros((weight_rows.shape[0], 1), weight_rows.dtype)], axis=1
    )
    token_pick = jnp.where(table < entry_count, table // top_count, token_count)
    sent_grad = jax.vmap(pick_rows)(padded_grad, token_pick)
    sent_weight = jax.vmap(pick_rows)(padded_weight, table)
    return (sent_grad, sent_weight)


def expert_rows_view(
    received_gradient,
    received_weight,
    retained_rows,
    frozen_down_weight,
    adapter_input_map,
    adapter_output_map,
):
    frozen_term = jnp.einsum(
        "mesd,efd->mesf", received_gradient, frozen_down_weight, preferred_element_type=jnp.float32
    )
    across_product = jnp.einsum(
        "hati,aki->hatk", received_gradient, adapter_output_map, preferred_element_type=jnp.float32
    ).astype(jnp.bfloat16)
    low_rank_state = jnp.einsum(
        "ptqv,tgv->ptqg", across_product, adapter_input_map, preferred_element_type=jnp.float32
    )
    capacity_slot_weight = received_weight.astype(jnp.float32)[..., None]
    hidden_state_gradient = (
        capacity_slot_weight * (frozen_term + adapter_scale * low_rank_state)
    ).astype(jnp.bfloat16)
    down_mapping = jnp.einsum(
        "lkgu,kup->lkgp", retained_rows, adapter_input_map, preferred_element_type=jnp.float32
    ).astype(jnp.bfloat16)
    complete_term = jnp.sum(frozen_term * retained_rows.astype(jnp.float32), axis=-1)
    adapter_term = jnp.einsum(
        "mesr,mesr->mes", down_mapping, across_product, preferred_element_type=jnp.float32
    )
    routing_rows = complete_term + adapter_scale * adapter_term
    scaled_gradient = (capacity_slot_weight * received_gradient).astype(jnp.bfloat16)
    scaled_across_product = (capacity_slot_weight * across_product.astype(jnp.float32)).astype(
        jnp.bfloat16
    )
    adapter_output_gradient = adapter_scale * jnp.einsum(
        "mesr,mesd->erd", down_mapping, scaled_gradient, preferred_element_type=jnp.float32
    )
    adapter_input_gradient = adapter_scale * jnp.einsum(
        "mesr,mesf->erf", scaled_across_product, retained_rows, preferred_element_type=jnp.float32
    )
    return (hidden_state_gradient, routing_rows, adapter_input_gradient, adapter_output_gradient)


def local_by_slots(
    output_gradient,
    chosen_expert_index,
    routing_gate_weight,
    hidden,
    frozen_down_weight,
    adapter_input_map,
    adapter_output_map,
):
    sources = lax.axis_size("expert")
    per_device = frozen_down_weight.shape[0]
    experts = per_device * sources
    micro_count = hidden.shape[0]
    slot_count = hidden.shape[2]
    capacity = slot_count // sources
    top_count = chosen_expert_index.shape[1]
    model_width = output_gradient.shape[1]
    buffer_len = experts * capacity
    grad_rows = output_gradient.reshape(micro_count, -1, model_width)
    id_rows = chosen_expert_index.reshape(micro_count, -1)
    weight_rows = routing_gate_weight.reshape(micro_count, -1)
    send_rows = slot_rows(id_rows, experts, per_device, sources, capacity)
    sent_grad, sent_weight = dispatch_buffers(
        grad_rows, weight_rows, send_rows, top_count, buffer_len
    )
    sent_grad = sent_grad.reshape(micro_count, per_device, sources, capacity, model_width)
    sent_weight = sent_weight.reshape(micro_count, per_device, sources, capacity)
    received_gradient, received_weight = (
        lax.all_to_all(sent_grad, "expert", split_axis=2, concat_axis=2, tiled=True),
        lax.all_to_all(sent_weight, "expert", split_axis=2, concat_axis=2, tiled=True),
    )
    received_gradient = received_gradient.reshape(micro_count, per_device, slot_count, model_width)
    received_weight = received_weight.reshape(micro_count, per_device, slot_count)
    hidden_grad, routing_rows, adapter_input_gradient, adapter_output_gradient = expert_rows_view(
        received_gradient,
        received_weight,
        hidden,
        frozen_down_weight,
        adapter_input_map,
        adapter_output_map,
    )
    router_home = lax.all_to_all(
        routing_rows.reshape(micro_count, per_device, sources, capacity),
        "expert",
        split_axis=2,
        concat_axis=2,
        tiled=True,
    )
    router_flat = router_home.reshape(micro_count, buffer_len)
    router_grad = jax.vmap(pick_rows)(router_flat, send_rows).reshape(-1, top_count)
    share_a, share_b = (
        lax.psum_scatter(adapter_input_gradient, "dp", scatter_dimension=2, tiled=True),
        lax.psum_scatter(adapter_output_gradient, "dp", scatter_dimension=2, tiled=True),
    )
    return (hidden_grad, router_grad, share_a, share_b)


def pad_rows(count):
    return -(-count // 16) * 16


def read_names(rows, span, top):
    wide = rows.astype(jnp.float32)
    per = wide.shape[1] // span
    lines = [
        wide[k // per : k // per + 1, (k % per) * span : (k % per + 1) * span]
        for k in range(2 * top)
    ]
    return lines[:top], lines[top:]


def slot_codes(names, first, capacity, experts, micro):
    sources = len(names)
    span = names[0][0][0].shape[1]
    block = span // micro
    number = lax.broadcasted_iota(jnp.int32, (experts, span), 0).astype(jnp.float32) + first
    from_row = lax.broadcasted_iota(jnp.int32, (span, span), 0)
    to_row = lax.broadcasted_iota(jnp.int32, (span, span), 1)
    earlier = jnp.where(
        (from_row // block == to_row // block) & (from_row < to_row), 1.0, 0.0
    ).astype(jnp.bfloat16)
    codes, gates = [], []
    for j in range(sources):
        named = jnp.zeros((experts, span), jnp.float32)
        gate = jnp.zeros((experts, span), jnp.float32)
        for name, weight in zip(*names[j]):
            hit = name == number
            named = jnp.where(hit, 1.0, named)
            gate = jnp.where(hit, weight, gate)
        before = jnp.dot(named.astype(jnp.bfloat16), earlier, preferred_element_type=jnp.float32)
        codes.append(jnp.where(named > 0.0, before + float(j * capacity), -1.0))
        gates.append(gate)

    def arrange(values):
        half = sources // 2
        return [
            [
                jnp.concatenate(
                    [c[:, m * block : (m + 1) * block] for c in values[h * half : (h + 1) * half]],
                    axis=1,
                )
                for h in range(2)
            ]
            for m in range(micro)
        ]

    return arrange(codes), arrange(gates)


def slot_windows(slots):
    half = slots // 2
    return [(h * half // 8 * 8, -(-(h + 1) * half // 8) * 8) for h in range(2)]


def slot_iota(window, lanes):
    shape = (window[1] - window[0], lanes)
    return lax.broadcasted_iota(jnp.int32, shape, 0).astype(jnp.float32) + float(window[0])


def join_windows(first_part, second_part, windows, padded, axis):
    (_, end), (start, last) = windows

    def rows(values, low, high):
        return lax.slice_in_dim(values, low, high, axis=axis)

    parts = [rows(first_part, 0, start)]
    if end > start:
        parts.append(rows(first_part, start, end) + rows(second_part, 0, end - start))
    parts.append(rows(second_part, end - start, last - start))
    if padded > last:
        shape = list(first_part.shape)
        shape[axis] = padded - last
        parts.append(jnp.zeros(shape, first_part.dtype))
    return jnp.concatenate(parts, axis=axis)


contract_last = (((1,), (1,)), ((), ()))
contract_first = (((0,), (0,)), ((), ()))


def shard_owner(index, sources):
    pairs = sources // 2
    me = lax.axis_index("expert")
    column, core = me // 2, lax.rem(me, 2)
    place = jnp.where(lax.rem(column, 2) == 0, column // 2, pairs - 1 - column // 2)
    place = lax.rem(place - index % pairs + pairs, pairs)
    column = jnp.where(2 * place < pairs, 2 * place, 2 * (pairs - 1 - place) + 1)
    return 2 * column + (core if index < pairs else 1 - core)


def payload_kernel(share, dy_ref, index_ref, gate_ref, *outs):
    top, span = index_ref.shape
    part = outs[0].shape[1]
    per = share // span
    names, gates = index_ref[...].astype(jnp.float32), gate_ref[...].astype(jnp.float32)
    lines = [names[k : k + 1] for k in range(top)] + [gates[k : k + 1] for k in range(top)]
    rows = [jnp.concatenate(lines[k : k + per], axis=1) for k in range(0, 2 * top, per)]
    spare = outs[0].shape[0] - span - len(rows)
    if spare:
        rows.append(jnp.zeros((spare, share), jnp.float32))
    below = jnp.concatenate(rows, axis=0).astype(jnp.bfloat16)
    for c, out in enumerate(outs):
        out[:span] = dy_ref[:, c * part : (c + 1) * part]
        for at in range(0, part, share):
            out[span:, at : at + share] = below


def expert_kernel(capacity, group_count, shards, chunks, *refs):
    token_refs = refs[: shards * chunks]
    refs = refs[shards * chunks :]
    hidden_hbm, u_hbm, weight_hbm, amap_hbm, bmap_hbm, hg_ref, rk_ref = refs[:7]
    la_outs = refs[7 : 7 + group_count]
    scratch = refs[7 + group_count :]
    dy_s, wb_s, rows_s, y_s, code_s, gate_s, back_s, la_s = scratch[:8]
    hidden_ref, u_ref, amap_ref, dy_sem, w_sem, b_sem, la_sem, in_sem = scratch[8:]
    top, span = rk_ref.shape[1:]
    micro, experts, slots, units = hidden_ref.shape
    rank = amap_ref.shape[1]
    width = dy_s.shape[2]
    block = span // micro
    padded = rows_s.shape[1] // micro
    first = (lax.axis_index("expert") * experts).astype(jnp.float32)

    part = width // chunks
    owners = [shard_owner(i, shards) for i in range(shards)]
    token_copies = [
        pltpu.make_async_copy(
            token_refs[i * chunks + c],
            dy_s.at[owners[i], :, pl.ds(c * part, part)],
            dy_sem.at[i, c],
        )
        for i in range(shards)
        for c in range(chunks)
    ]
    for copy in token_copies:
        copy.start()

    def weight_copies(x, slot):
        return (
            pltpu.make_async_copy(weight_hbm.at[x], wb_s.at[slot, pl.ds(0, units)], w_sem.at[x]),
            pltpu.make_async_copy(bmap_hbm.at[x], wb_s.at[slot, pl.ds(units, rank)], b_sem.at[x]),
        )

    half = experts // 2
    batch = 2 if half % 2 == 0 else 1
    groups = half // batch

    def members(step):
        at = [step * batch + i for i in range(batch)]
        picked = [(p, p, slice(0, rank)) for p in at]
        return picked + [(p + half, p, slice(rank, 2 * rank)) for p in at]

    def slot_at(step, i):
        return lax.rem(step, wb_s.shape[0] // (2 * batch)) * 2 * batch + i

    def request_weights(step):
        for i, (x, _, _) in enumerate(members(step)):
            for copy in weight_copies(x, slot_at(step, i)):
                copy.start()

    late_copies = [
        pltpu.make_async_copy(source, target, in_sem.at[k])
        for k, (source, target) in enumerate(
            [(hidden_hbm, hidden_ref), (u_hbm, u_ref), (amap_hbm, amap_ref)]
        )
    ]

    for copy in token_copies:
        copy.wait()
    request_weights(0)
    for copy in late_copies:
        copy.start()
    names = [
        read_names(dy_s[i, span:, width - width // group_count :], span, top) for i in range(shards)
    ]
    codes, gates = slot_codes(names, first, capacity, experts, micro)
    if groups > 1:
        request_weights(1)
    windows = slot_windows(slots)
    lanes_of = shards // 2 * block
    slot_of = [slot_iota(window, lanes_of) for window in windows]
    picks = []
    for m in range(micro):
        chosen = [[], []]
        for h in range(2):
            code_s[m, h] = codes[m][h]
        for x in range(experts):
            sums = []
            for h in range(2):
                hit = codes[m][h][x : x + 1, :] == slot_of[h]
                chosen[h].append(jnp.where(hit, 1.0, 0.0))
                sums.append(
                    jnp.sum(
                        jnp.where(hit, gates[m][h][x : x + 1, :], 0.0), axis=1, keepdims=True
                    )
                )
            gate_s[x, m * padded : (m + 1) * padded, :] = join_windows(
                sums[0], sums[1], windows, padded, 0
            )
        picks.append([jnp.concatenate(c, axis=0).astype(jnp.bfloat16) for c in chosen])

    tile = 512 if width % 512 == 0 else width
    for m in range(micro):
        for n in range(width // tile):
            cols = slice(n * tile, (n + 1) * tile)
            parts = []
            for h in range(2):
                tokens = jnp.concatenate(
                    [
                        dy_s[j, m * block : (m + 1) * block, cols]
                        for j in range(h * shards // 2, (h + 1) * shards // 2)
                    ],
                    axis=0,
                )
                rows = jnp.dot(picks[m][h], tokens, preferred_element_type=jnp.float32)
                parts.append(rows.reshape(experts, -1, tile))
            rows_s[:, m * padded : (m + 1) * padded, cols] = join_windows(
                parts[0], parts[1], windows, padded, 1
            ).astype(jnp.bfloat16)

    def main_products(step):
        xs = [x for x, _, _ in members(step)]
        for i, x in enumerate(xs):
            for copy in weight_copies(x, slot_at(step, i)):
                copy.wait()

        @pl.when(step + 2 < groups)
        def _():
            request_weights(step + 2)

        return [
            lax.dot_general(
                rows_s[x],
                wb_s[slot_at(step, i)],
                contract_last,
                preferred_element_type=jnp.float32,
            )
            for i, x in enumerate(xs)
        ]

    def keep_products(step, products):
        for (x, _, _), product in zip(members(step), products):
            y_s[x] = product

    share = units // group_count
    filler = jnp.zeros((padded - slots, units), jnp.float32)

    def small_steps(step):
        picked = members(step)
        xs = [x for x, _, _ in picked]
        mains = [y_s[x, :, :units] for x in xs]
        vs = [y_s[x, :, units:].astype(jnp.bfloat16) for x in xs]
        lows = [
            jnp.dot(v, amap_ref[x], preferred_element_type=jnp.float32) for v, x in zip(vs, xs)
        ]
        gates_x = [gate_s[x] for x in xs]
        wide = [
            jnp.concatenate(
                [
                    part
                    for m in range(micro)
                    for part in (hidden_ref[m, x].astype(jnp.float32), filler)
                ],
                axis=0,
            )
            for x in xs
        ]
        v_wide = [v.astype(jnp.float32) for v in vs]
        ws = [(gate * v).astype(jnp.bfloat16) for gate, v in zip(gates_x, v_wide)]
        las = [
            lax.dot_general(
                w, held.astype(jnp.bfloat16), contract_first, preferred_element_type=jnp.float32
            )
            for w, held in zip(ws, wide)
        ]
        routed = [
            jnp.sum(main * held, axis=1, keepdims=True)
            + adapter_scale
            * jnp.sum(u_ref[p, :, lanes].astype(jnp.float32) * v, axis=1, keepdims=True)
            for main, held, v, (_, p, lanes) in zip(mains, wide, v_wide, picked)
        ]
        grads = [
            (gate * (main + adapter_scale * low)).astype(jnp.bfloat16)
            for gate, main, low in zip(gates_x, mains, lows)
        ]
        for x, grad, la, back in zip(xs, grads, las, routed):
            for m in range(micro):
                hg_ref[m, x] = grad[m * padded : m * padded + slots]
                for h, (low, high) in enumerate(windows):
                    hit = code_s[m, h, pl.ds(x, 1), :] == slot_of[h]
                    rows = back[m * padded + low : m * padded + high]
                    back_s[m, h, pl.ds(x, 1), :] = jnp.sum(
                        jnp.where(hit, rows, 0.0), axis=0, keepdims=True
                    )
            for k in range(group_count):
                la_s[k, x] = (adapter_scale * la[:, k * share : (k + 1) * share]).astype(
                    la_s.dtype
                )

    def both_steps(step, carry):
        products = main_products(step)
        small_steps(step - 1)
        keep_products(step, products)
        return carry

    keep_products(0, main_products(0))
    for copy in late_copies:
        copy.wait()
    lax.fori_loop(1, groups, both_steps, 0)
    small_steps(groups - 1)

    group = lax.axis_index("dp")
    la_copies = [
        pltpu.make_async_copy(
            la_s.at[lax.rem(group + s, group_count)], la_outs[s], la_sem.at[s]
        )
        for s in range(group_count)
    ]
    for copy in la_copies:
        copy.start()
    number = lax.broadcasted_iota(jnp.int32, (experts, span), 0).astype(jnp.float32) + first
    for j in range(shards):
        h, k = j // (shards // 2), j % (shards // 2)
        back = jnp.concatenate(
            [back_s[m, h, :, k * block : (k + 1) * block] for m in range(micro)], axis=1
        )
        found = [
            jnp.sum(jnp.where(name == number, back, 0.0), axis=0, keepdims=True)
            for name in names[j][0]
        ]
        rk_ref[j] = jnp.concatenate(found, axis=0)
    for copy in la_copies:
        copy.wait()


def adapter_kernel(capacity, micro, span, top, group_count, shards, *refs):
    pairs = shards // 2
    early_ref, early_far_ref, near_ref, far_ref = refs[:4]
    lb_hbm, tok_s, q_s, u_refs, lb_ref, sem, u_sem, lb_sem = refs[4:]
    experts, rank, share = lb_ref.shape
    lb_copies = [
        pltpu.make_async_copy(lb_ref.at[x], lb_hbm.at[x], lb_sem.at[x]) for x in range(experts)
    ]
    blocks, tall = u_refs.shape[1:3]
    padded = tall // micro
    block = span // micro
    first = (lax.axis_index("expert") * experts).astype(jnp.float32)
    group = lax.axis_index("dp")
    owners = [shard_owner(i, shards) for i in range(shards)]
    copies, u_copies = [], []
    for g in range(group_count):
        home = lax.rem(group - g + group_count, group_count)
        for i in range(shards):
            if i % pairs:
                source = (far_ref if i >= pairs else near_ref).at[home, i % pairs - 1]
            elif i:
                source = early_far_ref.at[home]
            else:
                source = early_ref.at[home, pl.ds(blocks * tall, tok_s.shape[2])]
            copies.append(pltpu.make_async_copy(source, tok_s.at[g, owners[i]], sem.at[g, i]))
        for k in range(blocks):
            source = early_ref.at[home, pl.ds(k * tall, tall)]
            u_copies.append(pltpu.make_async_copy(source, u_refs.at[g, k], u_sem.at[g, k]))
    for copy in copies[:shards]:
        copy.start()
    slots = capacity * shards
    windows = slot_windows(slots)
    slot_of = [slot_iota(window, shards // 2 * block) for window in windows]
    for g in range(group_count):
        for copy in copies[g * shards : (g + 1) * shards]:
            copy.wait()
        for copy in copies[(g + 1) * shards : (g + 2) * shards] + (u_copies if g == 0 else []):
            copy.start()
        names = [read_names(tok_s[g, i, span:, :], span, top) for i in range(shards)]
        codes, gates = slot_codes(names, first, capacity, experts, micro)
        for m in range(micro):
            parts = []
            for h in range(2):
                picks = jnp.concatenate(
                    [
                        jnp.where(
                            codes[m][h][x : x + 1, :] == slot_of[h],
                            gates[m][h][x : x + 1, :],
                            0.0,
                        )
                        for x in range(experts)
                    ],
                    axis=0,
                ).astype(jnp.bfloat16)
                tokens = jnp.concatenate(
                    [
                        tok_s[g, j, m * block : (m + 1) * block, :]
                        for j in range(h * shards // 2, (h + 1) * shards // 2)
                    ],
                    axis=0,
                )
                rows = jnp.dot(picks, tokens, preferred_element_type=jnp.float32)
                parts.append(rows.reshape(experts, -1, share))
            q = join_windows(parts[0], parts[1], windows, padded, 1).astype(jnp.bfloat16)
            at = g * tall + m * padded
            q_s[:, at : at + padded, :] = q
    for copy in u_copies:
        copy.wait()
    half = experts // 2
    for x in range(half):
        lane = x // blocks * 2 * rank
        both = jnp.concatenate(
            [u_refs[g, x % blocks, :, lane : lane + 2 * rank] for g in range(group_count)], axis=0
        )
        lb_ref[x] = adapter_scale * lax.dot_general(
            both[:, :rank], q_s[x], contract_first, preferred_element_type=jnp.float32
        )
        lb_ref[x + half] = adapter_scale * lax.dot_general(
            both[:, rank:], q_s[x + half], contract_first, preferred_element_type=jnp.float32
        )
        lb_copies[x].start()
        lb_copies[x + half].start()
    for copy in lb_copies:
        copy.wait()


def ring_order(count):
    return list(range(0, count, 2)) + list(range(1, count, 2))[::-1]


def local_by_tokens(
    output_gradient,
    chosen_expert_index,
    routing_gate_weight,
    hidden,
    frozen_down_weight,
    adapter_input_map,
    adapter_output_map,
):
    sources = lax.axis_size("expert")
    group_count = lax.axis_size("dp")
    micro, experts, slots, units = hidden.shape
    span, top = chosen_expert_index.shape
    width = output_gradient.shape[1]
    rank = adapter_input_map.shape[2]
    capacity = slots // sources
    block = span // micro
    padded = pad_rows(slots)
    share = width // group_count
    pairs = sources // 2
    chunks = 2 if group_count % 2 == 0 else 1
    part = width // chunks

    order = ring_order(pairs)
    place = {z: i for i, z in enumerate(order)}
    ring = [
        (2 * z + c, 2 * order[(place[z] + 1) % pairs] + c) for z in range(pairs) for c in range(2)
    ]
    swap = [(e, e ^ 1) for e in range(sources)]

    amap = jnp.swapaxes(adapter_input_map, 1, 2)
    u = jnp.einsum("mesk,exk->emsx", hidden, amap, preferred_element_type=jnp.float32)
    u = u.astype(jnp.bfloat16)
    u = jnp.pad(u, ((0, 0), (0, 0), (0, padded - slots), (0, 0))).reshape(
        2, experts // 2, micro * padded, rank
    )
    u = lax.optimization_barrier(jnp.concatenate([u[0], u[1]], axis=-1))

    def shift_groups(array, by):
        return lax.ppermute(
            array, "dp", [(d, (d + by) % group_count) for d in range(group_count)]
        )

    def swap_partners(array):
        return lax.ppermute(array, "expert", swap)

    def exchange_columns(chosen):
        def columns(pieces, g):
            at = g * share % part
            return pieces[g * share // part][:, at : at + share]

        return jnp.stack(
            [jnp.stack([columns(pieces, g) for pieces in chosen]) for g in range(group_count)]
        )

    def across_groups(array):
        return lax.all_to_all(array, "dp", split_axis=0, concat_axis=0, tiled=True)

    others = range(1, group_count)
    lines = 2 * top * span // share
    extra = -(-lines // 8) * 8
    vmem = pl.BlockSpec(memory_space=pltpu.VMEM)
    sent = pl.pallas_call(
        functools.partial(payload_kernel, share),
        out_shape=[jax.ShapeDtypeStruct((span + extra, part), jnp.bfloat16)] * chunks,
        in_specs=[vmem] * 3,
        out_specs=[vmem] * chunks,
        compiler_params=pltpu.CompilerParams(vmem_limit_bytes=58 * 1024 * 1024),
        name="ring_payload",
    )(output_gradient, chosen_expert_index.T, routing_gate_weight.T)

    near, far = [list(sent)], []
    blocks = experts // 2 * 2 * rank // share
    packed = jnp.concatenate(
        [u[k * blocks : (k + 1) * blocks] for k in range(experts // 2 // blocks)], axis=-1
    ).reshape(blocks * micro * padded, share)
    early = jnp.stack(
        [
            jnp.concatenate(
                [packed, sent[g * share // part][:, g * share % part :][:, :share]], axis=0
            )
            for g in range(group_count)
        ]
    )
    early = across_groups(early)
    early_far = swap_partners(early[:, blocks * micro * padded :])
    for step in range(pairs - 1):
        if step > 1:
            tied = [
                lax.optimization_barrier((near[step][c], [shard[c] for shard in far]))
                for c in range(chunks)
            ]
            near[step] = [a for a, _ in tied]
            far = [[b[k] for _, b in tied] for k in range(len(far))]
        near.append([lax.ppermute(piece, "expert", ring) for piece in near[step]])
        far.append([swap_partners(piece) for piece in near[step]])
    far.append([swap_partners(piece) for piece in near[-1]])
    columns = exchange_columns(near[1:])
    columns, early, early_far, far[-2:] = lax.optimization_barrier(
        (columns, early, early_far, far[-2:])
    )
    columns = across_groups(columns)
    pieces = [piece for shard in near + far for piece in shard]

    anywhere = pl.BlockSpec(memory_space=pl.ANY)
    kept = 3 * (4 if experts % 4 == 0 else 2)
    part_a = jax.ShapeDtypeStruct((experts, rank, units // group_count), jnp.bfloat16)
    hidden_grad, routed, *parts = pl.pallas_call(
        functools.partial(expert_kernel, capacity, group_count, sources, chunks),
        out_shape=(
            jax.ShapeDtypeStruct(hidden.shape, jnp.bfloat16),
            jax.ShapeDtypeStruct((sources, top, span), jnp.float32),
        )
        + (part_a,) * group_count,
        in_specs=[anywhere] * (sources * chunks) + [anywhere] * 5,
        out_specs=(vmem,) * 2 + (anywhere,) * group_count,
        scratch_shapes=[
            pltpu.VMEM((sources, span + extra, width), jnp.bfloat16),
            pltpu.VMEM((min(experts, kept), units + rank, width), jnp.bfloat16),
            pltpu.VMEM((experts, micro * padded, width), jnp.bfloat16),
            pltpu.VMEM((experts, micro * padded, units + rank), jnp.float32),
            pltpu.VMEM((micro, 2, experts, sources // 2 * block), jnp.float32),
            pltpu.VMEM((experts, micro * padded, 1), jnp.float32),
            pltpu.VMEM((micro, 2, experts, sources // 2 * block), jnp.float32),
            pltpu.VMEM((group_count, experts, rank, units // group_count), jnp.bfloat16),
            pltpu.VMEM(hidden.shape, jnp.bfloat16),
            pltpu.VMEM(u.shape, jnp.bfloat16),
            pltpu.VMEM(amap.shape, jnp.bfloat16),
            pltpu.SemaphoreType.DMA((sources, chunks)),
            pltpu.SemaphoreType.DMA((experts,)),
            pltpu.SemaphoreType.DMA((experts,)),
            pltpu.SemaphoreType.DMA((group_count,)),
            pltpu.SemaphoreType.DMA((3,)),
        ],
        compiler_params=pltpu.CompilerParams(vmem_limit_bytes=58 * 1024 * 1024),
        cost_estimate=pl.CostEstimate(
            flops=2 * experts * micro * padded * width * (units + rank + sources * block),
            bytes_accessed=2 * experts * width * (units + rank) + 2 * sources * span * width,
            transcendentals=0,
        ),
        name="expert_rows",
    )(*pieces, hidden, u, frozen_down_weight, amap, adapter_output_map)

    columns, parts, routed = lax.optimization_barrier((columns, parts, routed))
    swapped = swap_partners(columns)
    arrived = [shift_groups(parts[s], s) for s in others]
    swapped, routed = lax.optimization_barrier((swapped, routed))
    home = lax.all_to_all(routed, "expert", split_axis=0, concat_axis=0, tiled=True)

    lora_b = pl.pallas_call(
        functools.partial(adapter_kernel, capacity, micro, span, top, group_count, sources),
        out_shape=jax.ShapeDtypeStruct((experts, rank, share), jnp.float32),
        in_specs=[anywhere] * 4,
        out_specs=anywhere,
        scratch_shapes=[
            pltpu.VMEM((group_count, sources, span + extra, share), jnp.bfloat16),
            pltpu.VMEM((experts, group_count * micro * padded, share), jnp.bfloat16),
            pltpu.VMEM((group_count, blocks, micro * padded, share), jnp.bfloat16),
            pltpu.VMEM((experts, rank, share), jnp.float32),
            pltpu.SemaphoreType.DMA((group_count, sources)),
            pltpu.SemaphoreType.DMA((group_count, blocks)),
            pltpu.SemaphoreType.DMA((experts,)),
        ],
        compiler_params=pltpu.CompilerParams(vmem_limit_bytes=58 * 1024 * 1024),
        cost_estimate=pl.CostEstimate(
            flops=2 * experts * micro * padded * share * group_count * (rank + sources * block),
            bytes_accessed=2 * group_count * sources * span * share + 4 * experts * rank * share,
            transcendentals=0,
        ),
        name="adapter_columns",
    )(early, early_far, columns, swapped)

    home, arrived, lora_b = lax.optimization_barrier((home, arrived, lora_b))
    router_grad = jnp.sum(home, axis=0).T
    lora_a = parts[0].astype(jnp.float32)
    for part in arrived:
        lora_a = lora_a + part.astype(jnp.float32)
    return (hidden_grad, router_grad, lora_a, lora_b)


def local(*arrays):
    sources, groups = lax.axis_size("expert"), lax.axis_size("dp")
    span, width = arrays[0].shape
    top, (micro, experts, slots, units) = arrays[1].shape[1], arrays[3].shape
    even = sources % 4 == 0 and experts % 2 == 0 and width % (128 * groups) == 0 and units % groups == 0
    rank = arrays[5].shape[2]
    packs = width // groups % (2 * rank) == 0 and experts * rank % (width // groups) == 0
    packs = packs and 2 * top * span % (width // groups) == 0 and (width // groups) % span == 0
    exact = experts * sources <= 256
    if even and packs and exact and sources * span <= micro * experts * slots:
        return local_by_tokens(*arrays)
    return local_by_slots(*arrays)


def solution(mesh):
    in_specs = (
        P(("dp", "expert"), None),
        P(("dp", "expert"), None),
        P(("dp", "expert"), None),
        P(None, ("dp", "expert"), None, None),
        P("expert", None, None),
        P("expert", None, None),
        P("expert", None, None),
    )
    out_specs = (
        P(None, ("dp", "expert"), None, None),
        P(("dp", "expert"), None),
        P("expert", None, "dp"),
        P("expert", None, "dp"),
    )
    return jax.shard_map(local, mesh=mesh, in_specs=in_specs, out_specs=out_specs, check_vma=False)
```

```python
import functools

import jax
import jax.numpy as jnp
from jax import lax
from jax.experimental import pallas as pl
from jax.experimental.pallas import tpu as pltpu
from jax.sharding import PartitionSpec as P

adapter_scale = 2.0


def slot_rows(id_rows, experts, per_device, sources, capacity):
    onehot = (id_rows[:, :, None] == jnp.arange(experts, dtype=jnp.int32)[None, None, :]).astype(
        jnp.int32
    )
    before = jnp.sum(jnp.cumsum(onehot, axis=1) * onehot, axis=2) - 1
    target_dev = id_rows // per_device
    target_slot = id_rows % per_device
    return (target_slot * sources + target_dev) * capacity + before


def pick_rows(source, indices):
    return source[indices]


def dispatch_buffers(grad_rows, weight_rows, send_rows, top_count, buffer_len):
    entry_count = send_rows.shape[1]
    token_count = grad_rows.shape[1]
    filler = jnp.full((buffer_len,), entry_count, jnp.int32)

    def invert(rows):
        return filler.at[rows].set(jnp.arange(entry_count, dtype=jnp.int32))

    table = jax.vmap(invert)(send_rows)
    padded_grad = jnp.concatenate(
        [grad_rows, jnp.zeros((grad_rows.shape[0], 1, grad_rows.shape[2]), grad_rows.dtype)], axis=1
    )
    padded_weight = jnp.concatenate(
        [weight_rows, jnp.zeros((weight_rows.shape[0], 1), weight_rows.dtype)], axis=1
    )
    token_pick = jnp.where(table < entry_count, table // top_count, token_count)
    sent_grad = jax.vmap(pick_rows)(padded_grad, token_pick)
    sent_weight = jax.vmap(pick_rows)(padded_weight, table)
    return (sent_grad, sent_weight)


def expert_rows_view(
    received_gradient,
    received_weight,
    retained_rows,
    frozen_down_weight,
    adapter_input_map,
    adapter_output_map,
):
    frozen_term = jnp.einsum(
        "mesd,efd->mesf", received_gradient, frozen_down_weight, preferred_element_type=jnp.float32
    )
    across_product = jnp.einsum(
        "hati,aki->hatk", received_gradient, adapter_output_map, preferred_element_type=jnp.float32
    ).astype(jnp.bfloat16)
    low_rank_state = jnp.einsum(
        "ptqv,tgv->ptqg", across_product, adapter_input_map, preferred_element_type=jnp.float32
    )
    capacity_slot_weight = received_weight.astype(jnp.float32)[..., None]
    hidden_state_gradient = (
        capacity_slot_weight * (frozen_term + adapter_scale * low_rank_state)
    ).astype(jnp.bfloat16)
    down_mapping = jnp.einsum(
        "lkgu,kup->lkgp", retained_rows, adapter_input_map, preferred_element_type=jnp.float32
    ).astype(jnp.bfloat16)
    complete_term = jnp.sum(frozen_term * retained_rows.astype(jnp.float32), axis=-1)
    adapter_term = jnp.einsum(
        "mesr,mesr->mes", down_mapping, across_product, preferred_element_type=jnp.float32
    )
    routing_rows = complete_term + adapter_scale * adapter_term
    scaled_gradient = (capacity_slot_weight * received_gradient).astype(jnp.bfloat16)
    scaled_across_product = (capacity_slot_weight * across_product.astype(jnp.float32)).astype(
        jnp.bfloat16
    )
    adapter_output_gradient = adapter_scale * jnp.einsum(
        "mesr,mesd->erd", down_mapping, scaled_gradient, preferred_element_type=jnp.float32
    )
    adapter_input_gradient = adapter_scale * jnp.einsum(
        "mesr,mesf->erf", scaled_across_product, retained_rows, preferred_element_type=jnp.float32
    )
    return (hidden_state_gradient, routing_rows, adapter_input_gradient, adapter_output_gradient)


def local_by_slots(
    output_gradient,
    chosen_expert_index,
    routing_gate_weight,
    hidden,
    frozen_down_weight,
    adapter_input_map,
    adapter_output_map,
):
    sources = lax.axis_size("expert")
    per_device = frozen_down_weight.shape[0]
    experts = per_device * sources
    micro_count = hidden.shape[0]
    slot_count = hidden.shape[2]
    capacity = slot_count // sources
    top_count = chosen_expert_index.shape[1]
    model_width = output_gradient.shape[1]
    buffer_len = experts * capacity
    grad_rows = output_gradient.reshape(micro_count, -1, model_width)
    id_rows = chosen_expert_index.reshape(micro_count, -1)
    weight_rows = routing_gate_weight.reshape(micro_count, -1)
    send_rows = slot_rows(id_rows, experts, per_device, sources, capacity)
    sent_grad, sent_weight = dispatch_buffers(
        grad_rows, weight_rows, send_rows, top_count, buffer_len
    )
    sent_grad = sent_grad.reshape(micro_count, per_device, sources, capacity, model_width)
    sent_weight = sent_weight.reshape(micro_count, per_device, sources, capacity)
    received_gradient, received_weight = (
        lax.all_to_all(sent_grad, "expert", split_axis=2, concat_axis=2, tiled=True),
        lax.all_to_all(sent_weight, "expert", split_axis=2, concat_axis=2, tiled=True),
    )
    received_gradient = received_gradient.reshape(micro_count, per_device, slot_count, model_width)
    received_weight = received_weight.reshape(micro_count, per_device, slot_count)
    hidden_grad, routing_rows, adapter_input_gradient, adapter_output_gradient = expert_rows_view(
        received_gradient,
        received_weight,
        hidden,
        frozen_down_weight,
        adapter_input_map,
        adapter_output_map,
    )
    router_home = lax.all_to_all(
        routing_rows.reshape(micro_count, per_device, sources, capacity),
        "expert",
        split_axis=2,
        concat_axis=2,
        tiled=True,
    )
    router_flat = router_home.reshape(micro_count, buffer_len)
    router_grad = jax.vmap(pick_rows)(router_flat, send_rows).reshape(-1, top_count)
    share_a, share_b = (
        lax.psum_scatter(adapter_input_gradient, "dp", scatter_dimension=2, tiled=True),
        lax.psum_scatter(adapter_output_gradient, "dp", scatter_dimension=2, tiled=True),
    )
    return (hidden_grad, router_grad, share_a, share_b)


def pad_rows(count):
    return -(-count // 16) * 16


def read_names(rows, span, top):
    wide = rows.astype(jnp.float32)
    per = wide.shape[1] // span
    lines = [
        wide[k // per : k // per + 1, (k % per) * span : (k % per + 1) * span]
        for k in range(2 * top)
    ]
    return lines[:top], lines[top:]


def slot_codes(names, first, capacity, experts, micro):
    sources = len(names)
    span = names[0][0][0].shape[1]
    block = span // micro
    number = lax.broadcasted_iota(jnp.int32, (experts, span), 0).astype(jnp.float32) + first
    from_row = lax.broadcasted_iota(jnp.int32, (span, span), 0)
    to_row = lax.broadcasted_iota(jnp.int32, (span, span), 1)
    earlier = jnp.where(
        (from_row // block == to_row // block) & (from_row < to_row), 1.0, 0.0
    ).astype(jnp.bfloat16)
    codes, gates = [], []
    for j in range(sources):
        named = jnp.zeros((experts, span), jnp.float32)
        gate = jnp.zeros((experts, span), jnp.float32)
        for name, weight in zip(*names[j]):
            hit = name == number
            named = jnp.where(hit, 1.0, named)
            gate = jnp.where(hit, weight, gate)
        before = jnp.dot(named.astype(jnp.bfloat16), earlier, preferred_element_type=jnp.float32)
        codes.append(jnp.where(named > 0.0, before + float(j * capacity), -1.0))
        gates.append(gate)

    def arrange(values):
        half = sources // 2
        return [
            [
                jnp.concatenate(
                    [c[:, m * block : (m + 1) * block] for c in values[h * half : (h + 1) * half]],
                    axis=1,
                )
                for h in range(2)
            ]
            for m in range(micro)
        ]

    return arrange(codes), arrange(gates)


def slot_windows(slots):
    half = slots // 2
    return [(h * half // 8 * 8, -(-(h + 1) * half // 8) * 8) for h in range(2)]


def slot_iota(window, lanes):
    shape = (window[1] - window[0], lanes)
    return lax.broadcasted_iota(jnp.int32, shape, 0).astype(jnp.float32) + float(window[0])


def join_windows(first_part, second_part, windows, padded, axis):
    (_, end), (start, last) = windows

    def rows(values, low, high):
        return lax.slice_in_dim(values, low, high, axis=axis)

    parts = [rows(first_part, 0, start)]
    if end > start:
        parts.append(rows(first_part, start, end) + rows(second_part, 0, end - start))
    parts.append(rows(second_part, end - start, last - start))
    if padded > last:
        shape = list(first_part.shape)
        shape[axis] = padded - last
        parts.append(jnp.zeros(shape, first_part.dtype))
    return jnp.concatenate(parts, axis=axis)


contract_last = (((1,), (1,)), ((), ()))
contract_first = (((0,), (0,)), ((), ()))


def shard_owner(index, sources):
    pairs = sources // 2
    me = lax.axis_index("expert")
    column, core = me // 2, lax.rem(me, 2)
    place = jnp.where(lax.rem(column, 2) == 0, column // 2, pairs - 1 - column // 2)
    place = lax.rem(place - index % pairs + pairs, pairs)
    column = jnp.where(2 * place < pairs, 2 * place, 2 * (pairs - 1 - place) + 1)
    return 2 * column + (core if index < pairs else 1 - core)


def payload_kernel(share, dy_ref, index_ref, gate_ref, *outs):
    top, span = index_ref.shape
    part = outs[0].shape[1]
    per = share // span
    names, gates = index_ref[...].astype(jnp.float32), gate_ref[...].astype(jnp.float32)
    lines = [names[k : k + 1] for k in range(top)] + [gates[k : k + 1] for k in range(top)]
    rows = [jnp.concatenate(lines[k : k + per], axis=1) for k in range(0, 2 * top, per)]
    spare = outs[0].shape[0] - span - len(rows)
    if spare:
        rows.append(jnp.zeros((spare, share), jnp.float32))
    below = jnp.concatenate(rows, axis=0).astype(jnp.bfloat16)
    for c, out in enumerate(outs):
        out[:span] = dy_ref[:, c * part : (c + 1) * part]
        for at in range(0, part, share):
            out[span:, at : at + share] = below


def expert_kernel(capacity, group_count, shards, chunks, *refs):
    token_refs = refs[: shards * chunks]
    refs = refs[shards * chunks :]
    hidden_hbm, u_hbm, weight_hbm, amap_hbm, bmap_hbm, hg_ref, rk_ref = refs[:7]
    la_outs = refs[7 : 7 + group_count]
    scratch = refs[7 + group_count :]
    dy_s, wb_s, rows_s, y_s, code_s, gate_s, back_s, la_s = scratch[:8]
    hidden_ref, u_ref, amap_ref, dy_sem, w_sem, b_sem, la_sem, in_sem = scratch[8:]
    top, span = rk_ref.shape[1:]
    micro, experts, slots, units = hidden_ref.shape
    rank = amap_ref.shape[1]
    width = dy_s.shape[2]
    block = span // micro
    padded = rows_s.shape[1] // micro
    first = (lax.axis_index("expert") * experts).astype(jnp.float32)

    part = width // chunks
    owners = [shard_owner(i, shards) for i in range(shards)]
    token_copies = [
        pltpu.make_async_copy(
            token_refs[i * chunks + c],
            dy_s.at[owners[i], :, pl.ds(c * part, part)],
            dy_sem.at[i, c],
        )
        for i in range(shards)
        for c in range(chunks)
    ]
    for copy in token_copies:
        copy.start()

    def weight_copies(x, slot):
        return (
            pltpu.make_async_copy(weight_hbm.at[x], wb_s.at[slot, pl.ds(0, units)], w_sem.at[x]),
            pltpu.make_async_copy(bmap_hbm.at[x], wb_s.at[slot, pl.ds(units, rank)], b_sem.at[x]),
        )

    half = experts // 2
    batch = 2 if half % 2 == 0 else 1
    groups = half // batch

    def members(step):
        at = [step * batch + i for i in range(batch)]
        picked = [(p, p, slice(0, rank)) for p in at]
        return picked + [(p + half, p, slice(rank, 2 * rank)) for p in at]

    def slot_at(step, i):
        return lax.rem(step, wb_s.shape[0] // (2 * batch)) * 2 * batch + i

    def request_weights(step):
        for i, (x, _, _) in enumerate(members(step)):
            for copy in weight_copies(x, slot_at(step, i)):
                copy.start()

    late_copies = [
        pltpu.make_async_copy(source, target, in_sem.at[k])
        for k, (source, target) in enumerate(
            [(hidden_hbm, hidden_ref), (u_hbm, u_ref), (amap_hbm, amap_ref)]
        )
    ]

    for copy in token_copies:
        copy.wait()
    request_weights(0)
    for copy in late_copies:
        copy.start()
    names = [
        read_names(dy_s[i, span:, width - width // group_count :], span, top) for i in range(shards)
    ]
    codes, gates = slot_codes(names, first, capacity, experts, micro)
    if groups > 1:
        request_weights(1)
    windows = slot_windows(slots)
    lanes_of = shards // 2 * block
    slot_of = [slot_iota(window, lanes_of) for window in windows]
    picks = []
    for m in range(micro):
        chosen = [[], []]
        for h in range(2):
            code_s[m, h] = codes[m][h]
        for x in range(experts):
            sums = []
            for h in range(2):
                hit = codes[m][h][x : x + 1, :] == slot_of[h]
                chosen[h].append(jnp.where(hit, 1.0, 0.0))
                sums.append(
                    jnp.sum(
                        jnp.where(hit, gates[m][h][x : x + 1, :], 0.0), axis=1, keepdims=True
                    )
                )
            gate_s[x, m * padded : (m + 1) * padded, :] = join_windows(
                sums[0], sums[1], windows, padded, 0
            )
        picks.append([jnp.concatenate(c, axis=0).astype(jnp.bfloat16) for c in chosen])

    tile = 512 if width % 512 == 0 else width
    for m in range(micro):
        for n in range(width // tile):
            cols = slice(n * tile, (n + 1) * tile)
            parts = []
            for h in range(2):
                tokens = jnp.concatenate(
                    [
                        dy_s[j, m * block : (m + 1) * block, cols]
                        for j in range(h * shards // 2, (h + 1) * shards // 2)
                    ],
                    axis=0,
                )
                rows = jnp.dot(picks[m][h], tokens, preferred_element_type=jnp.float32)
                parts.append(rows.reshape(experts, -1, tile))
            rows_s[:, m * padded : (m + 1) * padded, cols] = join_windows(
                parts[0], parts[1], windows, padded, 1
            ).astype(jnp.bfloat16)

    def main_products(step):
        xs = [x for x, _, _ in members(step)]
        for i, x in enumerate(xs):
            for copy in weight_copies(x, slot_at(step, i)):
                copy.wait()

        @pl.when(step + 2 < groups)
        def _():
            request_weights(step + 2)

        return [
            lax.dot_general(
                rows_s[x],
                wb_s[slot_at(step, i)],
                contract_last,
                preferred_element_type=jnp.float32,
            )
            for i, x in enumerate(xs)
        ]

    def keep_products(step, products):
        for (x, _, _), product in zip(members(step), products):
            y_s[x] = product

    share = units // group_count
    filler = jnp.zeros((padded - slots, units), jnp.float32)

    def small_steps(step):
        picked = members(step)
        xs = [x for x, _, _ in picked]
        mains = [y_s[x, :, :units] for x in xs]
        vs = [y_s[x, :, units:].astype(jnp.bfloat16) for x in xs]
        lows = [
            jnp.dot(v, amap_ref[x], preferred_element_type=jnp.float32) for v, x in zip(vs, xs)
        ]
        gates_x = [gate_s[x] for x in xs]
        wide = [
            jnp.concatenate(
                [
                    part
                    for m in range(micro)
                    for part in (hidden_ref[m, x].astype(jnp.float32), filler)
                ],
                axis=0,
            )
            for x in xs
        ]
        v_wide = [v.astype(jnp.float32) for v in vs]
        ws = [(gate * v).astype(jnp.bfloat16) for gate, v in zip(gates_x, v_wide)]
        las = [
            lax.dot_general(
                w, held.astype(jnp.bfloat16), contract_first, preferred_element_type=jnp.float32
            )
            for w, held in zip(ws, wide)
        ]
        routed = [
            jnp.sum(main * held, axis=1, keepdims=True)
            + adapter_scale
            * jnp.sum(u_ref[p, :, lanes].astype(jnp.float32) * v, axis=1, keepdims=True)
            for main, held, v, (_, p, lanes) in zip(mains, wide, v_wide, picked)
        ]
        grads = [
            (gate * (main + adapter_scale * low)).astype(jnp.bfloat16)
            for gate, main, low in zip(gates_x, mains, lows)
        ]
        for x, grad, la, back in zip(xs, grads, las, routed):
            for m in range(micro):
                hg_ref[m, x] = grad[m * padded : m * padded + slots]
                for h, (low, high) in enumerate(windows):
                    hit = code_s[m, h, pl.ds(x, 1), :] == slot_of[h]
                    rows = back[m * padded + low : m * padded + high]
                    back_s[m, h, pl.ds(x, 1), :] = jnp.sum(
                        jnp.where(hit, rows, 0.0), axis=0, keepdims=True
                    )
            for k in range(group_count):
                la_s[k, x] = (adapter_scale * la[:, k * share : (k + 1) * share]).astype(
                    la_s.dtype
                )

    def both_steps(step, carry):
        products = main_products(step)
        small_steps(step - 1)
        keep_products(step, products)
        return carry

    keep_products(0, main_products(0))
    for copy in late_copies:
        copy.wait()
    lax.fori_loop(1, groups, both_steps, 0)
    small_steps(groups - 1)

    group = lax.axis_index("dp")
    la_copies = [
        pltpu.make_async_copy(
            la_s.at[lax.rem(group + s, group_count)], la_outs[s], la_sem.at[s]
        )
        for s in range(group_count)
    ]
    for copy in la_copies:
        copy.start()
    number = lax.broadcasted_iota(jnp.int32, (experts, span), 0).astype(jnp.float32) + first
    for j in range(shards):
        h, k = j // (shards // 2), j % (shards // 2)
        back = jnp.concatenate(
            [back_s[m, h, :, k * block : (k + 1) * block] for m in range(micro)], axis=1
        )
        found = [
            jnp.sum(jnp.where(name == number, back, 0.0), axis=0, keepdims=True)
            for name in names[j][0]
        ]
        rk_ref[j] = jnp.concatenate(found, axis=0)
    for copy in la_copies:
        copy.wait()


def adapter_kernel(capacity, micro, span, top, group_count, shards, *refs):
    pairs = shards // 2
    early_ref, early_far_ref, near_ref, far_ref = refs[:4]
    lb_hbm, tok_s, q_s, u_refs, lb_ref, sem, u_sem, lb_sem = refs[4:]
    experts, rank, share = lb_ref.shape
    lb_copies = [
        pltpu.make_async_copy(lb_ref.at[x], lb_hbm.at[x], lb_sem.at[x]) for x in range(experts)
    ]
    blocks, tall = u_refs.shape[1:3]
    padded = tall // micro
    block = span // micro
    first = (lax.axis_index("expert") * experts).astype(jnp.float32)
    group = lax.axis_index("dp")
    owners = [shard_owner(i, shards) for i in range(shards)]
    copies, u_copies = [], []
    for g in range(group_count):
        home = lax.rem(group - g + group_count, group_count)
        for i in range(shards):
            if i % pairs:
                source = (far_ref if i >= pairs else near_ref).at[home, i % pairs - 1]
            elif i:
                source = early_far_ref.at[home]
            else:
                source = early_ref.at[home, pl.ds(blocks * tall, tok_s.shape[2])]
            copies.append(pltpu.make_async_copy(source, tok_s.at[g, owners[i]], sem.at[g, i]))
        for k in range(blocks):
            source = early_ref.at[home, pl.ds(k * tall, tall)]
            u_copies.append(pltpu.make_async_copy(source, u_refs.at[g, k], u_sem.at[g, k]))
    for copy in copies + u_copies:
        copy.start()
    slots = capacity * shards
    windows = slot_windows(slots)
    slot_of = [slot_iota(window, shards // 2 * block) for window in windows]
    for g in range(group_count):
        for copy in copies[g * shards : (g + 1) * shards]:
            copy.wait()
        names = [read_names(tok_s[g, i, span:, :], span, top) for i in range(shards)]
        codes, gates = slot_codes(names, first, capacity, experts, micro)
        for m in range(micro):
            parts = []
            for h in range(2):
                picks = jnp.concatenate(
                    [
                        jnp.where(
                            codes[m][h][x : x + 1, :] == slot_of[h],
                            gates[m][h][x : x + 1, :],
                            0.0,
                        )
                        for x in range(experts)
                    ],
                    axis=0,
                ).astype(jnp.bfloat16)
                tokens = jnp.concatenate(
                    [
                        tok_s[g, j, m * block : (m + 1) * block, :]
                        for j in range(h * shards // 2, (h + 1) * shards // 2)
                    ],
                    axis=0,
                )
                rows = jnp.dot(picks, tokens, preferred_element_type=jnp.float32)
                parts.append(rows.reshape(experts, -1, share))
            q = join_windows(parts[0], parts[1], windows, padded, 1).astype(jnp.bfloat16)
            at = g * tall + m * padded
            q_s[:, at : at + padded, :] = q
    for copy in u_copies:
        copy.wait()
    half = experts // 2
    for x in range(half):
        lane = x // blocks * 2 * rank
        both = jnp.concatenate(
            [u_refs[g, x % blocks, :, lane : lane + 2 * rank] for g in range(group_count)], axis=0
        )
        lb_ref[x] = adapter_scale * lax.dot_general(
            both[:, :rank], q_s[x], contract_first, preferred_element_type=jnp.float32
        )
        lb_ref[x + half] = adapter_scale * lax.dot_general(
            both[:, rank:], q_s[x + half], contract_first, preferred_element_type=jnp.float32
        )
        lb_copies[x].start()
        lb_copies[x + half].start()
    for copy in lb_copies:
        copy.wait()


def ring_order(count):
    return list(range(0, count, 2)) + list(range(1, count, 2))[::-1]


def local_by_tokens(
    output_gradient,
    chosen_expert_index,
    routing_gate_weight,
    hidden,
    frozen_down_weight,
    adapter_input_map,
    adapter_output_map,
):
    sources = lax.axis_size("expert")
    group_count = lax.axis_size("dp")
    micro, experts, slots, units = hidden.shape
    span, top = chosen_expert_index.shape
    width = output_gradient.shape[1]
    rank = adapter_input_map.shape[2]
    capacity = slots // sources
    block = span // micro
    padded = pad_rows(slots)
    share = width // group_count
    pairs = sources // 2
    chunks = 2 if group_count % 2 == 0 else 1
    part = width // chunks

    order = ring_order(pairs)
    place = {z: i for i, z in enumerate(order)}
    ring = [
        (2 * z + c, 2 * order[(place[z] + 1) % pairs] + c) for z in range(pairs) for c in range(2)
    ]
    swap = [(e, e ^ 1) for e in range(sources)]

    amap = jnp.swapaxes(adapter_input_map, 1, 2)
    u = jnp.einsum("mesk,exk->emsx", hidden, amap, preferred_element_type=jnp.float32)
    u = u.astype(jnp.bfloat16)
    u = jnp.pad(u, ((0, 0), (0, 0), (0, padded - slots), (0, 0))).reshape(
        2, experts // 2, micro * padded, rank
    )
    u = lax.optimization_barrier(jnp.concatenate([u[0], u[1]], axis=-1))

    def shift_groups(array, by):
        return lax.ppermute(
            array, "dp", [(d, (d + by) % group_count) for d in range(group_count)]
        )

    def swap_partners(array):
        return lax.ppermute(array, "expert", swap)

    def exchange_columns(chosen):
        def columns(pieces, g):
            at = g * share % part
            return pieces[g * share // part][:, at : at + share]

        return jnp.stack(
            [jnp.stack([columns(pieces, g) for pieces in chosen]) for g in range(group_count)]
        )

    def across_groups(array):
        return lax.all_to_all(array, "dp", split_axis=0, concat_axis=0, tiled=True)

    others = range(1, group_count)
    lines = 2 * top * span // share
    extra = -(-lines // 8) * 8
    vmem = pl.BlockSpec(memory_space=pltpu.VMEM)
    sent = pl.pallas_call(
        functools.partial(payload_kernel, share),
        out_shape=[jax.ShapeDtypeStruct((span + extra, part), jnp.bfloat16)] * chunks,
        in_specs=[vmem] * 3,
        out_specs=[vmem] * chunks,
        compiler_params=pltpu.CompilerParams(vmem_limit_bytes=58 * 1024 * 1024),
        name="ring_payload",
    )(output_gradient, chosen_expert_index.T, routing_gate_weight.T)

    near, far = [list(sent)], []
    blocks = experts // 2 * 2 * rank // share
    packed = jnp.concatenate(
        [u[k * blocks : (k + 1) * blocks] for k in range(experts // 2 // blocks)], axis=-1
    ).reshape(blocks * micro * padded, share)
    early = jnp.stack(
        [
            jnp.concatenate(
                [packed, sent[g * share // part][:, g * share % part :][:, :share]], axis=0
            )
            for g in range(group_count)
        ]
    )
    early = across_groups(early)
    early_far = swap_partners(early[:, blocks * micro * padded :])
    for step in range(pairs - 1):
        if step > 1:
            tied = [
                lax.optimization_barrier((near[step][c], [shard[c] for shard in far]))
                for c in range(chunks)
            ]
            near[step] = [a for a, _ in tied]
            far = [[b[k] for _, b in tied] for k in range(len(far))]
        near.append([lax.ppermute(piece, "expert", ring) for piece in near[step]])
        far.append([swap_partners(piece) for piece in near[step]])
    far.append([swap_partners(piece) for piece in near[-1]])
    columns = exchange_columns(near[1:])
    columns, early, early_far, far[-2:] = lax.optimization_barrier(
        (columns, early, early_far, far[-2:])
    )
    columns = across_groups(columns)
    pieces = [piece for shard in near + far for piece in shard]

    anywhere = pl.BlockSpec(memory_space=pl.ANY)
    kept = 3 * (4 if experts % 4 == 0 else 2)
    part_a = jax.ShapeDtypeStruct((experts, rank, units // group_count), jnp.bfloat16)
    hidden_grad, routed, *parts = pl.pallas_call(
        functools.partial(expert_kernel, capacity, group_count, sources, chunks),
        out_shape=(
            jax.ShapeDtypeStruct(hidden.shape, jnp.bfloat16),
            jax.ShapeDtypeStruct((sources, top, span), jnp.float32),
        )
        + (part_a,) * group_count,
        in_specs=[anywhere] * (sources * chunks) + [anywhere] * 5,
        out_specs=(vmem,) * 2 + (anywhere,) * group_count,
        scratch_shapes=[
            pltpu.VMEM((sources, span + extra, width), jnp.bfloat16),
            pltpu.VMEM((min(experts, kept), units + rank, width), jnp.bfloat16),
            pltpu.VMEM((experts, micro * padded, width), jnp.bfloat16),
            pltpu.VMEM((experts, micro * padded, units + rank), jnp.float32),
            pltpu.VMEM((micro, 2, experts, sources // 2 * block), jnp.float32),
            pltpu.VMEM((experts, micro * padded, 1), jnp.float32),
            pltpu.VMEM((micro, 2, experts, sources // 2 * block), jnp.float32),
            pltpu.VMEM((group_count, experts, rank, units // group_count), jnp.bfloat16),
            pltpu.VMEM(hidden.shape, jnp.bfloat16),
            pltpu.VMEM(u.shape, jnp.bfloat16),
            pltpu.VMEM(amap.shape, jnp.bfloat16),
            pltpu.SemaphoreType.DMA((sources, chunks)),
            pltpu.SemaphoreType.DMA((experts,)),
            pltpu.SemaphoreType.DMA((experts,)),
            pltpu.SemaphoreType.DMA((group_count,)),
            pltpu.SemaphoreType.DMA((3,)),
        ],
        compiler_params=pltpu.CompilerParams(vmem_limit_bytes=58 * 1024 * 1024),
        cost_estimate=pl.CostEstimate(
            flops=2 * experts * micro * padded * width * (units + rank + sources * block),
            bytes_accessed=2 * experts * width * (units + rank) + 2 * sources * span * width,
            transcendentals=0,
        ),
        name="expert_rows",
    )(*pieces, hidden, u, frozen_down_weight, amap, adapter_output_map)

    columns, parts, routed = lax.optimization_barrier((columns, parts, routed))
    swapped = swap_partners(columns)
    arrived = [shift_groups(parts[s], s) for s in others]
    swapped, routed = lax.optimization_barrier((swapped, routed))
    home = lax.all_to_all(routed, "expert", split_axis=0, concat_axis=0, tiled=True)

    lora_b = pl.pallas_call(
        functools.partial(adapter_kernel, capacity, micro, span, top, group_count, sources),
        out_shape=jax.ShapeDtypeStruct((experts, rank, share), jnp.float32),
        in_specs=[anywhere] * 4,
        out_specs=anywhere,
        scratch_shapes=[
            pltpu.VMEM((group_count, sources, span + extra, share), jnp.bfloat16),
            pltpu.VMEM((experts, group_count * micro * padded, share), jnp.bfloat16),
            pltpu.VMEM((group_count, blocks, micro * padded, share), jnp.bfloat16),
            pltpu.VMEM((experts, rank, share), jnp.float32),
            pltpu.SemaphoreType.DMA((group_count, sources)),
            pltpu.SemaphoreType.DMA((group_count, blocks)),
            pltpu.SemaphoreType.DMA((experts,)),
        ],
        compiler_params=pltpu.CompilerParams(vmem_limit_bytes=58 * 1024 * 1024),
        cost_estimate=pl.CostEstimate(
            flops=2 * experts * micro * padded * share * group_count * (rank + sources * block),
            bytes_accessed=2 * group_count * sources * span * share + 4 * experts * rank * share,
            transcendentals=0,
        ),
        name="adapter_columns",
    )(early, early_far, columns, swapped)

    home, arrived, lora_b = lax.optimization_barrier((home, arrived, lora_b))
    router_grad = jnp.sum(home, axis=0).T
    lora_a = parts[0].astype(jnp.float32)
    for part in arrived:
        lora_a = lora_a + part.astype(jnp.float32)
    return (hidden_grad, router_grad, lora_a, lora_b)


def local(*arrays):
    sources, groups = lax.axis_size("expert"), lax.axis_size("dp")
    span, width = arrays[0].shape
    top, (micro, experts, slots, units) = arrays[1].shape[1], arrays[3].shape
    even = sources % 4 == 0 and experts % 2 == 0 and width % (128 * groups) == 0 and units % groups == 0
    rank = arrays[5].shape[2]
    packs = width // groups % (2 * rank) == 0 and experts * rank % (width // groups) == 0
    packs = packs and 2 * top * span % (width // groups) == 0 and (width // groups) % span == 0
    exact = experts * sources <= 256
    if even and packs and exact and sources * span <= micro * experts * slots:
        return local_by_tokens(*arrays)
    return local_by_slots(*arrays)


def solution(mesh):
    in_specs = (
        P(("dp", "expert"), None),
        P(("dp", "expert"), None),
        P(("dp", "expert"), None),
        P(None, ("dp", "expert"), None, None),
        P("expert", None, None),
        P("expert", None, None),
        P("expert", None, None),
    )
    out_specs = (
        P(None, ("dp", "expert"), None, None),
        P(("dp", "expert"), None),
        P("expert", None, "dp"),
        P("expert", None, "dp"),
    )
    return jax.shard_map(local, mesh=mesh, in_specs=in_specs, out_specs=out_specs, check_vma=False)
```

```python
import functools

import jax
import jax.numpy as jnp
from jax import lax
from jax.experimental import pallas as pl
from jax.experimental.pallas import tpu as pltpu
from jax.sharding import PartitionSpec as P

adapter_scale = 2.0


def slot_rows(id_rows, experts, per_device, sources, capacity):
    onehot = (id_rows[:, :, None] == jnp.arange(experts, dtype=jnp.int32)[None, None, :]).astype(
        jnp.int32
    )
    before = jnp.sum(jnp.cumsum(onehot, axis=1) * onehot, axis=2) - 1
    target_dev = id_rows // per_device
    target_slot = id_rows % per_device
    return (target_slot * sources + target_dev) * capacity + before


def pick_rows(source, indices):
    return source[indices]


def dispatch_buffers(grad_rows, weight_rows, send_rows, top_count, buffer_len):
    entry_count = send_rows.shape[1]
    token_count = grad_rows.shape[1]
    filler = jnp.full((buffer_len,), entry_count, jnp.int32)

    def invert(rows):
        return filler.at[rows].set(jnp.arange(entry_count, dtype=jnp.int32))

    table = jax.vmap(invert)(send_rows)
    padded_grad = jnp.concatenate(
        [grad_rows, jnp.zeros((grad_rows.shape[0], 1, grad_rows.shape[2]), grad_rows.dtype)], axis=1
    )
    padded_weight = jnp.concatenate(
        [weight_rows, jnp.zeros((weight_rows.shape[0], 1), weight_rows.dtype)], axis=1
    )
    token_pick = jnp.where(table < entry_count, table // top_count, token_count)
    sent_grad = jax.vmap(pick_rows)(padded_grad, token_pick)
    sent_weight = jax.vmap(pick_rows)(padded_weight, table)
    return (sent_grad, sent_weight)


def expert_rows_view(
    received_gradient,
    received_weight,
    retained_rows,
    frozen_down_weight,
    adapter_input_map,
    adapter_output_map,
):
    frozen_term = jnp.einsum(
        "mesd,efd->mesf", received_gradient, frozen_down_weight, preferred_element_type=jnp.float32
    )
    across_product = jnp.einsum(
        "hati,aki->hatk", received_gradient, adapter_output_map, preferred_element_type=jnp.float32
    ).astype(jnp.bfloat16)
    low_rank_state = jnp.einsum(
        "ptqv,tgv->ptqg", across_product, adapter_input_map, preferred_element_type=jnp.float32
    )
    capacity_slot_weight = received_weight.astype(jnp.float32)[..., None]
    hidden_state_gradient = (
        capacity_slot_weight * (frozen_term + adapter_scale * low_rank_state)
    ).astype(jnp.bfloat16)
    down_mapping = jnp.einsum(
        "lkgu,kup->lkgp", retained_rows, adapter_input_map, preferred_element_type=jnp.float32
    ).astype(jnp.bfloat16)
    complete_term = jnp.sum(frozen_term * retained_rows.astype(jnp.float32), axis=-1)
    adapter_term = jnp.einsum(
        "mesr,mesr->mes", down_mapping, across_product, preferred_element_type=jnp.float32
    )
    routing_rows = complete_term + adapter_scale * adapter_term
    scaled_gradient = (capacity_slot_weight * received_gradient).astype(jnp.bfloat16)
    scaled_across_product = (capacity_slot_weight * across_product.astype(jnp.float32)).astype(
        jnp.bfloat16
    )
    adapter_output_gradient = adapter_scale * jnp.einsum(
        "mesr,mesd->erd", down_mapping, scaled_gradient, preferred_element_type=jnp.float32
    )
    adapter_input_gradient = adapter_scale * jnp.einsum(
        "mesr,mesf->erf", scaled_across_product, retained_rows, preferred_element_type=jnp.float32
    )
    return (hidden_state_gradient, routing_rows, adapter_input_gradient, adapter_output_gradient)


def local_by_slots(
    output_gradient,
    chosen_expert_index,
    routing_gate_weight,
    hidden,
    frozen_down_weight,
    adapter_input_map,
    adapter_output_map,
):
    sources = lax.axis_size("expert")
    per_device = frozen_down_weight.shape[0]
    experts = per_device * sources
    micro_count = hidden.shape[0]
    slot_count = hidden.shape[2]
    capacity = slot_count // sources
    top_count = chosen_expert_index.shape[1]
    model_width = output_gradient.shape[1]
    buffer_len = experts * capacity
    grad_rows = output_gradient.reshape(micro_count, -1, model_width)
    id_rows = chosen_expert_index.reshape(micro_count, -1)
    weight_rows = routing_gate_weight.reshape(micro_count, -1)
    send_rows = slot_rows(id_rows, experts, per_device, sources, capacity)
    sent_grad, sent_weight = dispatch_buffers(
        grad_rows, weight_rows, send_rows, top_count, buffer_len
    )
    sent_grad = sent_grad.reshape(micro_count, per_device, sources, capacity, model_width)
    sent_weight = sent_weight.reshape(micro_count, per_device, sources, capacity)
    received_gradient, received_weight = (
        lax.all_to_all(sent_grad, "expert", split_axis=2, concat_axis=2, tiled=True),
        lax.all_to_all(sent_weight, "expert", split_axis=2, concat_axis=2, tiled=True),
    )
    received_gradient = received_gradient.reshape(micro_count, per_device, slot_count, model_width)
    received_weight = received_weight.reshape(micro_count, per_device, slot_count)
    hidden_grad, routing_rows, adapter_input_gradient, adapter_output_gradient = expert_rows_view(
        received_gradient,
        received_weight,
        hidden,
        frozen_down_weight,
        adapter_input_map,
        adapter_output_map,
    )
    router_home = lax.all_to_all(
        routing_rows.reshape(micro_count, per_device, sources, capacity),
        "expert",
        split_axis=2,
        concat_axis=2,
        tiled=True,
    )
    router_flat = router_home.reshape(micro_count, buffer_len)
    router_grad = jax.vmap(pick_rows)(router_flat, send_rows).reshape(-1, top_count)
    share_a, share_b = (
        lax.psum_scatter(adapter_input_gradient, "dp", scatter_dimension=2, tiled=True),
        lax.psum_scatter(adapter_output_gradient, "dp", scatter_dimension=2, tiled=True),
    )
    return (hidden_grad, router_grad, share_a, share_b)


def pad_rows(count):
    return -(-count // 16) * 16


def read_names(rows, span, top):
    wide = rows.astype(jnp.float32)
    per = wide.shape[1] // span
    lines = [
        wide[k // per : k // per + 1, (k % per) * span : (k % per + 1) * span]
        for k in range(2 * top)
    ]
    return lines[:top], lines[top:]


def slot_codes(names, first, capacity, experts, micro):
    sources = len(names)
    span = names[0][0][0].shape[1]
    block = span // micro
    number = lax.broadcasted_iota(jnp.int32, (experts, span), 0).astype(jnp.float32) + first
    from_row = lax.broadcasted_iota(jnp.int32, (span, span), 0)
    to_row = lax.broadcasted_iota(jnp.int32, (span, span), 1)
    earlier = jnp.where(
        (from_row // block == to_row // block) & (from_row < to_row), 1.0, 0.0
    ).astype(jnp.bfloat16)
    codes, gates = [], []
    for j in range(sources):
        named = jnp.zeros((experts, span), jnp.float32)
        gate = jnp.zeros((experts, span), jnp.float32)
        for name, weight in zip(*names[j]):
            hit = name == number
            named = jnp.where(hit, 1.0, named)
            gate = jnp.where(hit, weight, gate)
        before = jnp.dot(named.astype(jnp.bfloat16), earlier, preferred_element_type=jnp.float32)
        codes.append(jnp.where(named > 0.0, before + float(j * capacity), -1.0))
        gates.append(gate)

    def arrange(values):
        half = sources // 2
        return [
            [
                jnp.concatenate(
                    [c[:, m * block : (m + 1) * block] for c in values[h * half : (h + 1) * half]],
                    axis=1,
                )
                for h in range(2)
            ]
            for m in range(micro)
        ]

    return arrange(codes), arrange(gates)


def slot_windows(slots):
    half = slots // 2
    return [(h * half // 8 * 8, -(-(h + 1) * half // 8) * 8) for h in range(2)]


def slot_iota(window, lanes):
    shape = (window[1] - window[0], lanes)
    return lax.broadcasted_iota(jnp.int32, shape, 0).astype(jnp.float32) + float(window[0])


def join_windows(first_part, second_part, windows, padded, axis):
    (_, end), (start, last) = windows

    def rows(values, low, high):
        return lax.slice_in_dim(values, low, high, axis=axis)

    parts = [rows(first_part, 0, start)]
    if end > start:
        parts.append(rows(first_part, start, end) + rows(second_part, 0, end - start))
    parts.append(rows(second_part, end - start, last - start))
    if padded > last:
        shape = list(first_part.shape)
        shape[axis] = padded - last
        parts.append(jnp.zeros(shape, first_part.dtype))
    return jnp.concatenate(parts, axis=axis)


contract_last = (((1,), (1,)), ((), ()))
contract_first = (((0,), (0,)), ((), ()))


def shard_owner(index, sources):
    pairs = sources // 2
    me = lax.axis_index("expert")
    column, core = me // 2, lax.rem(me, 2)
    place = jnp.where(lax.rem(column, 2) == 0, column // 2, pairs - 1 - column // 2)
    place = lax.rem(place - index % pairs + pairs, pairs)
    column = jnp.where(2 * place < pairs, 2 * place, 2 * (pairs - 1 - place) + 1)
    return 2 * column + (core if index < pairs else 1 - core)


def payload_kernel(share, dy_ref, index_ref, gate_ref, *outs):
    top, span = index_ref.shape
    part = outs[0].shape[1]
    per = share // span
    names, gates = index_ref[...].astype(jnp.float32), gate_ref[...].astype(jnp.float32)
    lines = [names[k : k + 1] for k in range(top)] + [gates[k : k + 1] for k in range(top)]
    rows = [jnp.concatenate(lines[k : k + per], axis=1) for k in range(0, 2 * top, per)]
    spare = outs[0].shape[0] - span - len(rows)
    if spare:
        rows.append(jnp.zeros((spare, share), jnp.float32))
    below = jnp.concatenate(rows, axis=0).astype(jnp.bfloat16)
    for c, out in enumerate(outs):
        out[:span] = dy_ref[:, c * part : (c + 1) * part]
        for at in range(0, part, share):
            out[span:, at : at + share] = below


def expert_kernel(capacity, group_count, shards, chunks, *refs):
    token_refs = refs[: shards * chunks]
    refs = refs[shards * chunks :]
    hidden_hbm, u_hbm, weight_hbm, amap_hbm, bmap_hbm, hg_ref, rk_ref = refs[:7]
    la_outs = refs[7 : 7 + group_count]
    scratch = refs[7 + group_count :]
    dy_s, wb_s, rows_s, y_s, code_s, gate_s, back_s, la_s = scratch[:8]
    hidden_ref, u_ref, amap_ref, dy_sem, w_sem, b_sem, la_sem, in_sem = scratch[8:]
    top, span = rk_ref.shape[1:]
    micro, experts, slots, units = hidden_ref.shape
    rank = amap_ref.shape[1]
    width = dy_s.shape[2]
    block = span // micro
    padded = rows_s.shape[1] // micro
    first = (lax.axis_index("expert") * experts).astype(jnp.float32)

    part = width // chunks
    owners = [shard_owner(i, shards) for i in range(shards)]
    token_copies = [
        pltpu.make_async_copy(
            token_refs[i * chunks + c],
            dy_s.at[owners[i], :, pl.ds(c * part, part)],
            dy_sem.at[i, c],
        )
        for i in range(shards)
        for c in range(chunks)
    ]
    for copy in token_copies:
        copy.start()

    def weight_copies(x, slot):
        return (
            pltpu.make_async_copy(weight_hbm.at[x], wb_s.at[slot, pl.ds(0, units)], w_sem.at[x]),
            pltpu.make_async_copy(bmap_hbm.at[x], wb_s.at[slot, pl.ds(units, rank)], b_sem.at[x]),
        )

    half = experts // 2
    batch = 2 if half % 2 == 0 else 1
    groups = half // batch

    def members(step):
        at = [step * batch + i for i in range(batch)]
        picked = [(p, p, slice(0, rank)) for p in at]
        return picked + [(p + half, p, slice(rank, 2 * rank)) for p in at]

    def slot_at(step, i):
        return lax.rem(step, wb_s.shape[0] // (2 * batch)) * 2 * batch + i

    def request_weights(step):
        for i, (x, _, _) in enumerate(members(step)):
            for copy in weight_copies(x, slot_at(step, i)):
                copy.start()

    late_copies = [
        pltpu.make_async_copy(source, target, in_sem.at[k])
        for k, (source, target) in enumerate(
            [(hidden_hbm, hidden_ref), (u_hbm, u_ref), (amap_hbm, amap_ref)]
        )
    ]

    for copy in token_copies:
        copy.wait()
    request_weights(0)
    for copy in late_copies:
        copy.start()
    names = [
        read_names(dy_s[i, span:, width - width // group_count :], span, top) for i in range(shards)
    ]
    codes, gates = slot_codes(names, first, capacity, experts, micro)
    if groups > 1:
        request_weights(1)
    windows = slot_windows(slots)
    lanes_of = shards // 2 * block
    slot_of = [slot_iota(window, lanes_of) for window in windows]
    picks = []
    for m in range(micro):
        chosen = [[], []]
        for h in range(2):
            code_s[m, h] = codes[m][h]
        for x in range(experts):
            sums = []
            for h in range(2):
                hit = codes[m][h][x : x + 1, :] == slot_of[h]
                chosen[h].append(jnp.where(hit, 1.0, 0.0))
                sums.append(
                    jnp.sum(
                        jnp.where(hit, gates[m][h][x : x + 1, :], 0.0), axis=1, keepdims=True
                    )
                )
            gate_s[x, m * padded : (m + 1) * padded, :] = join_windows(
                sums[0], sums[1], windows, padded, 0
            )
        picks.append([jnp.concatenate(c, axis=0).astype(jnp.bfloat16) for c in chosen])

    tile = 512 if width % 512 == 0 else width
    for m in range(micro):
        for n in range(width // tile):
            cols = slice(n * tile, (n + 1) * tile)
            parts = []
            for h in range(2):
                tokens = jnp.concatenate(
                    [
                        dy_s[j, m * block : (m + 1) * block, cols]
                        for j in range(h * shards // 2, (h + 1) * shards // 2)
                    ],
                    axis=0,
                )
                rows = jnp.dot(picks[m][h], tokens, preferred_element_type=jnp.float32)
                parts.append(rows.reshape(experts, -1, tile))
            rows_s[:, m * padded : (m + 1) * padded, cols] = join_windows(
                parts[0], parts[1], windows, padded, 1
            ).astype(jnp.bfloat16)

    def main_products(step):
        xs = [x for x, _, _ in members(step)]
        for i, x in enumerate(xs):
            for copy in weight_copies(x, slot_at(step, i)):
                copy.wait()

        @pl.when(step + 2 < groups)
        def _():
            request_weights(step + 2)

        return [
            lax.dot_general(
                rows_s[x],
                wb_s[slot_at(step, i)],
                contract_last,
                preferred_element_type=jnp.float32,
            )
            for i, x in enumerate(xs)
        ]

    def keep_products(step, products):
        for (x, _, _), product in zip(members(step), products):
            y_s[x] = product

    share = units // group_count
    filler = jnp.zeros((padded - slots, units), jnp.float32)

    def small_steps(step):
        picked = members(step)
        xs = [x for x, _, _ in picked]
        mains = [y_s[x, :, :units] for x in xs]
        vs = [y_s[x, :, units:].astype(jnp.bfloat16) for x in xs]
        lows = [
            jnp.dot(v, amap_ref[x], preferred_element_type=jnp.float32) for v, x in zip(vs, xs)
        ]
        gates_x = [gate_s[x] for x in xs]
        wide = [
            jnp.concatenate(
                [
                    part
                    for m in range(micro)
                    for part in (hidden_ref[m, x].astype(jnp.float32), filler)
                ],
                axis=0,
            )
            for x in xs
        ]
        v_wide = [v.astype(jnp.float32) for v in vs]
        ws = [(gate * v).astype(jnp.bfloat16) for gate, v in zip(gates_x, v_wide)]
        las = [
            lax.dot_general(
                w, held.astype(jnp.bfloat16), contract_first, preferred_element_type=jnp.float32
            )
            for w, held in zip(ws, wide)
        ]
        routed = [
            jnp.sum(main * held, axis=1, keepdims=True)
            + adapter_scale
            * jnp.sum(u_ref[p, :, lanes].astype(jnp.float32) * v, axis=1, keepdims=True)
            for main, held, v, (_, p, lanes) in zip(mains, wide, v_wide, picked)
        ]
        grads = [
            (gate * (main + adapter_scale * low)).astype(jnp.bfloat16)
            for gate, main, low in zip(gates_x, mains, lows)
        ]
        for x, grad, la, back in zip(xs, grads, las, routed):
            for m in range(micro):
                hg_ref[m, x] = grad[m * padded : m * padded + slots]
                for h, (low, high) in enumerate(windows):
                    hit = code_s[m, h, pl.ds(x, 1), :] == slot_of[h]
                    rows = back[m * padded + low : m * padded + high]
                    back_s[m, h, pl.ds(x, 1), :] = jnp.sum(
                        jnp.where(hit, rows, 0.0), axis=0, keepdims=True
                    )
            for k in range(group_count):
                la_s[k, x] = (adapter_scale * la[:, k * share : (k + 1) * share]).astype(
                    la_s.dtype
                )

    def both_steps(step, carry):
        products = main_products(step)
        small_steps(step - 1)
        keep_products(step, products)
        return carry

    keep_products(0, main_products(0))
    for copy in late_copies:
        copy.wait()
    lax.fori_loop(1, groups, both_steps, 0)
    small_steps(groups - 1)

    group = lax.axis_index("dp")
    la_copies = [
        pltpu.make_async_copy(
            la_s.at[lax.rem(group + s, group_count)], la_outs[s], la_sem.at[s]
        )
        for s in range(group_count)
    ]
    for copy in la_copies:
        copy.start()
    number = lax.broadcasted_iota(jnp.int32, (experts, span), 0).astype(jnp.float32) + first
    for j in range(shards):
        h, k = j // (shards // 2), j % (shards // 2)
        back = jnp.concatenate(
            [back_s[m, h, :, k * block : (k + 1) * block] for m in range(micro)], axis=1
        )
        found = [
            jnp.sum(jnp.where(name == number, back, 0.0), axis=0, keepdims=True)
            for name in names[j][0]
        ]
        rk_ref[j] = jnp.concatenate(found, axis=0)
    for copy in la_copies:
        copy.wait()


def adapter_kernel(capacity, micro, span, top, group_count, shards, *refs):
    pairs = shards // 2
    early_ref, early_far_ref, near_ref, far_ref = refs[:4]
    lb_hbm, tok_s, q_s, u_refs, lb_ref, sem, u_sem, lb_sem = refs[4:]
    experts, rank, share = lb_ref.shape
    lb_copies = [
        pltpu.make_async_copy(lb_ref.at[x], lb_hbm.at[x], lb_sem.at[x]) for x in range(experts)
    ]
    blocks, tall = u_refs.shape[1:3]
    padded = tall // micro
    block = span // micro
    first = (lax.axis_index("expert") * experts).astype(jnp.float32)
    group = lax.axis_index("dp")
    owners = [shard_owner(i, shards) for i in range(shards)]
    copies, u_copies = [], []
    for g in range(group_count):
        home = lax.rem(group - g + group_count, group_count)
        for i in range(shards):
            if i % pairs:
                source = (far_ref if i >= pairs else near_ref).at[home, i % pairs - 1]
            elif i:
                source = early_far_ref.at[home]
            else:
                source = early_ref.at[home, pl.ds(blocks * tall, tok_s.shape[2])]
            copies.append(pltpu.make_async_copy(source, tok_s.at[g, owners[i]], sem.at[g, i]))
        for k in range(blocks):
            source = early_ref.at[home, pl.ds(k * tall, tall)]
            u_copies.append(pltpu.make_async_copy(source, u_refs.at[g, k], u_sem.at[g, k]))
    for copy in copies + u_copies:
        copy.start()
    slots = capacity * shards
    windows = slot_windows(slots)
    slot_of = [slot_iota(window, shards // 2 * block) for window in windows]
    for g in range(group_count):
        for copy in copies[g * shards : (g + 1) * shards]:
            copy.wait()
        names = [read_names(tok_s[g, i, span:, :], span, top) for i in range(shards)]
        codes, gates = slot_codes(names, first, capacity, experts, micro)
        for m in range(micro):
            parts = []
            for h in range(2):
                picks = jnp.concatenate(
                    [
                        jnp.where(
                            codes[m][h][x : x + 1, :] == slot_of[h],
                            gates[m][h][x : x + 1, :],
                            0.0,
                        )
                        for x in range(experts)
                    ],
                    axis=0,
                ).astype(jnp.bfloat16)
                tokens = jnp.concatenate(
                    [
                        tok_s[g, j, m * block : (m + 1) * block, :]
                        for j in range(h * shards // 2, (h + 1) * shards // 2)
                    ],
                    axis=0,
                )
                rows = jnp.dot(picks, tokens, preferred_element_type=jnp.float32)
                parts.append(rows.reshape(experts, -1, share))
            q = join_windows(parts[0], parts[1], windows, padded, 1).astype(jnp.bfloat16)
            at = g * tall + m * padded
            q_s[:, at : at + padded, :] = q
    for copy in u_copies:
        copy.wait()
    half = experts // 2
    for x in range(half):
        lane = x // blocks * 2 * rank
        both = jnp.concatenate(
            [u_refs[g, x % blocks, :, lane : lane + 2 * rank] for g in range(group_count)], axis=0
        )
        lb_ref[x] = adapter_scale * lax.dot_general(
            both[:, :rank], q_s[x], contract_first, preferred_element_type=jnp.float32
        )
        lb_ref[x + half] = adapter_scale * lax.dot_general(
            both[:, rank:], q_s[x + half], contract_first, preferred_element_type=jnp.float32
        )
        lb_copies[x].start()
        lb_copies[x + half].start()
    for copy in lb_copies:
        copy.wait()


def ring_order(count):
    return list(range(0, count, 2)) + list(range(1, count, 2))[::-1]


def local_by_tokens(
    output_gradient,
    chosen_expert_index,
    routing_gate_weight,
    hidden,
    frozen_down_weight,
    adapter_input_map,
    adapter_output_map,
):
    sources = lax.axis_size("expert")
    group_count = lax.axis_size("dp")
    micro, experts, slots, units = hidden.shape
    span, top = chosen_expert_index.shape
    width = output_gradient.shape[1]
    rank = adapter_input_map.shape[2]
    capacity = slots // sources
    block = span // micro
    padded = pad_rows(slots)
    share = width // group_count
    pairs = sources // 2
    chunks = 2 if group_count % 2 == 0 else 1
    part = width // chunks

    order = ring_order(pairs)
    place = {z: i for i, z in enumerate(order)}
    ring = [
        (2 * z + c, 2 * order[(place[z] + 1) % pairs] + c) for z in range(pairs) for c in range(2)
    ]
    swap = [(e, e ^ 1) for e in range(sources)]

    amap = jnp.swapaxes(adapter_input_map, 1, 2)
    u = jnp.einsum("mesk,exk->emsx", hidden, amap, preferred_element_type=jnp.float32)
    u = u.astype(jnp.bfloat16)
    u = jnp.pad(u, ((0, 0), (0, 0), (0, padded - slots), (0, 0))).reshape(
        2, experts // 2, micro * padded, rank
    )
    u = lax.optimization_barrier(jnp.concatenate([u[0], u[1]], axis=-1))

    def shift_groups(array, by):
        return lax.ppermute(
            array, "dp", [(d, (d + by) % group_count) for d in range(group_count)]
        )

    def swap_partners(array):
        return lax.ppermute(array, "expert", swap)

    def exchange_columns(chosen):
        def columns(pieces, g):
            at = g * share % part
            return pieces[g * share // part][:, at : at + share]

        return jnp.stack(
            [jnp.stack([columns(pieces, g) for pieces in chosen]) for g in range(group_count)]
        )

    def across_groups(array):
        return lax.all_to_all(array, "dp", split_axis=0, concat_axis=0, tiled=True)

    others = range(1, group_count)
    lines = 2 * top * span // share
    extra = -(-lines // 8) * 8
    vmem = pl.BlockSpec(memory_space=pltpu.VMEM)
    sent = pl.pallas_call(
        functools.partial(payload_kernel, share),
        out_shape=[jax.ShapeDtypeStruct((span + extra, part), jnp.bfloat16)] * chunks,
        in_specs=[vmem] * 3,
        out_specs=[vmem] * chunks,
        compiler_params=pltpu.CompilerParams(vmem_limit_bytes=58 * 1024 * 1024),
        name="ring_payload",
    )(output_gradient, chosen_expert_index.T, routing_gate_weight.T)

    near, far = [list(sent)], []
    blocks = experts // 2 * 2 * rank // share
    packed = jnp.concatenate(
        [u[k * blocks : (k + 1) * blocks] for k in range(experts // 2 // blocks)], axis=-1
    ).reshape(blocks * micro * padded, share)
    early = jnp.stack(
        [
            jnp.concatenate(
                [packed, sent[g * share // part][:, g * share % part :][:, :share]], axis=0
            )
            for g in range(group_count)
        ]
    )
    early = across_groups(early)
    early_far = swap_partners(early[:, blocks * micro * padded :])
    for step in range(pairs - 1):
        if step > 1:
            tied = [
                lax.optimization_barrier((near[step][c], [shard[c] for shard in far]))
                for c in range(chunks)
            ]
            near[step] = [a for a, _ in tied]
            far = [[b[k] for _, b in tied] for k in range(len(far))]
        near.append([lax.ppermute(piece, "expert", ring) for piece in near[step]])
        far.append([swap_partners(piece) for piece in near[step]])
    far.append([swap_partners(piece) for piece in near[-1]])
    columns = exchange_columns(near[1:])
    columns, early, early_far, far[-2:] = lax.optimization_barrier(
        (columns, early, early_far, far[-2:])
    )
    columns = across_groups(columns)
    pieces = [piece for shard in near + far for piece in shard]

    anywhere = pl.BlockSpec(memory_space=pl.ANY)
    kept = 3 * (4 if experts % 4 == 0 else 2)
    part_a = jax.ShapeDtypeStruct((experts, rank, units // group_count), jnp.bfloat16)
    hidden_grad, routed, *parts = pl.pallas_call(
        functools.partial(expert_kernel, capacity, group_count, sources, chunks),
        out_shape=(
            jax.ShapeDtypeStruct(hidden.shape, jnp.bfloat16),
            jax.ShapeDtypeStruct((sources, top, span), jnp.float32),
        )
        + (part_a,) * group_count,
        in_specs=[anywhere] * (sources * chunks) + [anywhere] * 5,
        out_specs=(vmem,) * 2 + (anywhere,) * group_count,
        scratch_shapes=[
            pltpu.VMEM((sources, span + extra, width), jnp.bfloat16),
            pltpu.VMEM((min(experts, kept), units + rank, width), jnp.bfloat16),
            pltpu.VMEM((experts, micro * padded, width), jnp.bfloat16),
            pltpu.VMEM((experts, micro * padded, units + rank), jnp.float32),
            pltpu.VMEM((micro, 2, experts, sources // 2 * block), jnp.float32),
            pltpu.VMEM((experts, micro * padded, 1), jnp.float32),
            pltpu.VMEM((micro, 2, experts, sources // 2 * block), jnp.float32),
            pltpu.VMEM((group_count, experts, rank, units // group_count), jnp.bfloat16),
            pltpu.VMEM(hidden.shape, jnp.bfloat16),
            pltpu.VMEM(u.shape, jnp.bfloat16),
            pltpu.VMEM(amap.shape, jnp.bfloat16),
            pltpu.SemaphoreType.DMA((sources, chunks)),
            pltpu.SemaphoreType.DMA((experts,)),
            pltpu.SemaphoreType.DMA((experts,)),
            pltpu.SemaphoreType.DMA((group_count,)),
            pltpu.SemaphoreType.DMA((3,)),
        ],
        compiler_params=pltpu.CompilerParams(vmem_limit_bytes=58 * 1024 * 1024),
        cost_estimate=pl.CostEstimate(
            flops=2 * experts * micro * padded * width * (units + rank + sources * block),
            bytes_accessed=2 * experts * width * (units + rank) + 2 * sources * span * width,
            transcendentals=0,
        ),
        name="expert_rows",
    )(*pieces, hidden, u, frozen_down_weight, amap, adapter_output_map)

    columns, _, _ = lax.optimization_barrier((columns, parts, routed))
    swapped = swap_partners(columns)
    arrived = [shift_groups(parts[s], s) for s in others]
    swapped, routed = lax.optimization_barrier((swapped, routed))
    home = lax.all_to_all(routed, "expert", split_axis=0, concat_axis=0, tiled=True)

    lora_b = pl.pallas_call(
        functools.partial(adapter_kernel, capacity, micro, span, top, group_count, sources),
        out_shape=jax.ShapeDtypeStruct((experts, rank, share), jnp.float32),
        in_specs=[anywhere] * 4,
        out_specs=anywhere,
        scratch_shapes=[
            pltpu.VMEM((group_count, sources, span + extra, share), jnp.bfloat16),
            pltpu.VMEM((experts, group_count * micro * padded, share), jnp.bfloat16),
            pltpu.VMEM((group_count, blocks, micro * padded, share), jnp.bfloat16),
            pltpu.VMEM((experts, rank, share), jnp.float32),
            pltpu.SemaphoreType.DMA((group_count, sources)),
            pltpu.SemaphoreType.DMA((group_count, blocks)),
            pltpu.SemaphoreType.DMA((experts,)),
        ],
        compiler_params=pltpu.CompilerParams(vmem_limit_bytes=58 * 1024 * 1024),
        cost_estimate=pl.CostEstimate(
            flops=2 * experts * micro * padded * share * group_count * (rank + sources * block),
            bytes_accessed=2 * group_count * sources * span * share + 4 * experts * rank * share,
            transcendentals=0,
        ),
        name="adapter_columns",
    )(early, early_far, columns, swapped)

    home, arrived, lora_b = lax.optimization_barrier((home, arrived, lora_b))
    router_grad = jnp.sum(home, axis=0).T
    lora_a = parts[0].astype(jnp.float32)
    for part in arrived:
        lora_a = lora_a + part.astype(jnp.float32)
    return (hidden_grad, router_grad, lora_a, lora_b)


def local(*arrays):
    sources, groups = lax.axis_size("expert"), lax.axis_size("dp")
    span, width = arrays[0].shape
    top, (micro, experts, slots, units) = arrays[1].shape[1], arrays[3].shape
    even = sources % 4 == 0 and experts % 2 == 0 and width % (128 * groups) == 0 and units % groups == 0
    rank = arrays[5].shape[2]
    packs = width // groups % (2 * rank) == 0 and experts * rank % (width // groups) == 0
    packs = packs and 2 * top * span % (width // groups) == 0 and (width // groups) % span == 0
    exact = experts * sources <= 256
    if even and packs and exact and sources * span <= micro * experts * slots:
        return local_by_tokens(*arrays)
    return local_by_slots(*arrays)


def solution(mesh):
    in_specs = (
        P(("dp", "expert"), None),
        P(("dp", "expert"), None),
        P(("dp", "expert"), None),
        P(None, ("dp", "expert"), None, None),
        P("expert", None, None),
        P("expert", None, None),
        P("expert", None, None),
    )
    out_specs = (
        P(None, ("dp", "expert"), None, None),
        P(("dp", "expert"), None),
        P("expert", None, "dp"),
        P("expert", None, "dp"),
    )
    return jax.shard_map(local, mesh=mesh, in_specs=in_specs, out_specs=out_specs, check_vma=False)
```
